256 devices in a mesh: tile: 64 (over y, z_hi, x), mem: 4 (over z_lo, core).
Axes of the slice: x: 4, y: 4, z: 8 (z_hi: 4, z_lo: 2; z = z_hi * 2 + z_lo), core: 2. Of those that a mesh axis runs over, the one named last changes fastest.
Arguments:
- perturbations: bfloat16 [32, 16, 512, 256], P('mem', None, 'tile'), may hold values from -6 to 6
- classes: int32 [512, 256], P('tile'), may hold values from 0 to 3
- obs_tile: int32 [65536, 1], P('tile'), may hold values from 0 to 63; in each aligned block of 1024 rows (0 to 1023, 1024 to 2047, ...) at most 48 rows name the same one
- obs_cells: int32 [4, 65536], P(None, 'tile'), may hold values from 0 to 2047
- obs_interp: float32 [4, 65536], P(None, 'tile'), may hold values from 0.1 to 0.6
- obs_jacobian: float32 [16, 65536], P(None, 'tile'), may hold values from 0.1 to 1
- innovation: float32 [65536], P('tile'), may hold values from -10 to 10
- inv_error: float32 [65536], P('tile'), may hold values from 0.5 to 4
Outputs:
- control: float32 [32, 16, 512, 256], P('mem', None, 'tile')
- increment: float32 [16, 512, 256], P('mem', 'tile')
The draws below stay inside these ranges and needn't reach their ends.
Inputs may be any that keep to these rules, and one draw needn't show every extreme that they name: `obs_tile`: each device's 1024 rows name at most 48 observations in one band; some band gets exactly 48 from some device.
All inputs are finite; a program needn't handle non-finite values.
Results may differ from the reference program's by a relative error of at most 0.0003.
Values sent between devices are 32-bit elements; how exact they have to be, the bound alone decides.
A program may use at most 64 MiB of HBM per device.

```python
import math
import jax
import jax.numpy as jnp
import numpy as np
from jax import lax

LAT_DEV = 8
LON_DEV = 256
LEV = 16
SWEEPS = 4
OBS_DEV = 1024
TLAT = 64
MEMBERS = 32
NOBS = 65536
MOST = 48
N_TILE = 64


def plant(drawn, stream_key, least, high):
    longest = drawn.shape.index(max(drawn.shape))
    spots = []
    for shift in (0, 1):
        where = [jax.random.randint(jax.random.fold_in(stream_key, axis), (), 0, length) for axis, length in enumerate(drawn.shape)]
        where[longest] = (where[longest] + shift) % drawn.shape[longest]
        spots.append(tuple(where))
    return drawn.at[spots[0]].set(least).at[spots[1]].set(high)


def block_levels(own_key, shape, shards, smallest, top_value):
    loudness, own = 1.0, jax.random.fold_in(own_key, 6)
    for axis_at, shards_of in shards:
        heights = jnp.exp(jax.random.uniform(jax.random.fold_in(own, axis_at), (shards_of,), jnp.float32, smallest / len(shards), top_value / len(shards)))
        loudness = loudness * jnp.repeat(heights, shape[axis_at] // shards_of).reshape([-1 if axis == axis_at else 1 for axis in range(len(shape))])
    return loudness


def routed_block(key, own, number, rows, amount, top, bound, slope):
    sequence = jax.random.permutation(key, amount)
    crowded, common = portions_of(amount, rows * top, bound, slope, True), portions_of(amount, rows * top, bound, slope, False)
    places = jnp.arange(amount)

    def named(lengths, rotation):
        used = int((lengths > 0).sum())
        fixed = max(1, used // 4)
        moved = fixed + (places - fixed + rotation * (used - fixed)) % max(1, amount - fixed)
        return jnp.zeros((amount,), jnp.int32).at[sequence[jnp.where(places < fixed, places, moved)]].set(jnp.asarray(lengths, jnp.int32))

    lengths = jnp.where(number % 4 == 0, named(crowded, number // 4), named(common, number - number // 4 - 1))
    mixed = jax.random.permutation(jax.random.fold_in(own, 3), amount)
    giver, taker = mixed[0:amount // 2 * 2:2], mixed[1:amount // 2 * 2:2]
    margin = jnp.minimum(lengths[giver] - 1, bound - lengths[taker]) // 2
    margin = jnp.where((giver == sequence[0]) | (taker == sequence[0]) | (lengths[taker] == 0), 0, jnp.maximum(margin, 0))
    moved = jax.random.randint(jax.random.fold_in(own, 4), (amount // 2,), 0, 1 << 20) % (margin + 1)
    lengths = lengths.at[giver].add(-moved).at[taker].add(moved)
    items = jnp.searchsorted(jnp.cumsum(lengths), jnp.arange(rows * top), side="right").astype(jnp.int32)
    table = items.reshape(top, rows).T
    table = table[jax.random.permutation(jax.random.fold_in(own, 1), rows)]
    rotation = jax.random.randint(jax.random.fold_in(own, 2), (rows, 1), 0, top)
    return jnp.take_along_axis(table, (jnp.arange(top)[None, :] + rotation) % top, axis=1)


def portions_of(number_of, total, reach, skew, full):
    weights = [(1 << 20) // math.isqrt(grade ** skew) + 1 for grade in range(1, number_of + 1)]
    largest = reach if full else min(reach, max(-(-total // number_of), total * weights[0] // sum(weights)))
    least = 1 if total - largest >= number_of - 1 else 0
    given, surplus = [largest] + [least] * (number_of - 1), total - largest - least * (number_of - 1)
    while surplus > 0:
        candidates = [i for i in range(1, number_of) if given[i] < largest] or [i for i in range(1, number_of) if given[i] < reach]
        pool, remaining = sum([weights[i] for i in candidates]), surplus
        for i in candidates:
            more = min(reach - given[i], max(1, remaining * weights[i] // pool), surplus)
            given[i] = given[i] + more
            surplus = surplus - more
    return np.array(given)


def gaussian(stream_key, extent, deviation, limit, shards=(), dtype=jnp.bfloat16):
    values = jax.random.normal(stream_key, extent, jnp.float32) * deviation
    if len(shards) > 0:
        values = block_levels(stream_key, extent, shards, -0.22, 0.18) * values
    return jnp.clip(values, min=-limit, max=limit).astype(dtype)


def setup_inputs(seed: int = 0) -> dict:
    keys = jax.random.split(jax.random.key(seed), 9)
    perturbations = gaussian(keys[0], (MEMBERS, LEV, N_TILE * LAT_DEV, LON_DEV), 1.0, 6.0, ((0, 4), (2, 64)))
    classes = plant(jax.random.randint(keys[1], (N_TILE * LAT_DEV, LON_DEV), 0, 4), jax.random.fold_in(keys[1], 1), 0, 3).astype(jnp.int32)
    obs_tile_keys = jax.random.split(jax.random.fold_in(keys[2], 1), NOBS // OBS_DEV)
    obs_tile_turns = jax.random.permutation(jax.random.fold_in(keys[2], 3), NOBS // OBS_DEV)
    obs_tile = jax.vmap(lambda own, number: routed_block(jax.random.fold_in(keys[2], 2), own, number, OBS_DEV, N_TILE, 1, MOST, 2))(obs_tile_keys, obs_tile_turns).reshape((NOBS, 1))
    obs_cells = plant(jax.random.randint(keys[3], (4, NOBS), 0, LAT_DEV * LON_DEV), jax.random.fold_in(keys[3], 1), 0, (LAT_DEV * LON_DEV) - 1).astype(jnp.int32)
    obs_interp = jnp.clip(0.1 + 0.5 * jax.random.uniform(keys[4], (4, NOBS), jnp.float32) ** block_levels(keys[4], (4, NOBS), ((1, 64),), -0.2, 0.2), 0.1, 0.6)
    obs_jacobian = jnp.clip(jnp.exp(math.log(1.0) - 2.3025851 * jax.random.uniform(keys[5], (LEV, NOBS), jnp.float32) ** block_levels(keys[5], (LEV, NOBS), ((1, 64),), -0.2, 0.2)), 0.1, 1.0)
    innovation = gaussian(keys[6], (NOBS,), 2.0, 10.0, ((0, 64),), jnp.float32)
    inv_error = jnp.clip(jnp.exp(math.log(4.0) - 2.0794415 * jax.random.uniform(keys[7], (NOBS,), jnp.float32) ** block_levels(keys[7], (NOBS,), ((0, 64),), -0.2, 0.2)), 0.5, 4.0)
    return dict(perturbations=perturbations, classes=classes, obs_tile=obs_tile, obs_cells=obs_cells, obs_interp=obs_interp, obs_jacobian=obs_jacobian, innovation=innovation, inv_error=inv_error)


diffusivities = (0.06, 0.1, 0.15, 0.22)
step_length = 0.5

def lookup(classes):
    out = jnp.zeros(classes.shape, jnp.float32)
    for position, coefficient in enumerate(diffusivities):
        out = out + jnp.where(classes == position, jnp.float32(coefficient), jnp.float32(0.0))
    return out

def to_global(array):
    lead = array.shape[:-2]
    count = len(lead)
    t_lon = N_TILE // TLAT
    blocks = array.reshape(lead + (t_lon, TLAT, LAT_DEV, LON_DEV))
    blocks = jnp.moveaxis(blocks, count, count + 2)
    return blocks.reshape(lead + (TLAT * LAT_DEV, t_lon * LON_DEV))

def to_tiles(array):
    lead = array.shape[:-2]
    count = len(lead)
    t_lon = N_TILE // TLAT
    blocks = array.reshape(lead + (TLAT, LAT_DEV, t_lon, LON_DEV))
    blocks = jnp.moveaxis(blocks, count + 2, count)
    return blocks.reshape(lead + (N_TILE * LAT_DEV, LON_DEV))

def neighbours(field):
    padded = jnp.pad(field, ((0, 0), (1, 1), (0, 0)))
    total = padded[:, 2:] + padded[:, :-2]
    return total + jnp.roll(field, 1, axis=2) + jnp.roll(field, -1, axis=2)

def diffuse(field, kappa, adjoint):
    for sweep_id in range(SWEEPS):
        if adjoint:
            source = kappa * field
            field = field + neighbours(source) - 4.0 * source
        else:
            field = field + kappa * (neighbours(field) - 4.0 * field)
    return field

def reference(perturbations, classes, obs_tile, obs_cells, obs_interp, obs_jacobian, innovation, inv_error):
    scale = 1.0 / math.sqrt(MEMBERS - 1)
    kappa = to_global(lookup(classes))[None]
    cells_tile = LAT_DEV * LON_DEV
    index = [(obs_tile[:, 0] * cells_tile + obs_cells[c]).astype(jnp.int32) for c in range(4)]

    def apply_h(state):
        flat = state.reshape(LEV, N_TILE * cells_tile)
        mixed = jnp.zeros((LEV, NOBS), jnp.float32)
        for c in range(4):
            mixed = mixed + obs_interp[c] * flat[:, index[c]]
        return lax.optimization_barrier(jnp.sum(obs_jacobian * mixed, axis=0))

    def adjoint_h(values):
        contrib = obs_jacobian * values[None]
        flat = jnp.zeros((LEV, N_TILE * cells_tile), jnp.float32)
        for c in range(4):
            flat = flat.at[:, index[c]].add(obs_interp[c] * contrib)
        return flat.reshape(LEV, N_TILE * LAT_DEV, LON_DEV)

    def forward(control_now):

        def add(total, pair):
            member, field = pair
            smooth = to_tiles(diffuse(to_global(field), kappa, False))
            return (total + member.astype(jnp.float32) * smooth, None)
        start = jnp.zeros((LEV, N_TILE * LAT_DEV, LON_DEV), jnp.float32)
        total, unused = lax.scan(add, start, (perturbations, control_now))
        return total * scale

    def adjoint_members(adjoint_state):

        def one(member):
            return to_tiles(diffuse(to_global(member.astype(jnp.float32) * adjoint_state * scale), kappa, True))
        return lax.map(one, perturbations)
    first = adjoint_h(-(inv_error * innovation))
    control_one = -step_length * adjoint_members(first)
    misfit = inv_error * (apply_h(forward(control_one)) - innovation)
    gradient = control_one + adjoint_members(adjoint_h(misfit))
    control = control_one - step_length * gradient
    increment = forward(control)
    return (control, increment)
```

```python
import functools
import math

import jax
import jax.numpy as jnp
from jax import lax
from jax.experimental import pallas as pl
from jax.experimental.pallas import tpu as pltpu
from jax.sharding import PartitionSpec as P

MESH = pl.DeviceIdType.MESH
BF = jnp.bfloat16
F32 = jnp.float32
DIFFUSIVITIES = (0.06, 0.1, 0.15, 0.22)
STEP = 0.5
MOST = 48
FEATURES = 32
HALO = 4
LANES = 128

(A2A, KAP_U, KAP_D, PERT_U, PERT_D, RS0, AG0, HU0, HD0, RSU, RUU, RUD, AGU, RS1, AG1, HU1, HD1,
 RSV, RVU, RVD, N_SEM) = range(21)


def nt(a, b):
    return lax.dot_general(a, b, (((1,), (1,)), ((), ())), preferred_element_type=F32)


def nn(a, b):
    return jnp.dot(a, b, preferred_element_type=F32)


def split2(x):
    hi = x.astype(BF).astype(F32)
    return hi, x - hi


def kernel(
    tiles, groups, members,
    pert_ref, classes_ref, target_ref, cells_ref, interp_ref, jac_ref, innov_ref, inv_ref,
    control_ref, incr_ref,
    perm, pay, val, out_buf, in_buf, feat, onehot, a_hi, a_lo,
    pert, stage, kap_rows, kap, cen, ikap,
    s0, s1, rs0, rs1, x0, x1, up, rsu, ruu, rud, u, vp, rsv, rvu, rvd, flat,
    ssem, rsem, lsem,
):
    t = lax.axis_index("tile")
    j = lax.axis_index("mem")
    north, south = lax.rem(t + tiles - 1, tiles), lax.rem(t + 1, tiles)
    slots = MOST // groups
    levels = 16
    scale = 1.0 / math.sqrt(members * groups - 1)
    obs = pay.shape[1]

    def peer(d):
        return lax.rem(j + d, groups)

    def band(d):
        return lax.rem(t + d, tiles)

    def send(src, dst, k, tile, mem):
        pltpu.make_async_remote_copy(
            src_ref=src, dst_ref=dst, send_sem=ssem.at[k], recv_sem=rsem.at[k],
            device_id={"tile": tile, "mem": mem}, device_id_type=MESH,
        ).start()

    def arrived(like, k):
        pltpu.make_async_copy(like, like, rsem.at[k]).wait()

    def sent(like, k):
        pltpu.make_async_copy(like, like, ssem.at[k]).wait()

    barrier = pltpu.get_barrier_semaphore()

    def greet(tile, mem):
        pl.semaphore_signal(
            barrier, inc=1, device_id={"tile": tile, "mem": mem}, device_id_type=MESH
        )

    def greet_band(d, carry):
        greet(band(d), j)
        return carry

    lax.fori_loop(1, tiles, greet_band, 0)
    for d in range(1, groups):
        greet(t, peer(d))
        greet(north, peer(d))
        greet(south, peer(d))

    row_id = lax.broadcasted_iota(jnp.int32, (256, 256), 0)
    col_id = lax.broadcasted_iota(jnp.int32, (256, 256), 1)
    perm[0] = jnp.where(col_id == (row_id & 1) * 128 + (row_id >> 1), 1.0, 0.0).astype(BF)
    perm[1] = jnp.where(row_id == (col_id & 1) * 128 + (col_id >> 1), 1.0, 0.0).astype(BF)

    target = target_ref[...]
    bands = lax.broadcasted_iota(jnp.int32, (tiles, obs), 0)
    member_of = jnp.where(target == bands, 1.0, 0.0)
    member_bf = member_of.astype(BF)
    before = jnp.where(row_id < col_id, 1.0, 0.0).astype(BF)
    base = jnp.zeros((tiles, 1), F32)
    ranks = []
    for b in range(obs // 256):
        part = slice(b * 256, (b + 1) * 256)
        count = nn(member_bf[:, part], before) + base
        ranks.append(jnp.sum(member_of[:, part] * count, axis=0, keepdims=True))
        base = base + jnp.sum(member_of[:, part], axis=1, keepdims=True)
    rank = jnp.concatenate(ranks, axis=1).astype(jnp.int32) - j * slots

    pay[0:16, :] = jac_ref[...]
    pay[16:24, :] = jnp.concatenate([cells_ref[...].astype(F32), interp_ref[...]], axis=0)
    pay[24:32, :] = jnp.concatenate(
        [innov_ref[...], inv_ref[...], jnp.zeros((6, obs), F32)], axis=0
    )
    whole = pay[...]
    high = whole.astype(BF).astype(F32)
    rest = whole - high
    middle = rest.astype(BF).astype(F32)
    low = rest - middle
    for q in range(slots):
        mine = rank == q
        for k, piece in enumerate((high, middle, low)):
            val[k, q * FEATURES : (q + 1) * FEATURES, :] = jnp.where(mine, piece, 0.0).astype(BF)
    packed = nt(member_bf, val[0]) + nt(member_bf, val[1]) + nt(member_bf, val[2])
    out_buf[:, 0, :] = packed

    def arrange(m, carry):
        block = pert_ref[m].astype(F32).reshape(levels * 8, 256).astype(BF)
        moved = nn(block, perm[0])
        stage[0] = moved[:, :LANES]
        stage[1] = moved[:, LANES:]
        for r in range(8):
            for lh in range(2):
                at = pl.ds(pl.multiple_of(m * levels + lh * 8, 8), 8)
                for h in range(2):
                    pert[HALO + r, h, at, :] = stage[h, pl.ds(lh * 64 + r, 8, stride=8), :]
        return carry

    lax.fori_loop(0, members, arrange, 0)

    classes = nn(classes_ref[...].astype(F32).astype(BF), perm[0])
    kappa = jnp.zeros(classes.shape, F32)
    for position, coefficient in enumerate(DIFFUSIVITIES):
        kappa = kappa + jnp.where(classes == float(position), coefficient, 0.0)
    kap_rows[1] = kappa

    pl.semaphore_wait(barrier, tiles - 1 + 3 * (groups - 1))

    def send_band(d, carry):
        send(out_buf.at[band(d)], in_buf.at[t], A2A, band(d), j)
        return carry

    lax.fori_loop(1, tiles, send_band, 0)
    own = pltpu.make_async_copy(out_buf.at[t], in_buf.at[t], lsem.at[0])
    own.start()
    send(kap_rows.at[1], kap_rows.at[0], KAP_U, south, j)
    send(kap_rows.at[1], kap_rows.at[2], KAP_D, north, j)
    send(pert.at[pl.ds(8, 4)], pert.at[pl.ds(0, 4)], PERT_U, south, j)
    send(pert.at[pl.ds(4, 4)], pert.at[pl.ds(12, 4)], PERT_D, north, j)

    arrived(kap_rows.at[0], KAP_U)
    arrived(kap_rows.at[2], KAP_D)
    for r in range(16):
        block, row = divmod(r + 4, 8)
        line = kap_rows[block, row : row + 1, :]
        if r < 4:
            line = jnp.where(t == 0, 0.0, line)
        if r >= 12:
            line = jnp.where(t == tiles - 1, 0.0, line)
        for h in range(2):
            wide = jnp.broadcast_to(line[:, h * LANES : (h + 1) * LANES], (8, LANES))
            kap[r, h] = wide
            cen[r, h] = 1.0 - 4.0 * wide
            if 4 <= r < 12:
                ikap[r - 4, h] = 1.0 / wide

    own.wait()
    arrived(in_buf.at[pl.ds(0, tiles - 1)], A2A)

    parts = [in_buf[:, 0, g * LANES : (g + 1) * LANES] for g in range(3)]
    pair = jnp.concatenate(parts[:2], axis=0).T
    last = jnp.concatenate([parts[2], parts[2]], axis=0).T
    for b in range(4):
        feat[b] = pair[b * FEATURES : (b + 1) * FEATURES, :]
    lane = lax.broadcasted_iota(jnp.int32, (FEATURES, LANES), 1)
    for b in range(2):
        one = last[2 * b * FEATURES : (2 * b + 1) * FEATURES, :]
        two = last[(2 * b + 1) * FEATURES : (2 * b + 2) * FEATURES, :]
        feat[4 + b] = jnp.where(lane < 64, one, two)
    blocks = 6

    def place(b, c):
        cell = feat[b, 16 + c : 17 + c, :].astype(jnp.int32)
        code = (cell & 1) * 8 + (cell >> 8)
        low = (cell & 255) >> 1
        return code, low

    def hits(code):
        return lax.broadcasted_iota(jnp.int32, (16, 8, LANES), 0) == code.reshape(1, 1, LANES)

    def build(b, carry):
        for c in range(4):
            low = place(b, c)[1]
            spot = lax.broadcasted_iota(jnp.int32, (LANES, LANES), 0) == low
            onehot[b, :, c * LANES : (c + 1) * LANES] = jnp.where(spot, 1.0, 0.0).astype(BF)
        return carry

    lax.fori_loop(0, blocks, build, 0)

    def adjoint_obs(b, z, total):
        jac = feat[b, 0:16, :]
        for c in range(4):
            code = place(b, c)[0]
            value = jac * (feat[b, 20 + c : 21 + c, :] * z)
            mask = hits(code)[None]
            for piece, where_to in zip(split2(value), (a_hi, a_lo)):
                wide = jnp.where(mask, piece.reshape(2, 1, 8, LANES), 0.0)
                where_to[:, c * LANES : (c + 1) * LANES] = wide.reshape(256, LANES).astype(BF)
        new = nt(a_hi[...], onehot[b]) + nt(a_lo[...], onehot[b])
        total[...] += new.reshape(4, 8, 8, LANES)

    def first(b, carry):
        z = -(feat[b, 25:26, :] * feat[b, 24:25, :])
        adjoint_obs(b, z, s0)
        return carry

    s0[...] = jnp.zeros(s0.shape, F32)
    lax.fori_loop(0, blocks, first, 0)

    def scatter(source, into, k):
        for d in range(1, groups):
            send(source.at[peer(d)], into.at[d - 1], k, t, peer(d))

    def spread(x, k, k_up, k_down):
        for d in range(1, groups):
            here = x.at[j, pl.ds(HALO, 8)]
            send(here, here, k, t, peer(d))
        for d in range(groups):
            send(x.at[j, pl.ds(8, 4)], x.at[j, pl.ds(0, 4)], k_up, south, peer(d))
            send(x.at[j, pl.ds(4, 4)], x.at[j, pl.ds(12, 4)], k_down, north, peer(d))
        arrived(x.at[pl.ds(0, groups - 1), pl.ds(HALO, 8)], k)
        arrived(x.at[:, pl.ds(0, 4)], k_up)
        arrived(x.at[:, pl.ds(12, 4)], k_down)

    scatter(s0, rs0, RS0)
    arrived(rs0, RS0)
    x0[j, pl.ds(HALO, 8)] = s0[j] + rs0[0] + rs0[1] + rs0[2]
    spread(x0, AG0, HU0, HD0)
    arrived(pert.at[pl.ds(0, 4)], PERT_U)
    arrived(pert.at[pl.ds(12, 4)], PERT_D)

    def sweep(f, lo, hi):
        even, odd = f
        n = hi - lo
        e, o = even[1 : 1 + n], odd[1 : 1 + n]
        ring_e = even[:n] + even[2:] + (o + pltpu.roll(o, 1, 2))
        ring_o = odd[:n] + odd[2:] + (e + pltpu.roll(e, LANES - 1, 2))
        return (
            cen[lo:hi, 0] * e + kap[lo:hi, 0] * ring_e,
            cen[lo:hi, 1] * o + kap[lo:hi, 1] * ring_o,
        )

    def local_pass(x, control_out):
        up[...] = jnp.zeros(up.shape, F32)

        def group(i, carry):
            lh, m = i // members, lax.rem(i, members)
            at = pl.ds(pl.multiple_of(m * levels + lh * 8, 8), 8)
            f = tuple(kap[:, h] * pert[:, h, at, :] * x[lh * 2 + h] for h in range(2))
            for k in range(4):
                f = sweep(f, k + 1, 15 - k)
            f = tuple(f[h] * ikap[:, h] for h in range(2))
            if control_out:
                for h in range(2):
                    for r in range(8):
                        stage_at = pl.ds(m * 128 + lh * 64 + r, 8, stride=8)
                        flat[h, stage_at, :] = f[h][r]
            zero = jnp.zeros((2, 8, LANES), F32)
            for k in range(4):
                f = sweep(
                    tuple(jnp.concatenate([zero, g, zero], axis=0) for g in f), 3 - k, 13 + k
                )
            for h in range(2):
                up[lh * 2 + h] += pert[:, h, at, :] * f[h]
            return carry

        lax.fori_loop(0, 2 * members, group, 0)

    def reduce(source, near, from_north, from_south, k, k_up, k_down):
        for d in range(1, groups):
            q = peer(d)
            send(source.at[q, pl.ds(HALO, 8)], near.at[d - 1], k, t, q)
        for d in range(groups):
            q = peer(d)
            send(source.at[q, pl.ds(12, 4)], from_north.at[j], k_up, south, q)
            send(source.at[q, pl.ds(0, 4)], from_south.at[j], k_down, north, q)
        arrived(near, k)
        arrived(from_north, k_up)
        arrived(from_south, k_down)
        total = source[j, pl.ds(HALO, 8)] + near[0] + near[1] + near[2]
        top = from_north[0] + from_north[1] + from_north[2] + from_north[3]
        bottom = from_south[0] + from_south[1] + from_south[2] + from_south[3]
        return total + jnp.concatenate([top, bottom], axis=0)

    local_pass(x0, False)
    u[j] = (-STEP * scale * scale) * reduce(up, rsu, ruu, rud, RSU, RUU, RUD)
    for d in range(1, groups):
        send(u.at[j], u.at[j], AGU, t, peer(d))
    arrived(u.at[pl.ds(0, groups - 1)], AGU)

    state_hi, state_lo = (g.astype(BF) for g in split2(u[...].reshape(256, LANES)))

    def second(b, carry):
        state_h, state_l = carry
        mixed = nn(state_h, onehot[b]) + nn(state_l, onehot[b])
        jac = feat[b, 0:16, :].reshape(2, 8, LANES)
        total = jnp.zeros((2, 8, LANES), F32)
        for c in range(4):
            mask = hits(place(b, c)[0])[None]
            part = mixed[:, c * LANES : (c + 1) * LANES].reshape(2, 16, 8, LANES)
            picked = jnp.sum(jnp.where(mask, part, 0.0), axis=1)
            total = total + feat[b, 20 + c : 21 + c, :].reshape(1, 1, LANES) * picked
        y = jnp.sum((jac * total).reshape(16, LANES), axis=0, keepdims=True)
        z = feat[b, 25:26, :] * (y - feat[b, 24:25, :])
        adjoint_obs(b, z, s1)
        return carry

    s1[...] = jnp.zeros(s1.shape, F32)
    lax.fori_loop(0, blocks, second, (state_hi, state_lo))

    scatter(s1, rs1, RS1)
    arrived(rs1, RS1)
    x1[j, pl.ds(HALO, 8)] = (-scale * STEP) * (
        STEP * x0[j, pl.ds(HALO, 8)] + s1[j] + rs1[0] + rs1[1] + rs1[2]
    )
    spread(x1, AG1, HU1, HD1)
    sent(rsu, RSU)
    sent(ruu, RUU)
    sent(rud, RUD)
    local_pass(x1, True)

    sub = lax.broadcasted_iota(jnp.int32, (16, 8, LANES), 1)
    for lh in range(2):
        even, odd = up[lh * 2], up[lh * 2 + 1]
        vp[lh * 2] = jnp.where(sub < 4, even, pltpu.roll(odd, 4, 1))
        vp[lh * 2 + 1] = jnp.where(sub < 4, pltpu.roll(even, 4, 1), odd)

    def unmix(m, carry):
        rows = pl.ds(pl.multiple_of(m * 128, 128), 128)
        wide = jnp.concatenate([flat[0, rows, :], flat[1, rows, :]], axis=1)
        hi, lo = split2(wide)
        back = nn(hi.astype(BF), perm[1]) + nn(lo.astype(BF), perm[1])
        control_ref[m] = back.reshape(levels, 8, 256)
        return carry

    lax.fori_loop(0, members, unmix, 0)

    final = scale * reduce(vp, rsv, rvu, rvd, RSV, RVU, RVD)
    wide = jnp.concatenate(
        [final.reshape(64, LANES), pltpu.roll(final, 4, 1).reshape(64, LANES)], axis=1
    )
    hi, lo = split2(wide)
    back = nn(hi.astype(BF), perm[1]) + nn(lo.astype(BF), perm[1])
    for h in range(2):
        stage[h, 0:64, :] = back[:, h * LANES : (h + 1) * LANES]
        for level in range(4):
            incr_ref[level, :, h * LANES : (h + 1) * LANES] = stage[h, pl.ds(level, 8, stride=8), :]

    sent(in_buf.at[pl.ds(0, tiles - 1)], A2A)
    sent(kap_rows.at[0], KAP_U)
    sent(kap_rows.at[2], KAP_D)
    sent(pert.at[pl.ds(0, 4)], PERT_U)
    sent(pert.at[pl.ds(12, 4)], PERT_D)
    for k in (RS0, AG0, AGU, RS1, AG1, RSV):
        sent(rs0, k)
    for k in (HU0, HD0, HU1, HD1, RVU, RVD):
        sent(ruu, k)


def on_device(tiles, groups, perturbations, classes, target, cells, interp, jac, innov, inverse):
    members, levels, rows, cols = perturbations.shape
    obs = target.shape[0]
    vm = pl.BlockSpec(memory_space=pltpu.VMEM)
    quarter = (groups, 8, 8, LANES)
    window = (groups, 16, 8, LANES)
    near = (groups - 1, 8, 8, LANES)
    halo = (groups, 4, 8, LANES)
    scratch = [
        ((2, 256, 256), BF),
        ((FEATURES, obs), F32),
        ((3, FEATURES * (MOST // groups), obs), BF),
        ((tiles, 1, FEATURES * (MOST // groups)), F32),
        ((tiles, 1, FEATURES * (MOST // groups)), F32),
        ((6, FEATURES, LANES), F32),
        ((6, LANES, 4 * LANES), BF),
        ((256, 4 * LANES), BF),
        ((256, 4 * LANES), BF),
        ((16, 2, members * levels, LANES), F32),
        ((2, LANES, LANES), F32),
        ((3, 8, 256), F32),
        ((16, 2, 8, LANES), F32),
        ((16, 2, 8, LANES), F32),
        ((8, 2, 8, LANES), F32),
        (quarter, F32), (quarter, F32),
        (near, F32), (near, F32),
        (window, F32), (window, F32),
        (window, F32),
        (near, F32), (halo, F32), (halo, F32),
        (quarter, F32),
        (window, F32),
        (near, F32), (halo, F32), (halo, F32),
        ((2, members * levels * rows, LANES), F32),
    ]
    return pl.pallas_call(
        functools.partial(kernel, tiles, groups, members),
        out_shape=(
            jax.ShapeDtypeStruct((members, levels, rows, cols), F32),
            jax.ShapeDtypeStruct((levels // groups, rows, cols), F32),
        ),
        in_specs=[vm] * 8,
        out_specs=(vm, vm),
        scratch_shapes=[pltpu.VMEM(shape, dtype) for shape, dtype in scratch]
        + [
            pltpu.SemaphoreType.DMA((N_SEM,)),
            pltpu.SemaphoreType.DMA((N_SEM,)),
            pltpu.SemaphoreType.DMA((1,)),
        ],
        compiler_params=pltpu.CompilerParams(
            collective_id=0, has_side_effects=True, vmem_limit_bytes=40 * 1024 * 1024
        ),
        name="assimilate",
    )(
        perturbations, classes, target.reshape(1, obs), cells, interp, jac,
        innov.reshape(1, obs), inverse.reshape(1, obs),
    )


def solution(mesh):
    in_specs = (
        P("mem", None, "tile", None),
        P("tile", None),
        P("tile", None),
        P(None, "tile"),
        P(None, "tile"),
        P(None, "tile"),
        P("tile"),
        P("tile"),
    )
    out_specs = (P("mem", None, "tile", None), P("mem", "tile", None))
    return jax.shard_map(
        functools.partial(on_device, mesh.shape["tile"], mesh.shape["mem"]),
        mesh=mesh, in_specs=in_specs, out_specs=out_specs, check_vma=False,
    )
```

```python
import functools
import math

import jax
import jax.numpy as jnp
from jax import lax
from jax.experimental import pallas as pl
from jax.experimental.pallas import tpu as pltpu
from jax.sharding import PartitionSpec as P

MESH = pl.DeviceIdType.MESH
BF = jnp.bfloat16
F32 = jnp.float32
DIFFUSIVITIES = (0.06, 0.1, 0.15, 0.22)
STEP = 0.5
MOST = 48
FEATURES = 32
HALO = 4
LANES = 128

(A2A, KAP_U, KAP_D, PERT_U, PERT_D, RS0, AG0, HU0, HD0, RSU, RUU, RUD, AGU, RS1, AG1, HU1, HD1,
 RSV, RVU, RVD, N_SEM) = range(21)


def nt(a, b):
    return lax.dot_general(a, b, (((1,), (1,)), ((), ())), preferred_element_type=F32)


def nn(a, b):
    return jnp.dot(a, b, preferred_element_type=F32)


def split2(x):
    hi = x.astype(BF).astype(F32)
    return hi, x - hi


def kernel(
    tiles, groups, members,
    pert_hbm, classes_hbm, target_hbm, cells_hbm, interp_hbm, jac_hbm, innov_hbm, inv_hbm,
    control_ref, incr_ref,
    pert_ref, classes_ref, target_ref, cells_ref, interp_ref, jac_ref, innov_ref, inv_ref,
    perm, pay, val, out_buf, in_buf, feat, onehot, a_hi, a_lo,
    pert, stage, kap_rows, kap, ikap,
    s0, s1, rs0, rs1, x0, x1, up, rsu, ruu, rud, u, vp, rsv, rvu, rvd, flat,
    ssem, rsem, lsem,
):
    t = lax.axis_index("tile")
    j = lax.axis_index("mem")
    north, south = lax.rem(t + tiles - 1, tiles), lax.rem(t + 1, tiles)
    slots = MOST // groups
    levels = 16
    scale = 1.0 / math.sqrt(members * groups - 1)
    obs = pay.shape[1]

    def peer(d):
        return lax.rem(j + d, groups)

    def band(d):
        return lax.rem(t + d, tiles)

    def send(src, dst, k, tile, mem):
        pltpu.make_async_remote_copy(
            src_ref=src, dst_ref=dst, send_sem=ssem.at[k], recv_sem=rsem.at[k],
            device_id={"tile": tile, "mem": mem}, device_id_type=MESH,
        ).start()

    def arrived(like, k):
        pltpu.make_async_copy(like, like, rsem.at[k]).wait()

    def sent(like, k):
        pltpu.make_async_copy(like, like, ssem.at[k]).wait()

    fetches = [
        pltpu.make_async_copy(source, into, lsem.at[1 + k])
        for k, (source, into) in enumerate((
            (target_hbm, target_ref), (cells_hbm, cells_ref), (interp_hbm, interp_ref),
            (jac_hbm, jac_ref), (innov_hbm, innov_ref), (inv_hbm, inv_ref),
            (pert_hbm, pert_ref), (classes_hbm, classes_ref),
        ))
    ]
    for fetch in fetches:
        fetch.start()

    barrier = pltpu.get_barrier_semaphore()

    def greet(tile, mem):
        pl.semaphore_signal(
            barrier, inc=1, device_id={"tile": tile, "mem": mem}, device_id_type=MESH
        )

    def greet_band(d, carry):
        greet(band(d), j)
        return carry

    lax.fori_loop(1, tiles, greet_band, 0)
    for d in range(1, groups):
        greet(t, peer(d))
        greet(north, peer(d))
        greet(south, peer(d))

    row_id = lax.broadcasted_iota(jnp.int32, (256, 256), 0)
    col_id = lax.broadcasted_iota(jnp.int32, (256, 256), 1)
    perm[0] = jnp.where(col_id == (row_id & 1) * 128 + (row_id >> 1), 1.0, 0.0).astype(BF)
    perm[1] = jnp.where(row_id == (col_id & 1) * 128 + (col_id >> 1), 1.0, 0.0).astype(BF)

    for fetch in fetches[:6]:
        fetch.wait()

    target = target_ref[...]
    bands = lax.broadcasted_iota(jnp.int32, (tiles, obs), 0)
    member_of = jnp.where(target == bands, 1.0, 0.0)
    member_bf = member_of.astype(BF)
    before = jnp.where(row_id < col_id, 1.0, 0.0).astype(BF)
    base = jnp.zeros((tiles, 1), F32)
    ranks = []
    for b in range(obs // 256):
        part = slice(b * 256, (b + 1) * 256)
        count = nn(member_bf[:, part], before) + base
        ranks.append(jnp.sum(member_of[:, part] * count, axis=0, keepdims=True))
        base = base + jnp.sum(member_of[:, part], axis=1, keepdims=True)
    rank = jnp.concatenate(ranks, axis=1).astype(jnp.int32) - j * slots

    pay[0:16, :] = jac_ref[...]
    pay[16:24, :] = jnp.concatenate([cells_ref[...].astype(F32), interp_ref[...]], axis=0)
    pay[24:32, :] = jnp.concatenate(
        [innov_ref[...], inv_ref[...], jnp.zeros((6, obs), F32)], axis=0
    )
    whole = pay[...]
    high = whole.astype(BF).astype(F32)
    rest = whole - high
    middle = rest.astype(BF).astype(F32)
    low = rest - middle
    for q in range(slots):
        mine = rank == q
        for k, piece in enumerate((high, middle, low)):
            val[k, q * FEATURES : (q + 1) * FEATURES, :] = jnp.where(mine, piece, 0.0).astype(BF)
    packed = nt(member_bf, val[0]) + nt(member_bf, val[1]) + nt(member_bf, val[2])
    out_buf[:, 0, :] = packed

    for fetch in fetches[6:]:
        fetch.wait()

    def arrange(m, carry):
        block = pert_ref[m].astype(F32).reshape(levels * 8, 256).astype(BF)
        moved = nn(block, perm[0])
        stage[0] = moved[:, :LANES]
        stage[1] = moved[:, LANES:]
        for r in range(8):
            for lh in range(2):
                at = pl.ds(pl.multiple_of(m * levels + lh * 8, 8), 8)
                for h in range(2):
                    pert[HALO + r, h, at, :] = stage[h, pl.ds(lh * 64 + r, 8, stride=8), :]
        return carry

    lax.fori_loop(0, members, arrange, 0)

    classes = nn(classes_ref[...].astype(F32).astype(BF), perm[0])
    kappa = jnp.zeros(classes.shape, F32)
    for position, coefficient in enumerate(DIFFUSIVITIES):
        kappa = kappa + jnp.where(classes == float(position), coefficient, 0.0)
    kap_rows[1] = kappa

    pl.semaphore_wait(barrier, tiles - 1 + 3 * (groups - 1))

    def send_band(d, carry):
        send(out_buf.at[band(d)], in_buf.at[t], A2A, band(d), j)
        return carry

    lax.fori_loop(1, tiles, send_band, 0)
    own = pltpu.make_async_copy(out_buf.at[t], in_buf.at[t], lsem.at[0])
    own.start()
    send(kap_rows.at[1], kap_rows.at[0], KAP_U, south, j)
    send(kap_rows.at[1], kap_rows.at[2], KAP_D, north, j)
    send(pert.at[pl.ds(8, 4)], pert.at[pl.ds(0, 4)], PERT_U, south, j)
    send(pert.at[pl.ds(4, 4)], pert.at[pl.ds(12, 4)], PERT_D, north, j)

    arrived(kap_rows.at[0], KAP_U)
    arrived(kap_rows.at[2], KAP_D)
    for r in range(16):
        block, row = divmod(r + 4, 8)
        line = kap_rows[block, row : row + 1, :]
        if r < 4:
            line = jnp.where(t == 0, 0.0, line)
        if r >= 12:
            line = jnp.where(t == tiles - 1, 0.0, line)
        for h in range(2):
            wide = jnp.broadcast_to(line[:, h * LANES : (h + 1) * LANES], (8, LANES))
            kap[r, h] = wide
            if 4 <= r < 12:
                ikap[r - 4, h] = 1.0 / wide

    own.wait()
    arrived(in_buf.at[pl.ds(0, tiles - 1)], A2A)

    parts = [in_buf[:, 0, g * LANES : (g + 1) * LANES] for g in range(3)]
    pair = jnp.concatenate(parts[:2], axis=0).T
    last = jnp.concatenate([parts[2], parts[2]], axis=0).T
    for b in range(4):
        feat[b] = pair[b * FEATURES : (b + 1) * FEATURES, :]
    lane = lax.broadcasted_iota(jnp.int32, (FEATURES, LANES), 1)
    for b in range(2):
        one = last[2 * b * FEATURES : (2 * b + 1) * FEATURES, :]
        two = last[(2 * b + 1) * FEATURES : (2 * b + 2) * FEATURES, :]
        feat[4 + b] = jnp.where(lane < 64, one, two)
    blocks = 6

    def place(b, c):
        cell = feat[b, 16 + c : 17 + c, :].astype(jnp.int32)
        code = (cell & 1) * 8 + (cell >> 8)
        low = (cell & 255) >> 1
        return code, low

    def hits(code):
        return lax.broadcasted_iota(jnp.int32, (16, 8, LANES), 0) == code.reshape(1, 1, LANES)

    def build(b, carry):
        for c in range(4):
            low = place(b, c)[1]
            spot = lax.broadcasted_iota(jnp.int32, (LANES, LANES), 0) == low
            onehot[b, :, c * LANES : (c + 1) * LANES] = jnp.where(spot, 1.0, 0.0).astype(BF)
        return carry

    lax.fori_loop(0, blocks, build, 0)

    def adjoint_obs(b, z, total):
        jac = feat[b, 0:16, :]
        for c in range(4):
            code = place(b, c)[0]
            value = jac * (feat[b, 20 + c : 21 + c, :] * z)
            mask = hits(code)[None]
            for piece, where_to in zip(split2(value), (a_hi, a_lo)):
                wide = jnp.where(mask, piece.reshape(2, 1, 8, LANES), 0.0)
                where_to[:, c * LANES : (c + 1) * LANES] = wide.reshape(256, LANES).astype(BF)
        new = nt(a_hi[...], onehot[b]) + nt(a_lo[...], onehot[b])
        total[...] += new.reshape(4, 8, 8, LANES)

    def first(b, carry):
        z = -(feat[b, 25:26, :] * feat[b, 24:25, :])
        adjoint_obs(b, z, s0)
        return carry

    s0[...] = jnp.zeros(s0.shape, F32)
    lax.fori_loop(0, blocks, first, 0)

    def scatter(source, into, k):
        for d in range(1, groups):
            send(source.at[peer(d)], into.at[d - 1], k, t, peer(d))

    def spread(x, k, k_up, k_down):
        for d in range(1, groups):
            here = x.at[j, pl.ds(HALO, 8)]
            send(here, here, k, t, peer(d))
        for d in range(groups):
            send(x.at[j, pl.ds(8, 4)], x.at[j, pl.ds(0, 4)], k_up, south, peer(d))
            send(x.at[j, pl.ds(4, 4)], x.at[j, pl.ds(12, 4)], k_down, north, peer(d))
        arrived(x.at[pl.ds(0, groups - 1), pl.ds(HALO, 8)], k)
        arrived(x.at[:, pl.ds(0, 4)], k_up)
        arrived(x.at[:, pl.ds(12, 4)], k_down)

    scatter(s0, rs0, RS0)
    arrived(rs0, RS0)
    x0[j, pl.ds(HALO, 8)] = s0[j] + rs0[0] + rs0[1] + rs0[2]
    spread(x0, AG0, HU0, HD0)
    arrived(pert.at[pl.ds(0, 4)], PERT_U)
    arrived(pert.at[pl.ds(12, 4)], PERT_D)

    def sweep(f, lo, hi):
        out = {}
        for r in range(lo, hi):
            here = f.get(r)
            beside = [f[n] for n in (r - 1, r + 1) if n in f]
            pair = []
            for h in range(2):
                terms = [row[h] for row in beside]
                if here is not None:
                    other = here[1 - h]
                    terms.append(other + pltpu.roll(other, (1, LANES - 1)[h], 1))
                beside_all = functools.reduce(jnp.add, terms)
                if here is None:
                    pair.append(kap[r, h] * beside_all)
                else:
                    pair.append(here[h] + kap[r, h] * (beside_all - 4.0 * here[h]))
            out[r] = pair
        return out

    def local_pass(x, control_out):
        up[...] = jnp.zeros(up.shape, F32)
        together = 4

        def group(i, carry):
            ids = []
            for g in range(together):
                lh, m = g % 2, i * (together // 2) + g // 2
                ids.append((lh, m, pl.ds(pl.multiple_of(m * levels + lh * 8, 8), 8)))
            fields = [
                {
                    r: [kap[r, h] * pert[r, h, at, :] * x[lh * 2 + h, r] for h in range(2)]
                    for r in range(16)
                }
                for lh, m, at in ids
            ]
            for k in range(4):
                fields = [sweep(f, k + 1, 15 - k) for f in fields]
            fields = [
                {r: [f[r][h] * ikap[r - HALO, h] for h in range(2)] for r in f} for f in fields
            ]
            if control_out:
                for f, (lh, m, at) in zip(fields, ids):
                    for r in range(8):
                        place_at = pl.ds(m * 128 + lh * 64 + r, 8, stride=8)
                        for h in range(2):
                            flat[h, place_at, :] = f[HALO + r][h]
            for k in range(4):
                fields = [sweep(f, 3 - k, 13 + k) for f in fields]
            for r in range(16):
                for h in range(2):
                    for half in range(2):
                        terms = [
                            pert[r, h, at, :] * f[r][h]
                            for f, (lh, m, at) in zip(fields, ids)
                            if lh == half
                        ]
                        up[half * 2 + h, r] += functools.reduce(jnp.add, terms)
            return carry

        lax.fori_loop(0, 2 * members // together, group, 0)

    def reduce(source, near, from_north, from_south, k, k_up, k_down):
        for d in range(1, groups):
            q = peer(d)
            send(source.at[q, pl.ds(HALO, 8)], near.at[d - 1], k, t, q)
        for d in range(groups):
            q = peer(d)
            send(source.at[q, pl.ds(12, 4)], from_north.at[j], k_up, south, q)
            send(source.at[q, pl.ds(0, 4)], from_south.at[j], k_down, north, q)
        arrived(near, k)
        arrived(from_north, k_up)
        arrived(from_south, k_down)
        total = source[j, pl.ds(HALO, 8)] + near[0] + near[1] + near[2]
        top = from_north[0] + from_north[1] + from_north[2] + from_north[3]
        bottom = from_south[0] + from_south[1] + from_south[2] + from_south[3]
        return total + jnp.concatenate([top, bottom], axis=0)

    local_pass(x0, False)
    u[j] = (-STEP * scale * scale) * reduce(up, rsu, ruu, rud, RSU, RUU, RUD)
    for d in range(1, groups):
        send(u.at[j], u.at[j], AGU, t, peer(d))
    arrived(u.at[pl.ds(0, groups - 1)], AGU)

    state_hi, state_lo = (g.astype(BF) for g in split2(u[...].reshape(256, LANES)))

    def second(b, carry):
        state_h, state_l = carry
        mixed = nn(state_h, onehot[b]) + nn(state_l, onehot[b])
        jac = feat[b, 0:16, :].reshape(2, 8, LANES)
        total = jnp.zeros((2, 8, LANES), F32)
        for c in range(4):
            mask = hits(place(b, c)[0])[None]
            part = mixed[:, c * LANES : (c + 1) * LANES].reshape(2, 16, 8, LANES)
            picked = jnp.sum(jnp.where(mask, part, 0.0), axis=1)
            total = total + feat[b, 20 + c : 21 + c, :].reshape(1, 1, LANES) * picked
        y = jnp.sum((jac * total).reshape(16, LANES), axis=0, keepdims=True)
        z = feat[b, 25:26, :] * (y - feat[b, 24:25, :])
        adjoint_obs(b, z, s1)
        return carry

    s1[...] = jnp.zeros(s1.shape, F32)
    lax.fori_loop(0, blocks, second, (state_hi, state_lo))

    scatter(s1, rs1, RS1)
    arrived(rs1, RS1)
    x1[j, pl.ds(HALO, 8)] = (-scale * STEP) * (
        STEP * x0[j, pl.ds(HALO, 8)] + s1[j] + rs1[0] + rs1[1] + rs1[2]
    )
    spread(x1, AG1, HU1, HD1)
    sent(rsu, RSU)
    sent(ruu, RUU)
    sent(rud, RUD)
    local_pass(x1, True)

    sub = lax.broadcasted_iota(jnp.int32, (16, 8, LANES), 1)
    for lh in range(2):
        even, odd = up[lh * 2], up[lh * 2 + 1]
        vp[lh * 2] = jnp.where(sub < 4, even, pltpu.roll(odd, 4, 1))
        vp[lh * 2 + 1] = jnp.where(sub < 4, pltpu.roll(even, 4, 1), odd)

    def unmix(m, carry):
        rows = pl.ds(pl.multiple_of(m * 128, 128), 128)
        wide = jnp.concatenate([flat[0, rows, :], flat[1, rows, :]], axis=1)
        hi, lo = split2(wide)
        back = nn(hi.astype(BF), perm[1]) + nn(lo.astype(BF), perm[1])
        control_ref[m] = back.reshape(levels, 8, 256)
        return carry

    lax.fori_loop(0, members, unmix, 0)

    final = scale * reduce(vp, rsv, rvu, rvd, RSV, RVU, RVD)
    wide = jnp.concatenate(
        [final.reshape(64, LANES), pltpu.roll(final, 4, 1).reshape(64, LANES)], axis=1
    )
    hi, lo = split2(wide)
    back = nn(hi.astype(BF), perm[1]) + nn(lo.astype(BF), perm[1])
    for h in range(2):
        stage[h, 0:64, :] = back[:, h * LANES : (h + 1) * LANES]
        for level in range(4):
            incr_ref[level, :, h * LANES : (h + 1) * LANES] = stage[h, pl.ds(level, 8, stride=8), :]

    sent(in_buf.at[pl.ds(0, tiles - 1)], A2A)
    sent(kap_rows.at[0], KAP_U)
    sent(kap_rows.at[2], KAP_D)
    sent(pert.at[pl.ds(0, 4)], PERT_U)
    sent(pert.at[pl.ds(12, 4)], PERT_D)
    for k in (RS0, AG0, AGU, RS1, AG1, RSV):
        sent(rs0, k)
    for k in (HU0, HD0, HU1, HD1, RVU, RVD):
        sent(ruu, k)


def on_device(tiles, groups, perturbations, classes, target, cells, interp, jac, innov, inverse):
    members, levels, rows, cols = perturbations.shape
    obs = target.shape[0]
    vm = pl.BlockSpec(memory_space=pltpu.VMEM)
    hbm = pl.BlockSpec(memory_space=pltpu.HBM)
    quarter = (groups, 8, 8, LANES)
    window = (groups, 16, 8, LANES)
    near = (groups - 1, 8, 8, LANES)
    halo = (groups, 4, 8, LANES)
    scratch = [
        (perturbations.shape, perturbations.dtype),
        (classes.shape, classes.dtype),
        ((1, obs), target.dtype),
        (cells.shape, cells.dtype),
        (interp.shape, interp.dtype),
        (jac.shape, jac.dtype),
        ((1, obs), innov.dtype),
        ((1, obs), inverse.dtype),
        ((2, 256, 256), BF),
        ((FEATURES, obs), F32),
        ((3, FEATURES * (MOST // groups), obs), BF),
        ((tiles, 1, FEATURES * (MOST // groups)), F32),
        ((tiles, 1, FEATURES * (MOST // groups)), F32),
        ((6, FEATURES, LANES), F32),
        ((6, LANES, 4 * LANES), BF),
        ((256, 4 * LANES), BF),
        ((256, 4 * LANES), BF),
        ((16, 2, members * levels, LANES), F32),
        ((2, LANES, LANES), F32),
        ((3, 8, 256), F32),
        ((16, 2, 8, LANES), F32),
        ((8, 2, 8, LANES), F32),
        (quarter, F32), (quarter, F32),
        (near, F32), (near, F32),
        (window, F32), (window, F32),
        (window, F32),
        (near, F32), (halo, F32), (halo, F32),
        (quarter, F32),
        (window, F32),
        (near, F32), (halo, F32), (halo, F32),
        ((2, members * levels * rows, LANES), F32),
    ]
    return pl.pallas_call(
        functools.partial(kernel, tiles, groups, members),
        out_shape=(
            jax.ShapeDtypeStruct((members, levels, rows, cols), F32),
            jax.ShapeDtypeStruct((levels // groups, rows, cols), F32),
        ),
        in_specs=[hbm] * 8,
        out_specs=(vm, vm),
        scratch_shapes=[pltpu.VMEM(shape, dtype) for shape, dtype in scratch]
        + [
            pltpu.SemaphoreType.DMA((N_SEM,)),
            pltpu.SemaphoreType.DMA((N_SEM,)),
            pltpu.SemaphoreType.DMA((9,)),
        ],
        compiler_params=pltpu.CompilerParams(
            collective_id=0, has_side_effects=True, vmem_limit_bytes=40 * 1024 * 1024
        ),
        name="assimilate",
    )(
        perturbations, classes, target.reshape(1, obs), cells, interp, jac,
        innov.reshape(1, obs), inverse.reshape(1, obs),
    )


def solution(mesh):
    in_specs = (
        P("mem", None, "tile", None),
        P("tile", None),
        P("tile", None),
        P(None, "tile"),
        P(None, "tile"),
        P(None, "tile"),
        P("tile"),
        P("tile"),
    )
    out_specs = (P("mem", None, "tile", None), P("mem", "tile", None))
    return jax.shard_map(
        functools.partial(on_device, mesh.shape["tile"], mesh.shape["mem"]),
        mesh=mesh, in_specs=in_specs, out_specs=out_specs, check_vma=False,
    )
```

```python
import functools
import math

import jax
import jax.numpy as jnp
from jax import lax
from jax.experimental import pallas as pl
from jax.experimental.pallas import tpu as pltpu
from jax.sharding import PartitionSpec as P

MESH = pl.DeviceIdType.MESH
BF = jnp.bfloat16
F32 = jnp.float32
DIFFUSIVITIES = (0.06, 0.1, 0.15, 0.22)
STEP = 0.5
MOST = 48
FEATURES = 32
HALO = 4
LANES = 128

(A2A, KAP_U, KAP_D, PERT_U, PERT_D, OBS, AC0, AZ0, AU0, AD0, FZ0, FU0, FD0, CR0, RZ0, RU0, RD0, YS,
 AC1, AZ1, AU1, AD1, FZ1, FU1, FD1, CR1, RZ1, RU1, RD1, N_SEM) = range(30)


def nt(a, b):
    return lax.dot_general(a, b, (((1,), (1,)), ((), ())), preferred_element_type=F32)


def nn(a, b):
    return jnp.dot(a, b, preferred_element_type=F32)


def split2(x):
    hi = x.astype(BF).astype(F32)
    return hi, x - hi


def kernel(
    tiles, groups, members,
    pert_hbm, classes_hbm, target_hbm, cells_hbm, interp_hbm, jac_hbm, innov_hbm, inv_hbm,
    control_ref, incr_ref,
    pert_ref, classes_ref, target_ref, cells_ref, interp_ref, jac_ref, innov_ref, inv_ref,
    perm, pay, val, out_buf, in_buf, feat, onehot, acols, acc,
    pert, stage, kap_rows, kap, ikap,
    x0, x1, up, vp, cr0, cs0, rz0, ru0, rd0, cr1, cs1, rz1, ru1, rd1, y_own, y_far, flat, ready,
    ssem, rsem, lsem,
):
    t = lax.axis_index("tile")
    j = lax.axis_index("mem")
    north, south = lax.rem(t + tiles - 1, tiles), lax.rem(t + 1, tiles)
    cores = 2
    chip, core = j // cores, lax.rem(j, cores)
    slots = MOST // cores
    levels = 16
    scale = 1.0 / math.sqrt(members * groups - 1)
    obs = pay.shape[1]

    sibling = j + 1 - 2 * core
    across = lax.rem(j + cores, groups)

    def peer(d):
        return lax.rem(j + d, groups)

    def band(d):
        return lax.rem(t + d, tiles)

    def send(src, dst, k, tile, mem):
        pltpu.make_async_remote_copy(
            src_ref=src, dst_ref=dst, send_sem=ssem.at[k], recv_sem=rsem.at[k],
            device_id={"tile": tile, "mem": mem}, device_id_type=MESH,
        ).start()

    def arrived(like, k):
        pltpu.make_async_copy(like, like, rsem.at[k]).wait()

    def sent(like, k):
        pltpu.make_async_copy(like, like, ssem.at[k]).wait()

    fetches = [
        pltpu.make_async_copy(source, into, lsem.at[1 + k])
        for k, (source, into) in enumerate((
            (target_hbm, target_ref), (cells_hbm, cells_ref), (interp_hbm, interp_ref),
            (jac_hbm, jac_ref), (innov_hbm, innov_ref), (inv_hbm, inv_ref),
            (pert_hbm, pert_ref), (classes_hbm, classes_ref),
        ))
    ]
    for fetch in fetches:
        fetch.start()

    barrier = pltpu.get_barrier_semaphore()

    def greet(tile, mem):
        pl.semaphore_signal(
            barrier, inc=1, device_id={"tile": tile, "mem": mem}, device_id_type=MESH
        )

    def greet_band(d, carry):
        greet(band(d), j)
        return carry

    lax.fori_loop(1, tiles, greet_band, 0)
    for d in range(1, groups):
        greet(t, peer(d))
    greet(north, across)
    greet(south, across)

    row_id = lax.broadcasted_iota(jnp.int32, (256, 256), 0)
    col_id = lax.broadcasted_iota(jnp.int32, (256, 256), 1)
    perm[0] = jnp.where(col_id == (row_id & 1) * 128 + (row_id >> 1), 1.0, 0.0).astype(BF)
    perm[1] = jnp.where(row_id == (col_id & 1) * 128 + (col_id >> 1), 1.0, 0.0).astype(BF)

    for fetch in fetches[:6]:
        fetch.wait()

    target = target_ref[...]
    bands = lax.broadcasted_iota(jnp.int32, (tiles, obs), 0)
    member_of = jnp.where(target == bands, 1.0, 0.0)
    member_bf = member_of.astype(BF)
    before = jnp.where(row_id < col_id, 1.0, 0.0).astype(BF)
    base = jnp.zeros((tiles, 1), F32)
    ranks = []
    for b in range(obs // 256):
        part = slice(b * 256, (b + 1) * 256)
        count = nn(member_bf[:, part], before) + base
        ranks.append(jnp.sum(member_of[:, part] * count, axis=0, keepdims=True))
        base = base + jnp.sum(member_of[:, part], axis=1, keepdims=True)
    rank = jnp.concatenate(ranks, axis=1).astype(jnp.int32) - core * slots

    pay[0:16, :] = jac_ref[...]
    pay[16:24, :] = jnp.concatenate([cells_ref[...].astype(F32), interp_ref[...]], axis=0)
    pay[24:32, :] = jnp.concatenate(
        [innov_ref[...], inv_ref[...], jnp.zeros((6, obs), F32)], axis=0
    )
    whole = pay[...]
    high = whole.astype(BF).astype(F32)
    rest = whole - high
    middle = rest.astype(BF).astype(F32)
    low = rest - middle
    for q in range(slots):
        mine = rank == q
        for k, piece in enumerate((high, middle, low)):
            val[k, q * FEATURES : (q + 1) * FEATURES, :] = jnp.where(mine, piece, 0.0).astype(BF)
    packed = nt(member_bf, val[0]) + nt(member_bf, val[1]) + nt(member_bf, val[2])
    out_buf[:, 0, :] = packed

    for fetch in fetches[6:]:
        fetch.wait()

    def arrange(m, carry):
        block = pert_ref[m].astype(F32).reshape(levels * 8, 256).astype(BF)
        moved = nn(block, perm[0])
        stage[0] = moved[:, :LANES]
        stage[1] = moved[:, LANES:]
        for r in range(8):
            for lh in range(2):
                at = pl.ds(pl.multiple_of(m * levels + lh * 8, 8), 8)
                for h in range(2):
                    pert[HALO + r, h, at, :] = stage[h, pl.ds(lh * 64 + r, 8, stride=8), :]
        return carry

    lax.fori_loop(0, members, arrange, 0)

    classes = nn(classes_ref[...].astype(F32).astype(BF), perm[0])
    kappa = jnp.zeros(classes.shape, F32)
    for position, coefficient in enumerate(DIFFUSIVITIES):
        kappa = kappa + jnp.where(classes == float(position), coefficient, 0.0)
    kap_rows[1] = kappa

    pl.semaphore_wait(barrier, tiles - 1 + groups - 1 + 2)

    def send_band(d, carry):
        send(out_buf.at[band(d)], in_buf.at[core, t], A2A, band(d), j)
        return carry

    lax.fori_loop(1, tiles, send_band, 0)
    own = pltpu.make_async_copy(out_buf.at[t], in_buf.at[core, t], lsem.at[0])
    own.start()
    send(kap_rows.at[1], kap_rows.at[0], KAP_U, south, j)
    send(kap_rows.at[1], kap_rows.at[2], KAP_D, north, j)
    send(pert.at[pl.ds(8, 4)], pert.at[pl.ds(0, 4)], PERT_U, south, j)
    send(pert.at[pl.ds(4, 4)], pert.at[pl.ds(12, 4)], PERT_D, north, j)

    arrived(kap_rows.at[0], KAP_U)
    arrived(kap_rows.at[2], KAP_D)
    for r in range(16):
        block, row = divmod(r + 4, 8)
        line = kap_rows[block, row : row + 1, :]
        if r < 4:
            line = jnp.where(t == 0, 0.0, line)
        if r >= 12:
            line = jnp.where(t == tiles - 1, 0.0, line)
        for h in range(2):
            wide = jnp.broadcast_to(line[:, h * LANES : (h + 1) * LANES], (8, LANES))
            kap[r, h] = wide
            if 4 <= r < 12:
                ikap[r - 4, h] = 1.0 / wide

    own.wait()
    arrived(in_buf.at[core, pl.ds(0, tiles - 1)], A2A)
    send(in_buf.at[core], in_buf.at[core], OBS, t, sibling)
    arrived(in_buf.at[1 - core], OBS)

    blocks = 0
    for source in range(cores):
        for g in range(0, slots * FEATURES // LANES, 2):
            both = jnp.concatenate(
                [
                    in_buf[source, :, 0, n * LANES : (n + 1) * LANES]
                    for n in (g, g + 1)
                ],
                axis=0,
            ).T
            for b in range(LANES // FEATURES):
                feat[blocks] = both[b * FEATURES : (b + 1) * FEATURES, :]
                blocks += 1
    along = 4

    def in_turn(step):
        def several(i, carry):
            step([i * along + n for n in range(along)])
            return carry

        lax.fori_loop(0, blocks // along, several, 0)

    my_levels = pl.ds(pl.multiple_of(chip * 8, 8), 8)

    def hits(b, c):
        cell = feat[b, 16 + c : 17 + c, :].astype(jnp.int32)
        row = jnp.where((cell & 1) == core, cell >> 8, -1)
        rows = lax.broadcasted_iota(jnp.int32, (8, 8, LANES), 0)
        return rows == row.reshape(1, 1, LANES)

    def build(which):
        for b in which:
            for c in range(4):
                low = (feat[b, 16 + c : 17 + c, :].astype(jnp.int32) & 255) >> 1
                spot = lax.broadcasted_iota(jnp.int32, (LANES, LANES), 0) == low
                onehot[b, :, c * LANES : (c + 1) * LANES] = jnp.where(spot, 1.0, 0.0).astype(BF)

    def adjoint_obs(which, residual):
        for n, b in enumerate(which):
            z = residual(b)
            jac = feat[b, my_levels, :]
            for c in range(4):
                value = jac * (feat[b, 20 + c : 21 + c, :] * z)
                mask = hits(b, c)
                for k, piece in enumerate(split2(value)):
                    wide = jnp.where(mask, piece.reshape(1, 8, LANES), 0.0).reshape(64, LANES)
                    acols[n, k * 64 : (k + 1) * 64, c * LANES : (c + 1) * LANES] = wide.astype(BF)
        total = acc[...]
        for n, b in enumerate(which):
            total = total + nt(acols[n], onehot[b])
        acc[...] = total

    def summed():
        both = acc[...]
        return (both[:64] + both[64:]).reshape(8, 8, LANES)

    def first(which):
        build(which)
        adjoint_obs(which, lambda b: -(feat[b, 25:26, :] * feat[b, 24:25, :]))

    acc[...] = jnp.zeros(acc.shape, F32)
    in_turn(first)
    x0[j, pl.ds(HALO, 8)] = summed()

    def spread(x, s_core, s_across, s_up, s_down, f_across, f_up, f_down):
        here = x.at[j, pl.ds(HALO, 8)]
        for to in (j, across):
            send(x.at[j, pl.ds(8, 4)], x.at[j, pl.ds(0, 4)], s_up, south, to)
            send(x.at[j, pl.ds(4, 4)], x.at[j, pl.ds(12, 4)], s_down, north, to)
        send(here, here, s_across, t, across)
        send(here, here, s_core, t, sibling)
        got = x.at[across, pl.ds(HALO, 8)]
        arrived(got, s_across)
        send(got, got, f_across, t, sibling)
        for key, forward, first_row in ((s_up, f_up, 0), (s_down, f_down, 12)):
            rows = pl.ds(first_row, 4)
            arrived(x.at[pl.ds(0, 2), rows], key)
            for half in range(2):
                edge = x.at[half * cores + core, rows]
                send(edge, edge, forward, t, sibling)
        arrived(here, s_core)
        arrived(got, f_across)
        arrived(x.at[pl.ds(0, 2), pl.ds(0, 4)], f_up)
        arrived(x.at[pl.ds(0, 2), pl.ds(12, 4)], f_down)

    spread(x0, AC0, AZ0, AU0, AD0, FZ0, FU0, FD0)
    arrived(pert.at[pl.ds(0, 4)], PERT_U)
    arrived(pert.at[pl.ds(12, 4)], PERT_D)

    def sweep(f, lo, hi):
        out = {}
        for r in range(lo, hi):
            here = f.get(r)
            beside = [f[n] for n in (r - 1, r + 1) if n in f]
            pair = []
            for h in range(2):
                terms = [row[h] for row in beside]
                if here is not None:
                    other = here[1 - h]
                    terms.append(other + pltpu.roll(other, (1, LANES - 1)[h], 1))
                beside_all = functools.reduce(jnp.add, terms)
                if here is None:
                    pair.append(kap[r, h] * beside_all)
                else:
                    pair.append(here[h] + kap[r, h] * (beside_all - 4.0 * here[h]))
            out[r] = pair
        return out

    def local_pass(x, control_out):
        up[...] = jnp.zeros(up.shape, F32)
        together = 4

        def group(i, carry):
            ids = []
            for g in range(together):
                lh, m = g % 2, i * (together // 2) + g // 2
                ids.append((lh, m, pl.ds(pl.multiple_of(m * levels + lh * 8, 8), 8)))
            fields = [
                {
                    r: [kap[r, h] * pert[r, h, at, :] * x[lh * 2 + h, r] for h in range(2)]
                    for r in range(16)
                }
                for lh, m, at in ids
            ]
            for k in range(4):
                fields = [sweep(f, k + 1, 15 - k) for f in fields]
            fields = [
                {r: [f[r][h] * ikap[r - HALO, h] for h in range(2)] for r in f} for f in fields
            ]
            if control_out:
                for f, (lh, m, at) in zip(fields, ids):
                    for r in range(8):
                        place_at = pl.ds(m * 128 + lh * 64 + r, 8, stride=8)
                        for h in range(2):
                            flat[h, place_at, :] = f[HALO + r][h]
            for k in range(4):
                fields = [sweep(f, 3 - k, 13 + k) for f in fields]
            for r in range(16):
                for h in range(2):
                    for half in range(2):
                        terms = [
                            pert[r, h, at, :] * f[r][h]
                            for f, (lh, m, at) in zip(fields, ids)
                            if lh == half
                        ]
                        up[half * 2 + h, r] += functools.reduce(jnp.add, terms)
            return carry

        lax.fori_loop(0, 2 * members // together, group, 0)

    def reduce_in_chip(source, from_core, key):
        for half in range(2):
            send(source.at[half * cores + 1 - core], from_core.at[half], key, t, sibling)

    def reduce_out(source, from_core, chip_sum, from_chip, from_north, from_south, keys):
        key, k_across, k_up, k_down = keys
        arrived(from_core, key)
        for half in range(2):
            chip_sum[half] = source[half * cores + core] + from_core[half]
        for half in range(2):
            to = half * cores + core
            send(chip_sum.at[half, pl.ds(12, 4)], from_north.at[chip], k_up, south, to)
            send(chip_sum.at[half, pl.ds(0, 4)], from_south.at[chip], k_down, north, to)
        send(chip_sum.at[1 - chip, pl.ds(HALO, 8)], from_chip, k_across, t, across)

    def reduced(chip_sum, from_chip, from_north, from_south, keys):
        key, k_across, k_up, k_down = keys
        arrived(from_chip, k_across)
        arrived(from_north, k_up)
        arrived(from_south, k_down)
        total = chip_sum[chip, pl.ds(HALO, 8)] + from_chip[...]
        edges = [from_north[0] + from_north[1], from_south[0] + from_south[1]]
        return total + jnp.concatenate(edges, axis=0)

    local_pass(x0, False)
    keys = (CR0, RZ0, RU0, RD0)
    reduce_in_chip(up, cr0, CR0)
    reduce_out(up, cr0, cs0, rz0, ru0, rd0, keys)
    state = (-STEP * scale * scale) * reduced(cs0, rz0, ru0, rd0, keys)
    state = jnp.concatenate(split2(state.reshape(64, LANES)), axis=0).astype(BF)

    def observe(which):
        for b in which:
            mixed = nn(state, onehot[b])
            mixed = mixed[:64] + mixed[64:]
            total = jnp.zeros((8, LANES), F32)
            for c in range(4):
                part = mixed[:, c * LANES : (c + 1) * LANES].reshape(8, 8, LANES)
                picked = jnp.sum(jnp.where(hits(b, c), part, 0.0), axis=0)
                total = total + feat[b, 20 + c : 21 + c, :] * picked
            y_own[b] = jnp.sum(feat[b, my_levels, :] * total, axis=0, keepdims=True)

    in_turn(observe)
    for d in range(1, groups):
        send(y_own, y_far.at[d - 1], YS, t, peer(d))
    arrived(y_far, YS)

    def misfit(b):
        y = y_own[b] + y_far[0, b] + y_far[1, b] + y_far[2, b]
        return feat[b, 25:26, :] * (y - feat[b, 24:25, :])

    acc[...] = jnp.zeros(acc.shape, F32)
    in_turn(lambda which: adjoint_obs(which, misfit))
    x1[j, pl.ds(HALO, 8)] = (-scale * STEP) * (STEP * x0[j, pl.ds(HALO, 8)] + summed())
    spread(x1, AC1, AZ1, AU1, AD1, FZ1, FU1, FD1)
    sent(cr0, CR0)
    local_pass(x1, True)

    sub = lax.broadcasted_iota(jnp.int32, (16, 8, LANES), 1)
    for lh in range(2):
        even, odd = up[lh * 2], up[lh * 2 + 1]
        vp[lh * 2] = jnp.where(sub < 4, even, pltpu.roll(odd, 4, 1))
        vp[lh * 2 + 1] = jnp.where(sub < 4, pltpu.roll(even, 4, 1), odd)

    def in_order(wide):
        hi, lo = split2(wide)
        return nn(hi.astype(BF), perm[1]) + nn(lo.astype(BF), perm[1])

    def written(m):
        return pltpu.make_async_copy(ready.at[m], control_ref.at[m], lsem.at[9 + m])

    def unmix(m):
        rows = pl.ds(m * 128, 128)
        wide = jnp.concatenate([flat[0, rows, :], flat[1, rows, :]], axis=1)
        ready[m] = in_order(wide).reshape(levels, 8, 256)
        written(m).start()

    keys = (CR1, RZ1, RU1, RD1)
    reduce_in_chip(vp, cr1, CR1)
    for m in range(members // 4):
        unmix(m)
    reduce_out(vp, cr1, cs1, rz1, ru1, rd1, keys)
    for m in range(members // 4, members):
        unmix(m)
    final = scale * reduced(cs1, rz1, ru1, rd1, keys)
    back = in_order(
        jnp.concatenate(
            [final.reshape(64, LANES), pltpu.roll(final, 4, 1).reshape(64, LANES)], axis=1
        )
    )
    for h in range(2):
        stage[h, 0:64, :] = back[:, h * LANES : (h + 1) * LANES]
        for level in range(4):
            incr_ref[level, :, h * LANES : (h + 1) * LANES] = stage[h, pl.ds(level, 8, stride=8), :]
    for m in range(members):
        written(m).wait()

    sent(in_buf.at[core, pl.ds(0, tiles - 1)], A2A)
    sent(kap_rows.at[0], KAP_U)
    sent(kap_rows.at[2], KAP_D)
    sent(pert.at[pl.ds(0, 4)], PERT_U)
    sent(pert.at[pl.ds(12, 4)], PERT_D)
    sent(in_buf.at[core], OBS)
    sent(y_far, YS)
    sent(cr1, CR1)
    for k in (AC0, AZ0, FZ0, RZ0, AC1, AZ1, FZ1, RZ1):
        sent(rz0, k)
    for k in (AU0, AD0, FU0, FD0, RU0, RD0, AU1, AD1, FU1, FD1, RU1, RD1):
        sent(ru0, k)


def on_device(tiles, groups, perturbations, classes, target, cells, interp, jac, innov, inverse):
    members, levels, rows, cols = perturbations.shape
    obs = target.shape[0]
    vm = pl.BlockSpec(memory_space=pltpu.VMEM)
    hbm = pl.BlockSpec(memory_space=pltpu.HBM)
    window = (groups, 16, 8, LANES)
    message = FEATURES * MOST // 2
    blocks = MOST * tiles // LANES
    reduction = [
        ((2, 16, 8, LANES), F32), ((2, 16, 8, LANES), F32), ((8, 8, LANES), F32),
        ((2, 4, 8, LANES), F32), ((2, 4, 8, LANES), F32),
    ]
    scratch = [
        (perturbations.shape, perturbations.dtype),
        (classes.shape, classes.dtype),
        ((1, obs), target.dtype),
        (cells.shape, cells.dtype),
        (interp.shape, interp.dtype),
        (jac.shape, jac.dtype),
        ((1, obs), innov.dtype),
        ((1, obs), inverse.dtype),
        ((2, 256, 256), BF),
        ((FEATURES, obs), F32),
        ((3, message, obs), BF),
        ((tiles, 1, message), F32),
        ((2, tiles, 1, message), F32),
        ((blocks, FEATURES, LANES), F32),
        ((blocks, LANES, 4 * LANES), BF),
        ((4, 128, 4 * LANES), BF),
        ((128, LANES), F32),
        ((16, 2, members * levels, LANES), F32),
        ((2, LANES, LANES), F32),
        ((3, 8, 256), F32),
        ((16, 2, 8, LANES), F32),
        ((8, 2, 8, LANES), F32),
        (window, F32), (window, F32), (window, F32), (window, F32),
        *reduction,
        *reduction,
        ((blocks, 1, LANES), F32),
        ((groups - 1, blocks, 1, LANES), F32),
        ((2, members * levels * rows, LANES), F32),
        ((members, levels, rows, cols), F32),
    ]
    return pl.pallas_call(
        functools.partial(kernel, tiles, groups, members),
        out_shape=(
            jax.ShapeDtypeStruct((members, levels, rows, cols), F32),
            jax.ShapeDtypeStruct((levels // groups, rows, cols), F32),
        ),
        in_specs=[hbm] * 8,
        out_specs=(hbm, vm),
        scratch_shapes=[pltpu.VMEM(shape, dtype) for shape, dtype in scratch]
        + [
            pltpu.SemaphoreType.DMA((N_SEM,)),
            pltpu.SemaphoreType.DMA((N_SEM,)),
            pltpu.SemaphoreType.DMA((9 + members,)),
        ],
        compiler_params=pltpu.CompilerParams(
            collective_id=0, has_side_effects=True, vmem_limit_bytes=60 * 1024 * 1024
        ),
        name="assimilate",
    )(
        perturbations, classes, target.reshape(1, obs), cells, interp, jac,
        innov.reshape(1, obs), inverse.reshape(1, obs),
    )


def solution(mesh):
    in_specs = (
        P("mem", None, "tile", None),
        P("tile", None),
        P("tile", None),
        P(None, "tile"),
        P(None, "tile"),
        P(None, "tile"),
        P("tile"),
        P("tile"),
    )
    out_specs = (P("mem", None, "tile", None), P("mem", "tile", None))
    return jax.shard_map(
        functools.partial(on_device, mesh.shape["tile"], mesh.shape["mem"]),
        mesh=mesh, in_specs=in_specs, out_specs=out_specs, check_vma=False,
    )
```

```python
import functools
import math

import jax
import jax.numpy as jnp
from jax import lax
from jax.experimental import pallas as pl
from jax.experimental.pallas import tpu as pltpu
from jax.sharding import PartitionSpec as P

MESH = pl.DeviceIdType.MESH
BF = jnp.bfloat16
F32 = jnp.float32
DIFFUSIVITIES = (0.06, 0.1, 0.15, 0.22)
STEP = 0.5
MOST = 48
FEATURES = 32
HALO = 4
LANES = 128

(A2A, KAP_U, KAP_D, OBS, AC0, AZ0, AU0, AD0, FZ0, FU0, FD0, CR0, RZ0, RU0, RD0, YS,
 AC1, AZ1, AU1, AD1, FZ1, FU1, FD1, CR1, RZ1, RU1, RD1, PERT) = range(28)
PARTS = ((0, 32), (32, 64), (64, 128))
EARLY = 1
N_SEM = PERT + 8 * len(PARTS)


def nt(a, b):
    return lax.dot_general(a, b, (((1,), (1,)), ((), ())), preferred_element_type=F32)


def nn(a, b):
    return jnp.dot(a, b, preferred_element_type=F32)


def split2(x):
    hi = x.astype(BF).astype(F32)
    return hi, x - hi


def kernel(
    tiles, groups, members,
    pert_hbm, classes_hbm, target_hbm, cells_hbm, interp_hbm, jac_hbm, innov_hbm, inv_hbm,
    control_ref, incr_ref,
    pert_ref, classes_ref, target_ref, cells_ref, interp_ref, jac_ref, innov_ref, inv_ref,
    perm, pay, val, out_buf, in_buf, feat, onehot, acols, acc,
    pert, stage, kap_rows, kap, ikap,
    x0, x1, up, vp, cr0, cs0, rz0, ru0, rd0, cr1, cs1, rz1, ru1, rd1, y_own, y_far, flat, ready, relay,
    ssem, rsem, lsem,
):
    t = lax.axis_index("tile")
    j = lax.axis_index("mem")
    north, south = lax.rem(t + tiles - 1, tiles), lax.rem(t + 1, tiles)
    cores = 2
    chip, core = j // cores, lax.rem(j, cores)
    slots = MOST // cores
    levels = 16
    scale = 1.0 / math.sqrt(members * groups - 1)
    obs = pay.shape[1]
    early = EARLY

    sibling = j + 1 - 2 * core
    across = lax.rem(j + cores, groups)

    def peer(d):
        return lax.rem(j + d, groups)

    def band(d):
        return lax.rem(t + d, tiles)

    def send(src, dst, k, tile, mem, k_out=None):
        pltpu.make_async_remote_copy(
            src_ref=src, dst_ref=dst, send_sem=ssem.at[k if k_out is None else k_out], recv_sem=rsem.at[k],
            device_id={"tile": tile, "mem": mem}, device_id_type=MESH,
        ).start()

    def arrived(like, k):
        pltpu.make_async_copy(like, like, rsem.at[k]).wait()

    def sent(like, k):
        pltpu.make_async_copy(like, like, ssem.at[k]).wait()

    fetches = [
        pltpu.make_async_copy(source, into, lsem.at[1 + k])
        for k, (source, into) in enumerate((
            (target_hbm, target_ref), (cells_hbm, cells_ref), (interp_hbm, interp_ref),
            (jac_hbm, jac_ref), (innov_hbm, innov_ref), (inv_hbm, inv_ref),
            (pert_hbm, pert_ref), (classes_hbm, classes_ref),
        ))
    ]
    for fetch in fetches:
        fetch.start()

    barrier = pltpu.get_barrier_semaphore()

    def greet(tile, mem):
        pl.semaphore_signal(
            barrier, inc=1, device_id={"tile": tile, "mem": mem}, device_id_type=MESH
        )

    def greet_band(d, carry):
        greet(band(d), j)
        return carry

    lax.fori_loop(1, tiles, greet_band, 0, unroll=9)
    for d in range(1, groups):
        greet(t, peer(d))
    greet(north, across)
    greet(south, across)

    row_id = lax.broadcasted_iota(jnp.int32, (256, 256), 0)
    col_id = lax.broadcasted_iota(jnp.int32, (256, 256), 1)
    perm[0] = jnp.where(col_id == (row_id & 1) * 128 + (row_id >> 1), 1.0, 0.0).astype(BF)
    perm[1] = jnp.where(row_id == (col_id & 1) * 128 + (col_id >> 1), 1.0, 0.0).astype(BF)

    for fetch in fetches[:6]:
        fetch.wait()

    target = target_ref[...]
    bands = lax.broadcasted_iota(jnp.int32, (tiles, obs), 0)
    member_of = jnp.where(target == bands, 1.0, 0.0)
    member_bf = member_of.astype(BF)
    before = jnp.where(row_id < col_id, 1.0, 0.0).astype(BF)
    base = jnp.zeros((tiles, 1), F32)
    ranks = []
    for b in range(obs // 256):
        part = slice(b * 256, (b + 1) * 256)
        count = nn(member_bf[:, part], before) + base
        ranks.append(jnp.sum(member_of[:, part] * count, axis=0, keepdims=True))
        base = base + jnp.sum(member_of[:, part], axis=1, keepdims=True)
    rank = jnp.concatenate(ranks, axis=1).astype(jnp.int32) - core * slots

    pay[0:16, :] = jac_ref[...]
    pay[16:24, :] = jnp.concatenate([cells_ref[...].astype(F32), interp_ref[...]], axis=0)
    pay[24:32, :] = jnp.concatenate(
        [innov_ref[...], inv_ref[...], jnp.zeros((6, obs), F32)], axis=0
    )
    whole = pay[...]
    high = whole.astype(BF).astype(F32)
    rest = whole - high
    middle = rest.astype(BF).astype(F32)
    low = rest - middle
    for q in range(slots):
        mine = rank == q
        for k, piece in enumerate((high, middle, low)):
            val[k, q * FEATURES : (q + 1) * FEATURES, :] = jnp.where(mine, piece, 0.0).astype(BF)
    packed = nt(member_bf, val[0]) + nt(member_bf, val[1]) + nt(member_bf, val[2])
    out_buf[:, 0, :] = packed

    for fetch in fetches[6:]:
        fetch.wait()

    def arrange(m, carry):
        block = pert_ref[m].astype(F32).reshape(levels * 8, 256).astype(BF)
        moved = nn(block, perm[0])
        stage[0] = moved[:, :LANES]
        stage[1] = moved[:, LANES:]
        for r in range(8):
            for lh in range(2):
                at = pl.ds(pl.multiple_of(m * levels + lh * 8, 8), 8)
                for h in range(2):
                    pert[HALO + r, h, at, :] = stage[h, pl.ds(lh * 64 + r, 8, stride=8), :]
        return carry

    lax.fori_loop(0, members, arrange, 0)

    classes = nn(classes_ref[...].astype(F32).astype(BF), perm[0])
    kappa = jnp.zeros(classes.shape, F32)
    for position, coefficient in enumerate(DIFFUSIVITIES):
        kappa = kappa + jnp.where(classes == float(position), coefficient, 0.0)
    kap_rows[1] = kappa

    pl.semaphore_wait(barrier, tiles - 1 + groups - 1 + 2)

    along_x = lax.rem(t, 4)
    ways = (
        (8, 0, south, 3, -3, 4),
        (4, 12, north, 0, 3, -4),
    )

    def edge(first_row, lo, hi):
        return pert.at[pl.ds(first_row, 4), :, pl.ds(lo, hi - lo)]

    def shares(part):
        lo, hi = PARTS[part]
        middle = (lo + hi) // 2
        return (lo, middle), (middle, hi)

    def key_of(way, part):
        return PERT + (way * len(PARTS) + part) * 4

    def waiting(way, part):
        lo, hi = shares(part)[1]
        return relay.at[way, :, :, pl.ds(PARTS[part][0] // 2, hi - lo)]

    def send_part(part):
        one, two = shares(part)
        for way, (here, there, to, wraps, hop, onward) in enumerate(ways):
            key = key_of(way, part)

            @pl.when(along_x == wraps)
            def _():
                send(edge(here, *two), waiting(way, part), key + 2, band(hop + tiles), j)

            send(edge(here, *one), edge(there, *one), key, to, j)

            @pl.when(along_x != wraps)
            def _():
                send(edge(here, *two), edge(there, *two), key + 1, to, j)

    def forward_part(part):
        two = shares(part)[1]
        for way, (here, there, to, wraps, hop, onward) in enumerate(ways):
            key = key_of(way, part)

            @pl.when(along_x == 3 - wraps)
            def _():
                arrived(waiting(way, part), key + 2)
                send(
                    waiting(way, part), edge(there, *two), key + 1, band(onward + tiles), j, key + 3
                )

    def part_arrived(part):
        one, two = shares(part)
        for way, (here, there, to, wraps, hop, onward) in enumerate(ways):
            arrived(edge(there, *one), key_of(way, part))
            arrived(edge(there, *two), key_of(way, part) + 1)

    def part_sent(part):
        one, two = shares(part)
        for way, (here, there, to, wraps, hop, onward) in enumerate(ways):
            key = key_of(way, part)
            sent(edge(here, *one), key)

            @pl.when(along_x == wraps)
            def _():
                sent(edge(here, *two), key + 2)

            @pl.when(along_x != wraps)
            def _():
                sent(edge(here, *two), key + 1)

            @pl.when(along_x == 3 - wraps)
            def _():
                sent(waiting(way, part), key + 3)

    send(kap_rows.at[1], kap_rows.at[0], KAP_U, south, j)
    send(kap_rows.at[1], kap_rows.at[2], KAP_D, north, j)
    for part in range(early):
        send_part(part)

    def send_band(d, carry):
        send(out_buf.at[band(d)], in_buf.at[core, t], A2A, band(d), j)
        return carry

    lax.fori_loop(1, tiles, send_band, 0, unroll=9)
    for part in range(early, len(PARTS)):
        send_part(part)
    for part in range(early):
        forward_part(part)
    own = pltpu.make_async_copy(out_buf.at[t], in_buf.at[core, t], lsem.at[0])
    own.start()
    arrived(kap_rows.at[0], KAP_U)
    arrived(kap_rows.at[2], KAP_D)
    for r in range(16):
        block, row = divmod(r + 4, 8)
        line = kap_rows[block, row : row + 1, :]
        if r < 4:
            line = jnp.where(t == 0, 0.0, line)
        if r >= 12:
            line = jnp.where(t == tiles - 1, 0.0, line)
        for h in range(2):
            wide = jnp.broadcast_to(line[:, h * LANES : (h + 1) * LANES], (8, LANES))
            kap[r, h] = wide
            if 4 <= r < 12:
                ikap[r - 4, h] = 1.0 / wide

    own.wait()
    arrived(in_buf.at[core, pl.ds(0, tiles - 1)], A2A)
    send(in_buf.at[core], in_buf.at[core], OBS, t, sibling)
    for part in range(early, len(PARTS)):
        forward_part(part)

    blocks = MOST * tiles // LANES
    per_core = blocks // cores

    def unpack(source):
        for g in range(0, slots * FEATURES // LANES, 2):
            both = jnp.concatenate(
                [in_buf[source, :, 0, n * LANES : (n + 1) * LANES] for n in (g, g + 1)], axis=0
            ).T
            for b in range(LANES // FEATURES):
                at = source * per_core + g * 2 + b
                feat[at] = both[b * FEATURES : (b + 1) * FEATURES, :]

    along = 4

    def in_turn(step, start=0, count=blocks):
        def several(i, carry):
            step([start + i * along + n for n in range(along)])
            return carry

        lax.fori_loop(0, count // along, several, 0)

    my_levels = pl.ds(pl.multiple_of(chip * 8, 8), 8)

    def hits(b, c):
        cell = feat[b, 16 + c : 17 + c, :].astype(jnp.int32)
        row = jnp.where((cell & 1) == core, cell >> 8, -1)
        rows = lax.broadcasted_iota(jnp.int32, (8, 8, LANES), 0)
        return rows == row.reshape(1, 1, LANES)

    def build(which):
        for b in which:
            for c in range(4):
                low = (feat[b, 16 + c : 17 + c, :].astype(jnp.int32) & 255) >> 1
                spot = lax.broadcasted_iota(jnp.int32, (LANES, LANES), 0) == low
                onehot[b, :, c * LANES : (c + 1) * LANES] = jnp.where(spot, 1.0, 0.0).astype(BF)

    def adjoint_obs(which, residual):
        for n, b in enumerate(which):
            z = residual(b)
            jac = feat[b, my_levels, :]
            for c in range(4):
                value = jac * (feat[b, 20 + c : 21 + c, :] * z)
                mask = hits(b, c)
                for k, piece in enumerate(split2(value)):
                    wide = jnp.where(mask, piece.reshape(1, 8, LANES), 0.0).reshape(64, LANES)
                    acols[n, k * 64 : (k + 1) * 64, c * LANES : (c + 1) * LANES] = wide.astype(BF)
        total = acc[...]
        for n, b in enumerate(which):
            total = total + nt(acols[n], onehot[b])
        acc[...] = total

    def summed():
        both = acc[...]
        return (both[:64] + both[64:]).reshape(8, 8, LANES)

    def first(which):
        build(which)
        adjoint_obs(which, lambda b: -(feat[b, 25:26, :] * feat[b, 24:25, :]))

    acc[...] = jnp.zeros(acc.shape, F32)
    unpack(core)
    in_turn(first, core * per_core, per_core)
    arrived(in_buf.at[1 - core], OBS)
    unpack(1 - core)
    in_turn(first, (1 - core) * per_core, per_core)
    x0[j, pl.ds(HALO, 8)] = summed()

    def spread(x, s_core, s_across, s_up, s_down, f_across, f_up, f_down):
        here = x.at[j, pl.ds(HALO, 8)]
        for to in (j, across):
            send(x.at[j, pl.ds(8, 4)], x.at[j, pl.ds(0, 4)], s_up, south, to)
            send(x.at[j, pl.ds(4, 4)], x.at[j, pl.ds(12, 4)], s_down, north, to)
        send(here, here, s_across, t, across)
        send(here, here, s_core, t, sibling)
        got = x.at[across, pl.ds(HALO, 8)]
        arrived(got, s_across)
        send(got, got, f_across, t, sibling)
        for key, forward, first_row in ((s_up, f_up, 0), (s_down, f_down, 12)):
            rows = pl.ds(first_row, 4)
            arrived(x.at[pl.ds(0, 2), rows], key)
            for half in range(2):
                edge = x.at[half * cores + core, rows]
                send(edge, edge, forward, t, sibling)
        arrived(here, s_core)
        arrived(got, f_across)
        arrived(x.at[pl.ds(0, 2), pl.ds(0, 4)], f_up)
        arrived(x.at[pl.ds(0, 2), pl.ds(12, 4)], f_down)

    spread(x0, AC0, AZ0, AU0, AD0, FZ0, FU0, FD0)
    for part in range(len(PARTS) - 1):
        part_arrived(part)

    def sweep(f, lo, hi):
        out = {}
        for r in range(lo, hi):
            here = f.get(r)
            beside = [f[n] for n in (r - 1, r + 1) if n in f]
            pair = []
            for h in range(2):
                terms = [row[h] for row in beside]
                if here is not None:
                    other = here[1 - h]
                    terms.append(other + pltpu.roll(other, (1, LANES - 1)[h], 1))
                beside_all = functools.reduce(jnp.add, terms)
                if here is None:
                    pair.append(kap[r, h] * beside_all)
                else:
                    pair.append(here[h] + kap[r, h] * (beside_all - 4.0 * here[h]))
            out[r] = pair
        return out

    def local_pass(x, control_out):
        up[...] = jnp.zeros(up.shape, F32)
        together = 4
        turns = 2 * members // together

        def group(i, carry):
            ids = []
            for g in range(together):
                lh, m = g % 2, i * (together // 2) + g // 2
                ids.append((lh, m, pl.ds(pl.multiple_of(m * levels + lh * 8, 8), 8)))
            fields = [
                {
                    r: [kap[r, h] * pert[r, h, at, :] * x[lh * 2 + h, r] for h in range(2)]
                    for r in range(16)
                }
                for lh, m, at in ids
            ]
            for k in range(4):
                fields = [sweep(f, k + 1, 15 - k) for f in fields]
            fields = [
                {r: [f[r][h] * ikap[r - HALO, h] for h in range(2)] for r in f} for f in fields
            ]
            if control_out:
                for f, (lh, m, at) in zip(fields, ids):
                    for r in range(8):
                        place_at = pl.ds(m * 128 + lh * 64 + r, 8, stride=8)
                        for h in range(2):
                            flat[h, place_at, :] = f[HALO + r][h]
            for k in range(4):
                fields = [sweep(f, 3 - k, 13 + k) for f in fields]
            for r in range(16):
                for h in range(2):
                    for half in range(2):
                        terms = [
                            pert[r, h, at, :] * f[r][h]
                            for f, (lh, m, at) in zip(fields, ids)
                            if lh == half
                        ]
                        up[half * 2 + h, r] += functools.reduce(jnp.add, terms)
            return carry

        lax.fori_loop(0, turns // 2, group, 0)
        if not control_out:
            part_arrived(len(PARTS) - 1)
        lax.fori_loop(turns // 2, turns, group, 0)

    def reduce_in_chip(source, from_core, key):
        for half in range(2):
            send(source.at[half * cores + 1 - core], from_core.at[half], key, t, sibling)

    def reduce_out(source, from_core, chip_sum, from_chip, from_north, from_south, keys):
        key, k_across, k_up, k_down = keys
        arrived(from_core, key)
        for half in range(2):
            chip_sum[half] = source[half * cores + core] + from_core[half]
        for half in range(2):
            to = half * cores + core
            send(chip_sum.at[half, pl.ds(12, 4)], from_north.at[chip], k_up, south, to)
            send(chip_sum.at[half, pl.ds(0, 4)], from_south.at[chip], k_down, north, to)
        send(chip_sum.at[1 - chip, pl.ds(HALO, 8)], from_chip, k_across, t, across)

    def reduced(chip_sum, from_chip, from_north, from_south, keys):
        key, k_across, k_up, k_down = keys
        arrived(from_chip, k_across)
        arrived(from_north, k_up)
        arrived(from_south, k_down)
        total = chip_sum[chip, pl.ds(HALO, 8)] + from_chip[...]
        edges = [from_north[0] + from_north[1], from_south[0] + from_south[1]]
        return total + jnp.concatenate(edges, axis=0)

    local_pass(x0, False)
    keys = (CR0, RZ0, RU0, RD0)
    reduce_in_chip(up, cr0, CR0)
    reduce_out(up, cr0, cs0, rz0, ru0, rd0, keys)
    state = (-STEP * scale * scale) * reduced(cs0, rz0, ru0, rd0, keys)
    state = jnp.concatenate(split2(state.reshape(64, LANES)), axis=0).astype(BF)

    def observe(which):
        for b in which:
            mixed = nn(state, onehot[b])
            mixed = mixed[:64] + mixed[64:]
            total = jnp.zeros((8, LANES), F32)
            for c in range(4):
                part = mixed[:, c * LANES : (c + 1) * LANES].reshape(8, 8, LANES)
                picked = jnp.sum(jnp.where(hits(b, c), part, 0.0), axis=0)
                total = total + feat[b, 20 + c : 21 + c, :] * picked
            y_own[b] = jnp.sum(feat[b, my_levels, :] * total, axis=0, keepdims=True)

    in_turn(observe)
    for d in range(1, groups):
        send(y_own, y_far.at[d - 1], YS, t, peer(d))
    arrived(y_far, YS)

    def misfit(b):
        y = y_own[b] + y_far[0, b] + y_far[1, b] + y_far[2, b]
        return feat[b, 25:26, :] * (y - feat[b, 24:25, :])

    acc[...] = jnp.zeros(acc.shape, F32)
    in_turn(lambda which: adjoint_obs(which, misfit))
    x1[j, pl.ds(HALO, 8)] = (-scale * STEP) * (STEP * x0[j, pl.ds(HALO, 8)] + summed())
    spread(x1, AC1, AZ1, AU1, AD1, FZ1, FU1, FD1)
    sent(cr0, CR0)
    local_pass(x1, True)

    sub = lax.broadcasted_iota(jnp.int32, (16, 8, LANES), 1)
    for lh in range(2):
        even, odd = up[lh * 2], up[lh * 2 + 1]
        vp[lh * 2] = jnp.where(sub < 4, even, pltpu.roll(odd, 4, 1))
        vp[lh * 2 + 1] = jnp.where(sub < 4, pltpu.roll(even, 4, 1), odd)

    def in_order(wide):
        hi, lo = split2(wide)
        return nn(hi.astype(BF), perm[1]) + nn(lo.astype(BF), perm[1])

    def written(m):
        return pltpu.make_async_copy(ready.at[m], control_ref.at[m], lsem.at[9 + m])

    def unmix(m):
        rows = pl.ds(m * 128, 128)
        wide = jnp.concatenate([flat[0, rows, :], flat[1, rows, :]], axis=1)
        ready[m] = in_order(wide).reshape(levels, 8, 256)
        written(m).start()

    keys = (CR1, RZ1, RU1, RD1)
    reduce_in_chip(vp, cr1, CR1)
    for m in range(members // 4):
        unmix(m)
    reduce_out(vp, cr1, cs1, rz1, ru1, rd1, keys)
    for m in range(members // 4, members):
        unmix(m)
    final = scale * reduced(cs1, rz1, ru1, rd1, keys)
    back = in_order(
        jnp.concatenate(
            [final.reshape(64, LANES), pltpu.roll(final, 4, 1).reshape(64, LANES)], axis=1
        )
    )
    for h in range(2):
        stage[h, 0:64, :] = back[:, h * LANES : (h + 1) * LANES]
        for level in range(4):
            incr_ref[level, :, h * LANES : (h + 1) * LANES] = stage[h, pl.ds(level, 8, stride=8), :]
    for m in range(members):
        written(m).wait()

    sent(in_buf.at[core, pl.ds(0, tiles - 1)], A2A)
    sent(kap_rows.at[0], KAP_U)
    sent(kap_rows.at[2], KAP_D)
    for part in range(len(PARTS)):
        part_sent(part)
    sent(in_buf.at[core], OBS)
    sent(y_far, YS)
    sent(cr1, CR1)
    for k in (AC0, AZ0, FZ0, RZ0, AC1, AZ1, FZ1, RZ1):
        sent(rz0, k)
    for k in (AU0, AD0, FU0, FD0, RU0, RD0, AU1, AD1, FU1, FD1, RU1, RD1):
        sent(ru0, k)


def on_device(tiles, groups, perturbations, classes, target, cells, interp, jac, innov, inverse):
    members, levels, rows, cols = perturbations.shape
    obs = target.shape[0]
    vm = pl.BlockSpec(memory_space=pltpu.VMEM)
    hbm = pl.BlockSpec(memory_space=pltpu.HBM)
    window = (groups, 16, 8, LANES)
    message = FEATURES * MOST // 2
    blocks = MOST * tiles // LANES
    reduction = [
        ((2, 16, 8, LANES), F32), ((2, 16, 8, LANES), F32), ((8, 8, LANES), F32),
        ((2, 4, 8, LANES), F32), ((2, 4, 8, LANES), F32),
    ]
    scratch = [
        (perturbations.shape, perturbations.dtype),
        (classes.shape, classes.dtype),
        ((1, obs), target.dtype),
        (cells.shape, cells.dtype),
        (interp.shape, interp.dtype),
        (jac.shape, jac.dtype),
        ((1, obs), innov.dtype),
        ((1, obs), inverse.dtype),
        ((2, 256, 256), BF),
        ((FEATURES, obs), F32),
        ((3, message, obs), BF),
        ((tiles, 1, message), F32),
        ((2, tiles, 1, message), F32),
        ((blocks, FEATURES, LANES), F32),
        ((blocks, LANES, 4 * LANES), BF),
        ((4, 128, 4 * LANES), BF),
        ((128, LANES), F32),
        ((16, 2, members * levels, LANES), F32),
        ((2, LANES, LANES), F32),
        ((3, 8, 256), F32),
        ((16, 2, 8, LANES), F32),
        ((8, 2, 8, LANES), F32),
        (window, F32), (window, F32), (window, F32), (window, F32),
        *reduction,
        *reduction,
        ((blocks, 1, LANES), F32),
        ((groups - 1, blocks, 1, LANES), F32),
        ((2, members * levels * rows, LANES), F32),
        ((members, levels, rows, cols), F32),
        ((2, 4, 2, members * levels // 2, LANES), F32),
    ]
    return pl.pallas_call(
        functools.partial(kernel, tiles, groups, members),
        out_shape=(
            jax.ShapeDtypeStruct((members, levels, rows, cols), F32),
            jax.ShapeDtypeStruct((levels // groups, rows, cols), F32),
        ),
        in_specs=[hbm] * 8,
        out_specs=(hbm, vm),
        scratch_shapes=[pltpu.VMEM(shape, dtype) for shape, dtype in scratch]
        + [
            pltpu.SemaphoreType.DMA((N_SEM,)),
            pltpu.SemaphoreType.DMA((N_SEM,)),
            pltpu.SemaphoreType.DMA((9 + members,)),
        ],
        compiler_params=pltpu.CompilerParams(
            collective_id=0, has_side_effects=True, vmem_limit_bytes=60 * 1024 * 1024
        ),
        name="assimilate",
    )(
        perturbations, classes, target.reshape(1, obs), cells, interp, jac,
        innov.reshape(1, obs), inverse.reshape(1, obs),
    )


def solution(mesh):
    in_specs = (
        P("mem", None, "tile", None),
        P("tile", None),
        P("tile", None),
        P(None, "tile"),
        P(None, "tile"),
        P(None, "tile"),
        P("tile"),
        P("tile"),
    )
    out_specs = (P("mem", None, "tile", None), P("mem", "tile", None))
    return jax.shard_map(
        functools.partial(on_device, mesh.shape["tile"], mesh.shape["mem"]),
        mesh=mesh, in_specs=in_specs, out_specs=out_specs, check_vma=False,
    )
```

```python
import functools
import math

import jax
import jax.numpy as jnp
from jax import lax
from jax.experimental import pallas as pl
from jax.experimental.pallas import tpu as pltpu
from jax.sharding import PartitionSpec as P

MESH = pl.DeviceIdType.MESH
BF = jnp.bfloat16
F32 = jnp.float32
DIFFUSIVITIES = (0.06, 0.1, 0.15, 0.22)
STEP = 0.5
MOST = 48
FEATURES = 32
HALO = 4
LANES = 128

(A2A, KAP_U, KAP_D, OBS, AC0, AZ0, AU0, AD0, FZ0, FU0, FD0, CR0, RZ0, RU0, RD0, YS,
 AC1, AZ1, AU1, AD1, FZ1, FU1, FD1, CR1, RZ1, RU1, RD1, PERT) = range(28)
PARTS = ((0, 32), (32, 64), (64, 128))
EARLY = 1
N_SEM = PERT + 8 * len(PARTS)


def nt(a, b):
    return lax.dot_general(a, b, (((1,), (1,)), ((), ())), preferred_element_type=F32)


def nn(a, b):
    return jnp.dot(a, b, preferred_element_type=F32)


def split2(x):
    hi = x.astype(BF).astype(F32)
    return hi, x - hi


def kernel(
    tiles, groups, members,
    pert_hbm, classes_hbm, target_hbm, cells_hbm, interp_hbm, jac_hbm, innov_hbm, inv_hbm,
    control_ref, incr_ref,
    pert_ref, classes_ref, target_ref, cells_ref, interp_ref, jac_ref, innov_ref, inv_ref,
    perm, pay, val, out_buf, in_buf, feat, onehot, acols, acc,
    pert, stage, kap_rows, kap, ikap,
    x0, x1, up, vp, cr0, cs0, rz0, ru0, rd0, cr1, cs1, rz1, ru1, rd1, y_own, y_far, flat, ready, relay,
    ssem, rsem, lsem,
):
    t = lax.axis_index("tile")
    j = lax.axis_index("mem")
    north, south = lax.rem(t + tiles - 1, tiles), lax.rem(t + 1, tiles)
    cores = 2
    chip, core = j // cores, lax.rem(j, cores)
    slots = MOST // cores
    levels = 16
    scale = 1.0 / math.sqrt(members * groups - 1)
    obs = pay.shape[1]
    early = EARLY

    sibling = j + 1 - 2 * core
    across = lax.rem(j + cores, groups)

    def peer(d):
        return lax.rem(j + d, groups)

    def band(d):
        return lax.rem(t + d, tiles)

    def send(src, dst, k, tile, mem, k_out=None):
        pltpu.make_async_remote_copy(
            src_ref=src, dst_ref=dst, send_sem=ssem.at[k if k_out is None else k_out], recv_sem=rsem.at[k],
            device_id={"tile": tile, "mem": mem}, device_id_type=MESH,
        ).start()

    def arrived(like, k):
        pltpu.make_async_copy(like, like, rsem.at[k]).wait()

    def sent(like, k):
        pltpu.make_async_copy(like, like, ssem.at[k]).wait()

    fetches = [
        pltpu.make_async_copy(source, into, lsem.at[1 + k])
        for k, (source, into) in enumerate((
            (target_hbm, target_ref), (cells_hbm, cells_ref), (interp_hbm, interp_ref),
            (jac_hbm, jac_ref), (innov_hbm, innov_ref), (inv_hbm, inv_ref),
            (pert_hbm, pert_ref), (classes_hbm, classes_ref),
        ))
    ]
    for fetch in fetches:
        fetch.start()

    barrier = pltpu.get_barrier_semaphore()

    def greet(tile, mem):
        pl.semaphore_signal(
            barrier, inc=1, device_id={"tile": tile, "mem": mem}, device_id_type=MESH
        )

    def greet_band(d, carry):
        greet(band(d), j)
        return carry

    lax.fori_loop(1, tiles, greet_band, 0, unroll=9)
    for d in range(1, groups):
        greet(t, peer(d))
    greet(north, across)
    greet(south, across)

    row_id = lax.broadcasted_iota(jnp.int32, (256, 256), 0)
    col_id = lax.broadcasted_iota(jnp.int32, (256, 256), 1)
    perm[0] = jnp.where(col_id == (row_id & 1) * 128 + (row_id >> 1), 1.0, 0.0).astype(BF)
    perm[1] = jnp.where(row_id == (col_id & 1) * 128 + (col_id >> 1), 1.0, 0.0).astype(BF)

    for fetch in fetches[:6]:
        fetch.wait()

    target = target_ref[...]
    bands = lax.broadcasted_iota(jnp.int32, (tiles, obs), 0)
    member_of = jnp.where(target == bands, 1.0, 0.0)
    member_bf = member_of.astype(BF)
    before = jnp.where(row_id < col_id, 1.0, 0.0).astype(BF)
    base = jnp.zeros((tiles, 1), F32)
    ranks = []
    for b in range(obs // 256):
        part = slice(b * 256, (b + 1) * 256)
        count = nn(member_bf[:, part], before) + base
        ranks.append(jnp.sum(member_of[:, part] * count, axis=0, keepdims=True))
        base = base + jnp.sum(member_of[:, part], axis=1, keepdims=True)
    rank = jnp.concatenate(ranks, axis=1).astype(jnp.int32) - core * slots

    pay[0:16, :] = jac_ref[...]
    pay[16:24, :] = jnp.concatenate([cells_ref[...].astype(F32), interp_ref[...]], axis=0)
    pay[24:32, :] = jnp.concatenate(
        [innov_ref[...], inv_ref[...], jnp.zeros((6, obs), F32)], axis=0
    )
    whole = pay[...]
    high = whole.astype(BF).astype(F32)
    rest = whole - high
    middle = rest.astype(BF).astype(F32)
    low = rest - middle
    for q in range(slots):
        mine = rank == q
        for k, piece in enumerate((high, middle, low)):
            val[k, q * FEATURES : (q + 1) * FEATURES, :] = jnp.where(mine, piece, 0.0).astype(BF)
    packed = nt(member_bf, val[0]) + nt(member_bf, val[1]) + nt(member_bf, val[2])
    out_buf[:, 0, :] = packed

    for fetch in fetches[6:]:
        fetch.wait()

    def arrange(m, carry):
        block = pert_ref[m].astype(F32).reshape(levels * 8, 256).astype(BF)
        moved = nn(block, perm[0])
        stage[0] = moved[:, :LANES]
        stage[1] = moved[:, LANES:]
        for r in range(8):
            for lh in range(2):
                at = pl.ds(pl.multiple_of(m * levels + lh * 8, 8), 8)
                for h in range(2):
                    pert[HALO + r, h, at, :] = stage[h, pl.ds(lh * 64 + r, 8, stride=8), :]
        return carry

    lax.fori_loop(0, members, arrange, 0)

    classes = nn(classes_ref[...].astype(F32).astype(BF), perm[0])
    kappa = jnp.zeros(classes.shape, F32)
    for position, coefficient in enumerate(DIFFUSIVITIES):
        kappa = kappa + jnp.where(classes == float(position), coefficient, 0.0)
    kap_rows[1] = kappa

    pl.semaphore_wait(barrier, tiles - 1 + groups - 1 + 2)

    along_x = lax.rem(t, 4)
    ways = (
        (8, 0, south, 3, -3, 4),
        (4, 12, north, 0, 3, -4),
    )

    def edge(first_row, lo, hi):
        return pert.at[pl.ds(first_row, 4), :, pl.ds(lo, hi - lo)]

    def shares(part):
        lo, hi = PARTS[part]
        middle = (lo + hi) // 2
        return (lo, middle), (middle, hi)

    def key_of(way, part):
        return PERT + (way * len(PARTS) + part) * 4

    def waiting(way, part):
        lo, hi = shares(part)[1]
        return relay.at[way, :, :, pl.ds(PARTS[part][0] // 2, hi - lo)]

    def send_part(part, to_relay):
        one, two = shares(part)
        for way, (here, there, to, wraps, hop, onward) in enumerate(ways):
            key = key_of(way, part)
            if to_relay:

                @pl.when(along_x == wraps)
                def _():
                    send(edge(here, *two), waiting(way, part), key + 2, band(hop + tiles), j)

            else:
                send(edge(here, *one), edge(there, *one), key, to, j)

                @pl.when(along_x != wraps)
                def _():
                    send(edge(here, *two), edge(there, *two), key + 1, to, j)

    def forward_part(part):
        two = shares(part)[1]
        for way, (here, there, to, wraps, hop, onward) in enumerate(ways):
            key = key_of(way, part)

            @pl.when(along_x == 3 - wraps)
            def _():
                arrived(waiting(way, part), key + 2)
                send(
                    waiting(way, part), edge(there, *two), key + 1, band(onward + tiles), j, key + 3
                )

    def part_arrived(part):
        one, two = shares(part)
        for way, (here, there, to, wraps, hop, onward) in enumerate(ways):
            arrived(edge(there, *one), key_of(way, part))
            arrived(edge(there, *two), key_of(way, part) + 1)

    def part_sent(part):
        one, two = shares(part)
        for way, (here, there, to, wraps, hop, onward) in enumerate(ways):
            key = key_of(way, part)
            sent(edge(here, *one), key)

            @pl.when(along_x == wraps)
            def _():
                sent(edge(here, *two), key + 2)

            @pl.when(along_x != wraps)
            def _():
                sent(edge(here, *two), key + 1)

            @pl.when(along_x == 3 - wraps)
            def _():
                sent(waiting(way, part), key + 3)

    send(kap_rows.at[1], kap_rows.at[0], KAP_U, south, j)
    send(kap_rows.at[1], kap_rows.at[2], KAP_D, north, j)
    for part in range(len(PARTS)):
        send_part(part, True)
    for part in range(early):
        send_part(part, False)

    def send_band(d, carry):
        send(out_buf.at[band(d)], in_buf.at[core, t], A2A, band(d), j)
        return carry

    lax.fori_loop(1, tiles, send_band, 0, unroll=9)
    for part in range(len(PARTS)):
        forward_part(part)
        if part >= early:
            send_part(part, False)
    own = pltpu.make_async_copy(out_buf.at[t], in_buf.at[core, t], lsem.at[0])
    own.start()
    arrived(kap_rows.at[0], KAP_U)
    arrived(kap_rows.at[2], KAP_D)
    for r in range(16):
        block, row = divmod(r + 4, 8)
        line = kap_rows[block, row : row + 1, :]
        if r < 4:
            line = jnp.where(t == 0, 0.0, line)
        if r >= 12:
            line = jnp.where(t == tiles - 1, 0.0, line)
        for h in range(2):
            wide = jnp.broadcast_to(line[:, h * LANES : (h + 1) * LANES], (8, LANES))
            kap[r, h] = wide
            if 4 <= r < 12:
                ikap[r - 4, h] = 1.0 / wide

    own.wait()
    arrived(in_buf.at[core, pl.ds(0, tiles - 1)], A2A)
    send(in_buf.at[core], in_buf.at[core], OBS, t, sibling)

    blocks = MOST * tiles // LANES
    per_core = blocks // cores

    def unpack(source):
        for g in range(0, slots * FEATURES // LANES, 2):
            both = jnp.concatenate(
                [in_buf[source, :, 0, n * LANES : (n + 1) * LANES] for n in (g, g + 1)], axis=0
            ).T
            for b in range(LANES // FEATURES):
                at = source * per_core + g * 2 + b
                feat[at] = both[b * FEATURES : (b + 1) * FEATURES, :]

    along = 12

    def in_turn(step, start=0, count=blocks):
        def several(i, carry):
            step([start + i * along + n for n in range(along)])
            return carry

        lax.fori_loop(0, count // along, several, 0)

    my_levels = pl.ds(pl.multiple_of(chip * 8, 8), 8)

    def hits(b, c):
        cell = feat[b, 16 + c : 17 + c, :].astype(jnp.int32)
        row = jnp.where((cell & 1) == core, cell >> 8, -1)
        rows = lax.broadcasted_iota(jnp.int32, (8, 8, LANES), 0)
        return rows == row.reshape(1, 1, LANES)

    def build(which):
        spots = lax.broadcasted_iota(jnp.int32, (LANES, LANES), 0).astype(F32).astype(BF)
        one, none = jnp.ones((), BF), jnp.zeros((), BF)
        for b in which:
            low = (feat[b, 16:24, :].astype(jnp.int32) & 255) >> 1
            low = low.astype(F32).astype(BF)
            for c in range(4):
                spot = spots == low[c : c + 1, :]
                onehot[b, :, c * LANES : (c + 1) * LANES] = jnp.where(spot, one, none)

    def adjoint_obs(which, residual):
        for n, b in enumerate(which):
            z = residual(b)
            jac = feat[b, my_levels, :]
            for c in range(4):
                value = jac * (feat[b, 20 + c : 21 + c, :] * z)
                mask = hits(b, c)
                for k, piece in enumerate(split2(value)):
                    wide = jnp.where(mask, piece.reshape(1, 8, LANES), 0.0).reshape(64, LANES)
                    acols[n, k * 64 : (k + 1) * 64, c * LANES : (c + 1) * LANES] = wide.astype(BF)
        total = acc[...]
        for n, b in enumerate(which):
            total = total + nt(acols[n], onehot[b])
        acc[...] = total

    def summed():
        both = acc[...]
        return (both[:64] + both[64:]).reshape(8, 8, LANES)

    def first(which):
        build(which)
        adjoint_obs(which, lambda b: -(feat[b, 25:26, :] * feat[b, 24:25, :]))

    acc[...] = jnp.zeros(acc.shape, F32)
    unpack(core)
    in_turn(first, core * per_core, per_core)
    arrived(in_buf.at[1 - core], OBS)
    unpack(1 - core)
    in_turn(first, (1 - core) * per_core, per_core)
    x0[j, pl.ds(HALO, 8)] = summed()

    def spread(x, s_core, s_across, s_up, s_down, f_across, f_up, f_down):
        here = x.at[j, pl.ds(HALO, 8)]
        for to in (j, across):
            send(x.at[j, pl.ds(8, 4)], x.at[j, pl.ds(0, 4)], s_up, south, to)
            send(x.at[j, pl.ds(4, 4)], x.at[j, pl.ds(12, 4)], s_down, north, to)
        send(here, here, s_across, t, across)
        send(here, here, s_core, t, sibling)
        got = x.at[across, pl.ds(HALO, 8)]
        arrived(got, s_across)
        send(got, got, f_across, t, sibling)
        for key, forward, first_row in ((s_up, f_up, 0), (s_down, f_down, 12)):
            rows = pl.ds(first_row, 4)
            arrived(x.at[pl.ds(0, 2), rows], key)
            for half in range(2):
                edge = x.at[half * cores + core, rows]
                send(edge, edge, forward, t, sibling)
        arrived(here, s_core)
        arrived(got, f_across)
        arrived(x.at[pl.ds(0, 2), pl.ds(0, 4)], f_up)
        arrived(x.at[pl.ds(0, 2), pl.ds(12, 4)], f_down)

    spread(x0, AC0, AZ0, AU0, AD0, FZ0, FU0, FD0)
    for part in range(len(PARTS) - 1):
        part_arrived(part)

    def sweep(f, lo, hi):
        out = {}
        for r in range(lo, hi):
            here = f.get(r)
            beside = [f[n] for n in (r - 1, r + 1) if n in f]
            pair = []
            for h in range(2):
                terms = [row[h] for row in beside]
                if here is not None:
                    other = here[1 - h]
                    terms.append(other + pltpu.roll(other, (1, LANES - 1)[h], 1))
                beside_all = functools.reduce(jnp.add, terms)
                if here is None:
                    pair.append(kap[r, h] * beside_all)
                else:
                    pair.append(here[h] + kap[r, h] * (beside_all - 4.0 * here[h]))
            out[r] = pair
        return out

    def local_pass(x, control_out):
        up[...] = jnp.zeros(up.shape, F32)
        together = 4
        turns = 2 * members // together

        def group(i, carry):
            ids = []
            for g in range(together):
                lh, m = g % 2, i * (together // 2) + g // 2
                ids.append((lh, m, pl.ds(pl.multiple_of(m * levels + lh * 8, 8), 8)))
            fields = [
                {
                    r: [kap[r, h] * pert[r, h, at, :] * x[lh * 2 + h, r] for h in range(2)]
                    for r in range(16)
                }
                for lh, m, at in ids
            ]
            for k in range(4):
                fields = [sweep(f, k + 1, 15 - k) for f in fields]
            fields = [
                {r: [f[r][h] * ikap[r - HALO, h] for h in range(2)] for r in f} for f in fields
            ]
            if control_out:
                for f, (lh, m, at) in zip(fields, ids):
                    for r in range(8):
                        place_at = pl.ds(m * 128 + lh * 64 + r, 8, stride=8)
                        for h in range(2):
                            flat[h, place_at, :] = f[HALO + r][h]
            for k in range(4):
                fields = [sweep(f, 3 - k, 13 + k) for f in fields]
            for r in range(16):
                for h in range(2):
                    for half in range(2):
                        terms = [
                            pert[r, h, at, :] * f[r][h]
                            for f, (lh, m, at) in zip(fields, ids)
                            if lh == half
                        ]
                        up[half * 2 + h, r] += functools.reduce(jnp.add, terms)
            return carry

        lax.fori_loop(0, turns // 2, group, 0)
        if not control_out:
            part_arrived(len(PARTS) - 1)
        lax.fori_loop(turns // 2, turns, group, 0)

    def reduce_in_chip(source, from_core, key):
        for half in range(2):
            send(source.at[half * cores + 1 - core], from_core.at[half], key, t, sibling)

    def reduce_out(source, from_core, chip_sum, from_chip, from_north, from_south, keys):
        key, k_across, k_up, k_down = keys
        arrived(from_core, key)
        for half in range(2):
            chip_sum[half] = source[half * cores + core] + from_core[half]
        for half in range(2):
            to = half * cores + core
            send(chip_sum.at[half, pl.ds(12, 4)], from_north.at[chip], k_up, south, to)
            send(chip_sum.at[half, pl.ds(0, 4)], from_south.at[chip], k_down, north, to)
        send(chip_sum.at[1 - chip, pl.ds(HALO, 8)], from_chip, k_across, t, across)

    def reduced(chip_sum, from_chip, from_north, from_south, keys):
        key, k_across, k_up, k_down = keys
        arrived(from_chip, k_across)
        arrived(from_north, k_up)
        arrived(from_south, k_down)
        total = chip_sum[chip, pl.ds(HALO, 8)] + from_chip[...]
        edges = [from_north[0] + from_north[1], from_south[0] + from_south[1]]
        return total + jnp.concatenate(edges, axis=0)

    local_pass(x0, False)
    keys = (CR0, RZ0, RU0, RD0)
    reduce_in_chip(up, cr0, CR0)
    reduce_out(up, cr0, cs0, rz0, ru0, rd0, keys)
    state = (-STEP * scale * scale) * reduced(cs0, rz0, ru0, rd0, keys)
    state = jnp.concatenate(split2(state.reshape(64, LANES)), axis=0).astype(BF)

    def observe(which):
        for b in which:
            mixed = nn(state, onehot[b])
            mixed = mixed[:64] + mixed[64:]
            total = jnp.zeros((8, LANES), F32)
            for c in range(4):
                part = mixed[:, c * LANES : (c + 1) * LANES].reshape(8, 8, LANES)
                picked = jnp.sum(jnp.where(hits(b, c), part, 0.0), axis=0)
                total = total + feat[b, 20 + c : 21 + c, :] * picked
            y_own[b] = jnp.sum(feat[b, my_levels, :] * total, axis=0, keepdims=True)

    in_turn(observe)
    for d in range(1, groups):
        send(y_own, y_far.at[d - 1], YS, t, peer(d))
    arrived(y_far, YS)

    def misfit(b):
        y = y_own[b] + y_far[0, b] + y_far[1, b] + y_far[2, b]
        return feat[b, 25:26, :] * (y - feat[b, 24:25, :])

    acc[...] = jnp.zeros(acc.shape, F32)
    in_turn(lambda which: adjoint_obs(which, misfit))
    x1[j, pl.ds(HALO, 8)] = (-scale * STEP) * (STEP * x0[j, pl.ds(HALO, 8)] + summed())
    spread(x1, AC1, AZ1, AU1, AD1, FZ1, FU1, FD1)
    sent(cr0, CR0)
    local_pass(x1, True)

    sub = lax.broadcasted_iota(jnp.int32, (16, 8, LANES), 1)
    for lh in range(2):
        even, odd = up[lh * 2], up[lh * 2 + 1]
        vp[lh * 2] = jnp.where(sub < 4, even, pltpu.roll(odd, 4, 1))
        vp[lh * 2 + 1] = jnp.where(sub < 4, pltpu.roll(even, 4, 1), odd)

    def in_order(wide):
        hi, lo = split2(wide)
        return nn(hi.astype(BF), perm[1]) + nn(lo.astype(BF), perm[1])

    def written(m):
        return pltpu.make_async_copy(ready.at[m], control_ref.at[m], lsem.at[9 + m])

    def unmix(m):
        rows = pl.ds(m * 128, 128)
        wide = jnp.concatenate([flat[0, rows, :], flat[1, rows, :]], axis=1)
        ready[m] = in_order(wide).reshape(levels, 8, 256)
        written(m).start()

    keys = (CR1, RZ1, RU1, RD1)
    reduce_in_chip(vp, cr1, CR1)
    for m in range(members // 4):
        unmix(m)
    reduce_out(vp, cr1, cs1, rz1, ru1, rd1, keys)
    for m in range(members // 4, members):
        unmix(m)
    final = scale * reduced(cs1, rz1, ru1, rd1, keys)
    back = in_order(
        jnp.concatenate(
            [final.reshape(64, LANES), pltpu.roll(final, 4, 1).reshape(64, LANES)], axis=1
        )
    )
    for h in range(2):
        stage[h, 0:64, :] = back[:, h * LANES : (h + 1) * LANES]
        for level in range(4):
            incr_ref[level, :, h * LANES : (h + 1) * LANES] = stage[h, pl.ds(level, 8, stride=8), :]
    for m in range(members):
        written(m).wait()

    sent(in_buf.at[core, pl.ds(0, tiles - 1)], A2A)
    sent(kap_rows.at[0], KAP_U)
    sent(kap_rows.at[2], KAP_D)
    for part in range(len(PARTS)):
        part_sent(part)
    sent(in_buf.at[core], OBS)
    sent(y_far, YS)
    sent(cr1, CR1)
    for k in (AC0, AZ0, FZ0, RZ0, AC1, AZ1, FZ1, RZ1):
        sent(rz0, k)
    for k in (AU0, AD0, FU0, FD0, RU0, RD0, AU1, AD1, FU1, FD1, RU1, RD1):
        sent(ru0, k)


def on_device(tiles, groups, perturbations, classes, target, cells, interp, jac, innov, inverse):
    members, levels, rows, cols = perturbations.shape
    obs = target.shape[0]
    vm = pl.BlockSpec(memory_space=pltpu.VMEM)
    hbm = pl.BlockSpec(memory_space=pltpu.HBM)
    window = (groups, 16, 8, LANES)
    message = FEATURES * MOST // 2
    blocks = MOST * tiles // LANES
    reduction = [
        ((2, 16, 8, LANES), F32), ((2, 16, 8, LANES), F32), ((8, 8, LANES), F32),
        ((2, 4, 8, LANES), F32), ((2, 4, 8, LANES), F32),
    ]
    scratch = [
        (perturbations.shape, perturbations.dtype),
        (classes.shape, classes.dtype),
        ((1, obs), target.dtype),
        (cells.shape, cells.dtype),
        (interp.shape, interp.dtype),
        (jac.shape, jac.dtype),
        ((1, obs), innov.dtype),
        ((1, obs), inverse.dtype),
        ((2, 256, 256), BF),
        ((FEATURES, obs), F32),
        ((3, message, obs), BF),
        ((tiles, 1, message), F32),
        ((2, tiles, 1, message), F32),
        ((blocks, FEATURES, LANES), F32),
        ((blocks, LANES, 4 * LANES), BF),
        ((12, 128, 4 * LANES), BF),
        ((128, LANES), F32),
        ((16, 2, members * levels, LANES), F32),
        ((2, LANES, LANES), F32),
        ((3, 8, 256), F32),
        ((16, 2, 8, LANES), F32),
        ((8, 2, 8, LANES), F32),
        (window, F32), (window, F32), (window, F32), (window, F32),
        *reduction,
        *reduction,
        ((blocks, 1, LANES), F32),
        ((groups - 1, blocks, 1, LANES), F32),
        ((2, members * levels * rows, LANES), F32),
        ((members, levels, rows, cols), F32),
        ((2, 4, 2, members * levels // 2, LANES), F32),
    ]
    return pl.pallas_call(
        functools.partial(kernel, tiles, groups, members),
        out_shape=(
            jax.ShapeDtypeStruct((members, levels, rows, cols), F32),
            jax.ShapeDtypeStruct((levels // groups, rows, cols), F32),
        ),
        in_specs=[hbm] * 8,
        out_specs=(hbm, vm),
        scratch_shapes=[pltpu.VMEM(shape, dtype) for shape, dtype in scratch]
        + [
            pltpu.SemaphoreType.DMA((N_SEM,)),
            pltpu.SemaphoreType.DMA((N_SEM,)),
            pltpu.SemaphoreType.DMA((9 + members,)),
        ],
        compiler_params=pltpu.CompilerParams(
            collective_id=0, has_side_effects=True, vmem_limit_bytes=60 * 1024 * 1024
        ),
        name="assimilate",
    )(
        perturbations, classes, target.reshape(1, obs), cells, interp, jac,
        innov.reshape(1, obs), inverse.reshape(1, obs),
    )


def solution(mesh):
    in_specs = (
        P("mem", None, "tile", None),
        P("tile", None),
        P("tile", None),
        P(None, "tile"),
        P(None, "tile"),
        P(None, "tile"),
        P("tile"),
        P("tile"),
    )
    out_specs = (P("mem", None, "tile", None), P("mem", "tile", None))
    return jax.shard_map(
        functools.partial(on_device, mesh.shape["tile"], mesh.shape["mem"]),
        mesh=mesh, in_specs=in_specs, out_specs=out_specs, check_vma=False,
    )
```

```python
import functools
import math

import jax
import jax.numpy as jnp
from jax import lax
from jax.experimental import pallas as pl
from jax.experimental.pallas import tpu as pltpu
from jax.sharding import PartitionSpec as P

MESH = pl.DeviceIdType.MESH
BF = jnp.bfloat16
F32 = jnp.float32
DIFFUSIVITIES = (0.06, 0.1, 0.15, 0.22)
STEP = 0.5
MOST = 48
FEATURES = 32
HALO = 4
LANES = 128

(A2A, KAP_U, KAP_D, OBS, AC0, AZ0, AU0, AD0, FZ0, FU0, FD0, CR0, RZ0, RU0, RD0, YS,
 AC1, AZ1, AU1, AD1, FZ1, FU1, FD1, CR1, RZ1, RU1, RD1, PERT) = range(28)
PARTS = ((0, 32), (32, 64), (64, 128))
EARLY = 1
N_SEM = PERT + 8 * len(PARTS)


def nt(a, b):
    return lax.dot_general(a, b, (((1,), (1,)), ((), ())), preferred_element_type=F32)


def nn(a, b):
    return jnp.dot(a, b, preferred_element_type=F32)


def split2(x):
    hi = x.astype(BF).astype(F32)
    return hi, x - hi


def kernel(
    tiles, groups, members,
    pert_hbm, classes_hbm, target_hbm, cells_hbm, interp_hbm, jac_hbm, innov_hbm, inv_hbm,
    control_ref, incr_ref,
    pert_ref, classes_ref, target_ref, cells_ref, interp_ref, jac_ref, innov_ref, inv_ref,
    perm, pay, val, out_buf, in_buf, feat, onehot, acols, acc,
    pert, stage, kap_rows, kap, ikap,
    x0, x1, up, vp, cr0, cs0, rz0, ru0, rd0, cr1, cs1, rz1, ru1, rd1, y_own, y_far, flat, ready, relay,
    ssem, rsem, lsem,
):
    t = lax.axis_index("tile")
    j = lax.axis_index("mem")
    north, south = lax.rem(t + tiles - 1, tiles), lax.rem(t + 1, tiles)
    cores = 2
    chip, core = j // cores, lax.rem(j, cores)
    parity, pair = lax.rem(t, 2), t // 2
    pairs = tiles // 2
    along_x = lax.rem(t, 4)
    levels = 16
    scale = 1.0 / math.sqrt(members * groups - 1)
    obs = pay.shape[1]
    early = EARLY

    sibling = j + 1 - 2 * core
    across = lax.rem(j + cores, groups)

    def peer(d):
        return lax.rem(j + d, groups)

    def band(d):
        return lax.rem(t + d, tiles)

    def send(src, dst, k, tile, mem, k_out=None):
        pltpu.make_async_remote_copy(
            src_ref=src, dst_ref=dst, send_sem=ssem.at[k if k_out is None else k_out], recv_sem=rsem.at[k],
            device_id={"tile": tile, "mem": mem}, device_id_type=MESH,
        ).start()

    def arrived(like, k):
        pltpu.make_async_copy(like, like, rsem.at[k]).wait()

    def sent(like, k):
        pltpu.make_async_copy(like, like, ssem.at[k]).wait()

    fetches = [
        pltpu.make_async_copy(source, into, lsem.at[1 + k])
        for k, (source, into) in enumerate((
            (target_hbm, target_ref), (cells_hbm, cells_ref), (interp_hbm, interp_ref),
            (jac_hbm, jac_ref), (innov_hbm, innov_ref), (inv_hbm, inv_ref),
            (pert_hbm, pert_ref), (classes_hbm, classes_ref),
        ))
    ]
    for fetch in fetches:
        fetch.start()

    barrier = pltpu.get_barrier_semaphore()

    def greet(tile, mem):
        pl.semaphore_signal(
            barrier, inc=1, device_id={"tile": tile, "mem": mem}, device_id_type=MESH
        )

    def partner(d):
        return 2 * lax.rem(pair + d, pairs) + core, chip * cores + parity

    def greet_partner(d, carry):
        greet(*partner(d))
        return carry

    lax.fori_loop(1, pairs, greet_partner, 0)

    @pl.when(core != parity)
    def _():
        greet(*partner(0))

    for d in range(1, groups):
        greet(t, peer(d))
    for other in (north, south):
        greet(other, j)
        greet(other, across)
    greet(band(4), j)
    greet(band(tiles - 4), j)

    @pl.when(along_x == 0)
    def _():
        greet(band(3), j)

    @pl.when(along_x == 3)
    def _():
        greet(band(tiles - 3), j)

    row_id = lax.broadcasted_iota(jnp.int32, (256, 256), 0)
    col_id = lax.broadcasted_iota(jnp.int32, (256, 256), 1)
    perm[0] = jnp.where(col_id == (row_id & 1) * 128 + (row_id >> 1), 1.0, 0.0).astype(BF)
    perm[1] = jnp.where(row_id == (col_id & 1) * 128 + (col_id >> 1), 1.0, 0.0).astype(BF)

    for fetch in fetches[:6]:
        fetch.wait()

    target = target_ref[...]
    bands = 2 * lax.broadcasted_iota(jnp.int32, (pairs, obs), 0) + core
    member_of = jnp.where(target == bands, 1.0, 0.0)
    member_bf = member_of.astype(BF)
    before = jnp.where(row_id < col_id, 1.0, 0.0).astype(BF)
    base = jnp.zeros((pairs, 1), F32)
    ranks = []
    for b in range(obs // 256):
        part = slice(b * 256, (b + 1) * 256)
        count = nn(member_bf[:, part], before) + base
        ranks.append(jnp.sum(member_of[:, part] * count, axis=0, keepdims=True))
        base = base + jnp.sum(member_of[:, part], axis=1, keepdims=True)
    rank = jnp.concatenate(ranks, axis=1).astype(jnp.int32)

    pay[0:16, :] = jac_ref[...]
    pay[16:24, :] = jnp.concatenate([cells_ref[...].astype(F32), interp_ref[...]], axis=0)
    pay[24:32, :] = jnp.concatenate(
        [innov_ref[...], inv_ref[...], jnp.zeros((6, obs), F32)], axis=0
    )
    whole = pay[...]
    high = whole.astype(BF).astype(F32)
    rest = whole - high
    middle = rest.astype(BF).astype(F32)
    low = rest - middle
    for q in range(MOST):
        mine = rank == q
        for k, piece in enumerate((high, middle, low)):
            val[k, q * FEATURES : (q + 1) * FEATURES, :] = jnp.where(mine, piece, 0.0).astype(BF)
    packed = nt(member_bf, val[0]) + nt(member_bf, val[1]) + nt(member_bf, val[2])
    out_buf[:, 0, :] = packed

    for fetch in fetches[6:]:
        fetch.wait()

    def arrange(m, carry):
        block = pert_ref[m].astype(F32).reshape(levels * 8, 256).astype(BF)
        moved = nn(block, perm[0])
        stage[0] = moved[:, :LANES]
        stage[1] = moved[:, LANES:]
        for r in range(8):
            for lh in range(2):
                at = pl.ds(pl.multiple_of(m * levels + lh * 8, 8), 8)
                for h in range(2):
                    pert[HALO + r, h, at, :] = stage[h, pl.ds(lh * 64 + r, 8, stride=8), :]
        return carry

    lax.fori_loop(0, members, arrange, 0)

    classes = nn(classes_ref[...].astype(F32).astype(BF), perm[0])
    kappa = jnp.zeros(classes.shape, F32)
    for position, coefficient in enumerate(DIFFUSIVITIES):
        kappa = kappa + jnp.where(classes == float(position), coefficient, 0.0)
    kap_rows[1] = kappa

    more = lax.rem(core + parity, 2)
    turns = 1 - along_x * (3 - along_x) // 2
    pl.semaphore_wait(barrier, pairs - 1 + groups - 1 + 6 + more + turns)

    ways = (
        (8, 0, south, 3, -3, 4),
        (4, 12, north, 0, 3, -4),
    )

    def edge(first_row, lo, hi):
        return pert.at[pl.ds(first_row, 4), :, pl.ds(lo, hi - lo)]

    def shares(part):
        lo, hi = PARTS[part]
        middle = (lo + hi) // 2
        return (lo, middle), (middle, hi)

    def key_of(way, part):
        return PERT + (way * len(PARTS) + part) * 4

    def waiting(way, part):
        lo, hi = shares(part)[1]
        return relay.at[way, :, :, pl.ds(PARTS[part][0] // 2, hi - lo)]

    def send_part(part, to_relay):
        one, two = shares(part)
        for way, (here, there, to, wraps, hop, onward) in enumerate(ways):
            key = key_of(way, part)
            if to_relay:

                @pl.when(along_x == wraps)
                def _():
                    send(edge(here, *two), waiting(way, part), key + 2, band(hop + tiles), j)

            else:
                send(edge(here, *one), edge(there, *one), key, to, j)

                @pl.when(along_x != wraps)
                def _():
                    send(edge(here, *two), edge(there, *two), key + 1, to, j)

    def forward_part(part):
        two = shares(part)[1]
        for way, (here, there, to, wraps, hop, onward) in enumerate(ways):
            key = key_of(way, part)

            @pl.when(along_x == 3 - wraps)
            def _():
                arrived(waiting(way, part), key + 2)
                send(
                    waiting(way, part), edge(there, *two), key + 1, band(onward + tiles), j, key + 3
                )

    def part_arrived(part):
        one, two = shares(part)
        for way, (here, there, to, wraps, hop, onward) in enumerate(ways):
            arrived(edge(there, *one), key_of(way, part))
            arrived(edge(there, *two), key_of(way, part) + 1)

    def part_sent(part):
        one, two = shares(part)
        for way, (here, there, to, wraps, hop, onward) in enumerate(ways):
            key = key_of(way, part)
            sent(edge(here, *one), key)

            @pl.when(along_x == wraps)
            def _():
                sent(edge(here, *two), key + 2)

            @pl.when(along_x != wraps)
            def _():
                sent(edge(here, *two), key + 1)

            @pl.when(along_x == 3 - wraps)
            def _():
                sent(waiting(way, part), key + 3)

    send(kap_rows.at[1], kap_rows.at[0], KAP_U, south, j)
    send(kap_rows.at[1], kap_rows.at[2], KAP_D, north, j)
    for part in range(len(PARTS)):
        send_part(part, True)
    for part in range(early):
        send_part(part, False)

    def send_partner(d, carry):
        tile, mem = partner(d)
        send(out_buf.at[lax.rem(pair + d, pairs)], in_buf.at[parity, pair], A2A, tile, mem)
        return carry

    lax.fori_loop(1, pairs, send_partner, 0, unroll=31)
    own = pltpu.make_async_copy(out_buf.at[pair], in_buf.at[core, pair], lsem.at[0])

    @pl.when(core != parity)
    def _():
        send_partner(0, 0)

    @pl.when(core == parity)
    def _():
        own.start()

    for part in range(len(PARTS)):
        forward_part(part)
        if part >= early:
            send_part(part, False)
    arrived(kap_rows.at[0], KAP_U)
    arrived(kap_rows.at[2], KAP_D)
    for r in range(16):
        block, row = divmod(r + 4, 8)
        line = kap_rows[block, row : row + 1, :]
        if r < 4:
            line = jnp.where(t == 0, 0.0, line)
        if r >= 12:
            line = jnp.where(t == tiles - 1, 0.0, line)
        for h in range(2):
            wide = jnp.broadcast_to(line[:, h * LANES : (h + 1) * LANES], (8, LANES))
            kap[r, h] = wide
            if 4 <= r < 12:
                ikap[r - 4, h] = 1.0 / wide

    @pl.when(core == parity)
    def _():
        own.wait()
        arrived(in_buf.at[core, pl.ds(0, pairs - 1)], A2A)

    @pl.when(core != parity)
    def _():
        arrived(in_buf.at[core], A2A)

    send(in_buf.at[core], in_buf.at[core], OBS, t, sibling)

    blocks = MOST * tiles // LANES
    per_core = blocks // cores

    def unpack(source):
        for g in range(0, MOST * FEATURES // LANES, 4):
            both = jnp.concatenate(
                [in_buf[source, :, 0, n * LANES : (n + 1) * LANES] for n in range(g, g + 4)], axis=0
            ).T
            for b in range(LANES // FEATURES):
                at = source * per_core + g + b
                feat[at] = both[b * FEATURES : (b + 1) * FEATURES, :]

    along = 12

    def in_turn(step, start=0, count=blocks):
        def several(i, carry):
            step([start + i * along + n for n in range(along)])
            return carry

        lax.fori_loop(0, count // along, several, 0)

    my_levels = pl.ds(pl.multiple_of(chip * 8, 8), 8)

    def hits(b, c):
        cell = feat[b, 16 + c : 17 + c, :].astype(jnp.int32)
        row = jnp.where((cell & 1) == core, cell >> 8, -1)
        rows = lax.broadcasted_iota(jnp.int32, (8, 8, LANES), 0)
        return rows == row.reshape(1, 1, LANES)

    def build(which):
        spots = lax.broadcasted_iota(jnp.int32, (LANES, LANES), 0).astype(F32).astype(BF)
        one, none = jnp.ones((), BF), jnp.zeros((), BF)
        for b in which:
            low = (feat[b, 16:24, :].astype(jnp.int32) & 255) >> 1
            low = low.astype(F32).astype(BF)
            for c in range(4):
                spot = spots == low[c : c + 1, :]
                onehot[b, :, c * LANES : (c + 1) * LANES] = jnp.where(spot, one, none)

    def adjoint_obs(which, residual):
        for n, b in enumerate(which):
            z = residual(b)
            jac = feat[b, my_levels, :]
            for c in range(4):
                value = jac * (feat[b, 20 + c : 21 + c, :] * z)
                mask = hits(b, c)
                for k, piece in enumerate(split2(value)):
                    wide = jnp.where(mask, piece.reshape(1, 8, LANES), 0.0).reshape(64, LANES)
                    acols[n, k * 64 : (k + 1) * 64, c * LANES : (c + 1) * LANES] = wide.astype(BF)
        total = acc[...]
        for n, b in enumerate(which):
            total = total + nt(acols[n], onehot[b])
        acc[...] = total

    def summed():
        both = acc[...]
        return (both[:64] + both[64:]).reshape(8, 8, LANES)

    def first(which):
        build(which)
        adjoint_obs(which, lambda b: -(feat[b, 25:26, :] * feat[b, 24:25, :]))

    acc[...] = jnp.zeros(acc.shape, F32)
    unpack(core)
    in_turn(first, core * per_core, per_core)
    arrived(in_buf.at[1 - core], OBS)
    unpack(1 - core)
    in_turn(first, (1 - core) * per_core, per_core)
    x0[j, pl.ds(HALO, 8)] = summed()

    def spread(x, s_core, s_across, s_up, s_down, f_across, f_up, f_down):
        here = x.at[j, pl.ds(HALO, 8)]
        for to in (j, across):
            send(x.at[j, pl.ds(8, 4)], x.at[j, pl.ds(0, 4)], s_up, south, to)
            send(x.at[j, pl.ds(4, 4)], x.at[j, pl.ds(12, 4)], s_down, north, to)
        send(here, here, s_across, t, across)
        send(here, here, s_core, t, sibling)
        got = x.at[across, pl.ds(HALO, 8)]
        arrived(got, s_across)
        send(got, got, f_across, t, sibling)
        for key, forward, first_row in ((s_up, f_up, 0), (s_down, f_down, 12)):
            rows = pl.ds(first_row, 4)
            arrived(x.at[pl.ds(0, 2), rows], key)
            for half in range(2):
                edge = x.at[half * cores + core, rows]
                send(edge, edge, forward, t, sibling)
        arrived(here, s_core)
        arrived(got, f_across)
        arrived(x.at[pl.ds(0, 2), pl.ds(0, 4)], f_up)
        arrived(x.at[pl.ds(0, 2), pl.ds(12, 4)], f_down)

    spread(x0, AC0, AZ0, AU0, AD0, FZ0, FU0, FD0)
    for part in range(len(PARTS) - 1):
        part_arrived(part)

    def sweep(f, lo, hi):
        out = {}
        for r in range(lo, hi):
            here = f.get(r)
            beside = [f[n] for n in (r - 1, r + 1) if n in f]
            pair = []
            for h in range(2):
                terms = [row[h] for row in beside]
                if here is not None:
                    other = here[1 - h]
                    terms.append(other + pltpu.roll(other, (1, LANES - 1)[h], 1))
                beside_all = functools.reduce(jnp.add, terms)
                if here is None:
                    pair.append(kap[r, h] * beside_all)
                else:
                    pair.append(here[h] + kap[r, h] * (beside_all - 4.0 * here[h]))
            out[r] = pair
        return out

    def local_pass(x, control_out):
        up[...] = jnp.zeros(up.shape, F32)
        together = 4
        turns = 2 * members // together

        def group(i, carry):
            ids = []
            for g in range(together):
                lh, m = g % 2, i * (together // 2) + g // 2
                ids.append((lh, m, pl.ds(pl.multiple_of(m * levels + lh * 8, 8), 8)))
            fields = [
                {
                    r: [kap[r, h] * pert[r, h, at, :] * x[lh * 2 + h, r] for h in range(2)]
                    for r in range(16)
                }
                for lh, m, at in ids
            ]
            for k in range(4):
                fields = [sweep(f, k + 1, 15 - k) for f in fields]
            fields = [
                {r: [f[r][h] * ikap[r - HALO, h] for h in range(2)] for r in f} for f in fields
            ]
            if control_out:
                for f, (lh, m, at) in zip(fields, ids):
                    for r in range(8):
                        place_at = pl.ds(m * 128 + lh * 64 + r, 8, stride=8)
                        for h in range(2):
                            flat[h, place_at, :] = f[HALO + r][h]
            for k in range(4):
                fields = [sweep(f, 3 - k, 13 + k) for f in fields]
            for r in range(16):
                for h in range(2):
                    for half in range(2):
                        terms = [
                            pert[r, h, at, :] * f[r][h]
                            for f, (lh, m, at) in zip(fields, ids)
                            if lh == half
                        ]
                        up[half * 2 + h, r] += functools.reduce(jnp.add, terms)
            return carry

        lax.fori_loop(0, turns // 2, group, 0)
        if not control_out:
            part_arrived(len(PARTS) - 1)
        lax.fori_loop(turns // 2, turns, group, 0)

    def reduce_in_chip(source, from_core, key):
        for half in range(2):
            send(source.at[half * cores + 1 - core], from_core.at[half], key, t, sibling)

    def reduce_out(source, from_core, chip_sum, from_chip, from_north, from_south, keys):
        key, k_across, k_up, k_down = keys
        arrived(from_core, key)
        for half in range(2):
            chip_sum[half] = source[half * cores + core] + from_core[half]
        for half in range(2):
            to = half * cores + core
            send(chip_sum.at[half, pl.ds(12, 4)], from_north.at[chip], k_up, south, to)
            send(chip_sum.at[half, pl.ds(0, 4)], from_south.at[chip], k_down, north, to)
        send(chip_sum.at[1 - chip, pl.ds(HALO, 8)], from_chip, k_across, t, across)

    def reduced(chip_sum, from_chip, from_north, from_south, keys):
        key, k_across, k_up, k_down = keys
        arrived(from_chip, k_across)
        arrived(from_north, k_up)
        arrived(from_south, k_down)
        total = chip_sum[chip, pl.ds(HALO, 8)] + from_chip[...]
        edges = [from_north[0] + from_north[1], from_south[0] + from_south[1]]
        return total + jnp.concatenate(edges, axis=0)

    local_pass(x0, False)
    keys = (CR0, RZ0, RU0, RD0)
    reduce_in_chip(up, cr0, CR0)
    reduce_out(up, cr0, cs0, rz0, ru0, rd0, keys)
    state = (-STEP * scale * scale) * reduced(cs0, rz0, ru0, rd0, keys)
    state = jnp.concatenate(split2(state.reshape(64, LANES)), axis=0).astype(BF)

    def observe(which):
        for b in which:
            mixed = nn(state, onehot[b])
            mixed = mixed[:64] + mixed[64:]
            total = jnp.zeros((8, LANES), F32)
            for c in range(4):
                part = mixed[:, c * LANES : (c + 1) * LANES].reshape(8, 8, LANES)
                picked = jnp.sum(jnp.where(hits(b, c), part, 0.0), axis=0)
                total = total + feat[b, 20 + c : 21 + c, :] * picked
            y_own[b] = jnp.sum(feat[b, my_levels, :] * total, axis=0, keepdims=True)

    in_turn(observe)
    for d in range(1, groups):
        send(y_own, y_far.at[d - 1], YS, t, peer(d))
    arrived(y_far, YS)

    def misfit(b):
        y = y_own[b] + y_far[0, b] + y_far[1, b] + y_far[2, b]
        return feat[b, 25:26, :] * (y - feat[b, 24:25, :])

    acc[...] = jnp.zeros(acc.shape, F32)
    in_turn(lambda which: adjoint_obs(which, misfit))
    x1[j, pl.ds(HALO, 8)] = (-scale * STEP) * (STEP * x0[j, pl.ds(HALO, 8)] + summed())
    spread(x1, AC1, AZ1, AU1, AD1, FZ1, FU1, FD1)
    sent(cr0, CR0)
    local_pass(x1, True)

    sub = lax.broadcasted_iota(jnp.int32, (16, 8, LANES), 1)
    for lh in range(2):
        even, odd = up[lh * 2], up[lh * 2 + 1]
        vp[lh * 2] = jnp.where(sub < 4, even, pltpu.roll(odd, 4, 1))
        vp[lh * 2 + 1] = jnp.where(sub < 4, pltpu.roll(even, 4, 1), odd)

    def in_order(wide):
        hi, lo = split2(wide)
        return nn(hi.astype(BF), perm[1]) + nn(lo.astype(BF), perm[1])

    def written(m):
        return pltpu.make_async_copy(ready.at[m], control_ref.at[m], lsem.at[9 + m])

    def unmix(m):
        rows = pl.ds(m * 128, 128)
        wide = jnp.concatenate([flat[0, rows, :], flat[1, rows, :]], axis=1)
        ready[m] = in_order(wide).reshape(levels, 8, 256)
        written(m).start()

    keys = (CR1, RZ1, RU1, RD1)
    reduce_in_chip(vp, cr1, CR1)
    for m in range(members // 4):
        unmix(m)
    reduce_out(vp, cr1, cs1, rz1, ru1, rd1, keys)
    for m in range(members // 4, members):
        unmix(m)
    final = scale * reduced(cs1, rz1, ru1, rd1, keys)
    back = in_order(
        jnp.concatenate(
            [final.reshape(64, LANES), pltpu.roll(final, 4, 1).reshape(64, LANES)], axis=1
        )
    )
    for h in range(2):
        stage[h, 0:64, :] = back[:, h * LANES : (h + 1) * LANES]
        for level in range(4):
            incr_ref[level, :, h * LANES : (h + 1) * LANES] = stage[h, pl.ds(level, 8, stride=8), :]
    for m in range(members):
        written(m).wait()

    @pl.when(core == parity)
    def _():
        sent(in_buf.at[core, pl.ds(0, pairs - 1)], A2A)

    @pl.when(core != parity)
    def _():
        sent(in_buf.at[core], A2A)

    sent(kap_rows.at[0], KAP_U)
    sent(kap_rows.at[2], KAP_D)
    for part in range(len(PARTS)):
        part_sent(part)
    sent(in_buf.at[core], OBS)
    sent(y_far, YS)
    sent(cr1, CR1)
    for k in (AC0, AZ0, FZ0, RZ0, AC1, AZ1, FZ1, RZ1):
        sent(rz0, k)
    for k in (AU0, AD0, FU0, FD0, RU0, RD0, AU1, AD1, FU1, FD1, RU1, RD1):
        sent(ru0, k)


def write_out(control_ref, incr_ref, control_out, incr_out, sems):
    count = control_ref.shape[0]
    copies = [
        pltpu.make_async_copy(control_ref.at[m], control_out.at[m], sems.at[m])
        for m in range(count)
    ]
    copies.append(pltpu.make_async_copy(incr_ref, incr_out, sems.at[count]))
    for copy in copies:
        copy.start()
    for copy in copies:
        copy.wait()


def on_device(tiles, groups, perturbations, classes, target, cells, interp, jac, innov, inverse):
    members, levels, rows, cols = perturbations.shape
    obs = target.shape[0]
    vm = pl.BlockSpec(memory_space=pltpu.VMEM)
    hbm = pl.BlockSpec(memory_space=pltpu.HBM)
    window = (groups, 16, 8, LANES)
    message = FEATURES * MOST
    blocks = MOST * tiles // LANES
    reduction = [
        ((2, 16, 8, LANES), F32), ((2, 16, 8, LANES), F32), ((8, 8, LANES), F32),
        ((2, 4, 8, LANES), F32), ((2, 4, 8, LANES), F32),
    ]
    scratch = [
        (perturbations.shape, perturbations.dtype),
        (classes.shape, classes.dtype),
        ((1, obs), target.dtype),
        (cells.shape, cells.dtype),
        (interp.shape, interp.dtype),
        (jac.shape, jac.dtype),
        ((1, obs), innov.dtype),
        ((1, obs), inverse.dtype),
        ((2, 256, 256), BF),
        ((FEATURES, obs), F32),
        ((3, message, obs), BF),
        ((tiles // 2, 1, message), F32),
        ((2, tiles // 2, 1, message), F32),
        ((blocks, FEATURES, LANES), F32),
        ((blocks, LANES, 4 * LANES), BF),
        ((12, 128, 4 * LANES), BF),
        ((128, LANES), F32),
        ((16, 2, members * levels, LANES), F32),
        ((2, LANES, LANES), F32),
        ((3, 8, 256), F32),
        ((16, 2, 8, LANES), F32),
        ((8, 2, 8, LANES), F32),
        (window, F32), (window, F32), (window, F32), (window, F32),
        *reduction,
        *reduction,
        ((blocks, 1, LANES), F32),
        ((groups - 1, blocks, 1, LANES), F32),
        ((2, members * levels * rows, LANES), F32),
        ((members, levels, rows, cols), F32),
        ((2, 4, 2, members * levels // 2, LANES), F32),
    ]
    control, increment = pl.pallas_call(
        functools.partial(kernel, tiles, groups, members),
        out_shape=(
            jax.ShapeDtypeStruct((members, levels, rows, cols), F32),
            jax.ShapeDtypeStruct((levels // groups, rows, cols), F32),
        ),
        in_specs=[hbm] * 8,
        out_specs=(hbm, vm),
        scratch_shapes=[pltpu.VMEM(shape, dtype) for shape, dtype in scratch]
        + [
            pltpu.SemaphoreType.DMA((N_SEM,)),
            pltpu.SemaphoreType.DMA((N_SEM,)),
            pltpu.SemaphoreType.DMA((9 + members,)),
        ],
        compiler_params=pltpu.CompilerParams(
            collective_id=0, has_side_effects=True, vmem_limit_bytes=60 * 1024 * 1024
        ),
        name="assimilate",
    )(
        perturbations, classes, target.reshape(1, obs), cells, interp, jac,
        innov.reshape(1, obs), inverse.reshape(1, obs),
    )
    return pl.pallas_call(
        write_out,
        out_shape=(
            jax.ShapeDtypeStruct(control.shape, F32), jax.ShapeDtypeStruct(increment.shape, F32)
        ),
        in_specs=[hbm, hbm],
        out_specs=(hbm, hbm),
        scratch_shapes=[pltpu.SemaphoreType.DMA((members + 1,))],
        compiler_params=pltpu.CompilerParams(vmem_limit_bytes=60 * 1024 * 1024),
        name="write_out",
    )(control, increment)


def solution(mesh):
    in_specs = (
        P("mem", None, "tile", None),
        P("tile", None),
        P("tile", None),
        P(None, "tile"),
        P(None, "tile"),
        P(None, "tile"),
        P("tile"),
        P("tile"),
    )
    out_specs = (P("mem", None, "tile", None), P("mem", "tile", None))
    return jax.shard_map(
        functools.partial(on_device, mesh.shape["tile"], mesh.shape["mem"]),
        mesh=mesh, in_specs=in_specs, out_specs=out_specs, check_vma=False,
    )
```

```python
import functools
import math

import jax
import jax.numpy as jnp
from jax import lax
from jax.experimental import pallas as pl
from jax.experimental.pallas import tpu as pltpu
from jax.sharding import PartitionSpec as P

MESH = pl.DeviceIdType.MESH
BF = jnp.bfloat16
F32 = jnp.float32
DIFFUSIVITIES = (0.06, 0.1, 0.15, 0.22)
STEP = 0.5
MOST = 48
FEATURES = 32
HALO = 4
LANES = 128

(A2A, KAP_U, KAP_D, OBS, AC0, AZ0, AU0, AD0, FZ0, FU0, FD0, CR0, RZ0, RU0, RD0, YS,
 AC1, AZ1, AU1, AD1, FZ1, FU1, FD1, CR1, RZ1, RU1, RD1, PERT) = range(28)
PARTS = ((0, 32), (32, 64), (64, 128))
EARLY = 1
N_SEM = PERT + 8 * len(PARTS)


def nt(a, b):
    return lax.dot_general(a, b, (((1,), (1,)), ((), ())), preferred_element_type=F32)


def nn(a, b):
    return jnp.dot(a, b, preferred_element_type=F32)


def split2(x):
    hi = x.astype(BF).astype(F32)
    return hi, x - hi


def kernel(
    tiles, groups, members,
    pert_hbm, classes_hbm, target_hbm, cells_hbm, interp_hbm, jac_hbm, innov_hbm, inv_hbm,
    control_ref, incr_ref,
    pert_ref, classes_ref, target_ref, cells_ref, interp_ref, jac_ref, innov_ref, inv_ref,
    perm, pay, val, out_buf, in_buf, feat, onehot, acols, acc,
    pert, stage, kap_rows, kap, ikap,
    x0, x1, up, vp, cr0, cs0, rz0, ru0, rd0, cr1, cs1, rz1, ru1, rd1, y_own, y_far, flat, ready, relay,
    ssem, rsem, lsem,
):
    t = lax.axis_index("tile")
    j = lax.axis_index("mem")
    north, south = lax.rem(t + tiles - 1, tiles), lax.rem(t + 1, tiles)
    cores = 2
    chip, core = j // cores, lax.rem(j, cores)
    slots = MOST // cores
    levels = 16
    scale = 1.0 / math.sqrt(members * groups - 1)
    obs = pay.shape[1]
    early = EARLY

    sibling = j + 1 - 2 * core
    across = lax.rem(j + cores, groups)

    def peer(d):
        return lax.rem(j + d, groups)

    def band(d):
        return lax.rem(t + d, tiles)

    def send(src, dst, k, tile, mem, k_out=None):
        pltpu.make_async_remote_copy(
            src_ref=src, dst_ref=dst, send_sem=ssem.at[k if k_out is None else k_out], recv_sem=rsem.at[k],
            device_id={"tile": tile, "mem": mem}, device_id_type=MESH,
        ).start()

    def arrived(like, k):
        pltpu.make_async_copy(like, like, rsem.at[k]).wait()

    def sent(like, k):
        pltpu.make_async_copy(like, like, ssem.at[k]).wait()

    fetches = [
        pltpu.make_async_copy(source, into, lsem.at[1 + k])
        for k, (source, into) in enumerate((
            (pert_hbm, pert_ref), (classes_hbm, classes_ref),
            (target_hbm, target_ref), (cells_hbm, cells_ref), (interp_hbm, interp_ref),
            (jac_hbm, jac_ref), (innov_hbm, innov_ref), (inv_hbm, inv_ref),
        ))
    ]
    for fetch in fetches:
        fetch.start()

    barrier = pltpu.get_barrier_semaphore()

    def greet(tile, mem):
        pl.semaphore_signal(
            barrier, inc=1, device_id={"tile": tile, "mem": mem}, device_id_type=MESH
        )

    def greet_band(d, carry):
        greet(band(d), j)
        return carry

    lax.fori_loop(1, tiles, greet_band, 0, unroll=9)
    for d in range(1, groups):
        greet(t, peer(d))
    greet(north, across)
    greet(south, across)

    row_id = lax.broadcasted_iota(jnp.int32, (256, 256), 0)
    col_id = lax.broadcasted_iota(jnp.int32, (256, 256), 1)
    perm[0] = jnp.where(col_id == (row_id & 1) * 128 + (row_id >> 1), 1.0, 0.0).astype(BF)
    perm[1] = jnp.where(row_id == (col_id & 1) * 128 + (col_id >> 1), 1.0, 0.0).astype(BF)

    for fetch in fetches[:2]:
        fetch.wait()

    def arrange(m, carry):
        block = pert_ref[m].astype(F32).reshape(levels * 8, 256).astype(BF)
        moved = nn(block, perm[0])
        stage[0] = moved[:, :LANES]
        stage[1] = moved[:, LANES:]
        for r in range(8):
            for lh in range(2):
                at = pl.ds(pl.multiple_of(m * levels + lh * 8, 8), 8)
                for h in range(2):
                    pert[HALO + r, h, at, :] = stage[h, pl.ds(lh * 64 + r, 8, stride=8), :]
        return carry

    lax.fori_loop(0, members, arrange, 0)

    classes = nn(classes_ref[...].astype(F32).astype(BF), perm[0])
    kappa = jnp.zeros(classes.shape, F32)
    for position, coefficient in enumerate(DIFFUSIVITIES):
        kappa = kappa + jnp.where(classes == float(position), coefficient, 0.0)
    kap_rows[1] = kappa

    pl.semaphore_wait(barrier, tiles - 1 + groups - 1 + 2)

    along_x = lax.rem(t, 4)
    ways = (
        (8, 0, south, 3, -3, 4),
        (4, 12, north, 0, 3, -4),
    )

    def edge(first_row, lo, hi):
        return pert.at[pl.ds(first_row, 4), :, pl.ds(lo, hi - lo)]

    def shares(part):
        lo, hi = PARTS[part]
        middle = (lo + hi) // 2
        return (lo, middle), (middle, hi)

    def key_of(way, part):
        return PERT + (way * len(PARTS) + part) * 4

    def waiting(way, part):
        lo, hi = shares(part)[1]
        return relay.at[way, :, :, pl.ds(PARTS[part][0] // 2, hi - lo)]

    def send_part(part, to_relay):
        one, two = shares(part)
        for way, (here, there, to, wraps, hop, onward) in enumerate(ways):
            key = key_of(way, part)
            if to_relay:

                @pl.when(along_x == wraps)
                def _():
                    send(edge(here, *two), waiting(way, part), key + 2, band(hop + tiles), j)

            else:
                send(edge(here, *one), edge(there, *one), key, to, j)

                @pl.when(along_x != wraps)
                def _():
                    send(edge(here, *two), edge(there, *two), key + 1, to, j)

    def forward_part(part):
        two = shares(part)[1]
        for way, (here, there, to, wraps, hop, onward) in enumerate(ways):
            key = key_of(way, part)

            @pl.when(along_x == 3 - wraps)
            def _():
                arrived(waiting(way, part), key + 2)
                send(
                    waiting(way, part), edge(there, *two), key + 1, band(onward + tiles), j, key + 3
                )

    def part_arrived(part):
        one, two = shares(part)
        for way, (here, there, to, wraps, hop, onward) in enumerate(ways):
            arrived(edge(there, *one), key_of(way, part))
            arrived(edge(there, *two), key_of(way, part) + 1)

    def part_sent(part):
        one, two = shares(part)
        for way, (here, there, to, wraps, hop, onward) in enumerate(ways):
            key = key_of(way, part)
            sent(edge(here, *one), key)

            @pl.when(along_x == wraps)
            def _():
                sent(edge(here, *two), key + 2)

            @pl.when(along_x != wraps)
            def _():
                sent(edge(here, *two), key + 1)

            @pl.when(along_x == 3 - wraps)
            def _():
                sent(waiting(way, part), key + 3)

    send(kap_rows.at[1], kap_rows.at[0], KAP_U, south, j)
    send(kap_rows.at[1], kap_rows.at[2], KAP_D, north, j)
    for part in range(len(PARTS)):
        send_part(part, True)
    for part in range(early):
        send_part(part, False)

    for fetch in fetches[2:]:
        fetch.wait()

    target = target_ref[...]
    bands = lax.broadcasted_iota(jnp.int32, (tiles, obs), 0)
    member_of = jnp.where(target == bands, 1.0, 0.0)
    member_bf = member_of.astype(BF)
    before = jnp.where(row_id < col_id, 1.0, 0.0).astype(BF)
    base = jnp.zeros((tiles, 1), F32)
    ranks = []
    for b in range(obs // 256):
        part = slice(b * 256, (b + 1) * 256)
        count = nn(member_bf[:, part], before) + base
        ranks.append(jnp.sum(member_of[:, part] * count, axis=0, keepdims=True))
        base = base + jnp.sum(member_of[:, part], axis=1, keepdims=True)
    rank = jnp.concatenate(ranks, axis=1).astype(jnp.int32) - core * slots

    pay[0:16, :] = jac_ref[...]
    pay[16:24, :] = jnp.concatenate([cells_ref[...].astype(F32), interp_ref[...]], axis=0)
    pay[24:32, :] = jnp.concatenate(
        [innov_ref[...], inv_ref[...], jnp.zeros((6, obs), F32)], axis=0
    )
    whole = pay[...]
    high = whole.astype(BF).astype(F32)
    rest = whole - high
    middle = rest.astype(BF).astype(F32)
    low = rest - middle
    for q in range(slots):
        mine = rank == q
        for k, piece in enumerate((high, middle, low)):
            val[k, q * FEATURES : (q + 1) * FEATURES, :] = jnp.where(mine, piece, 0.0).astype(BF)
    packed = nt(member_bf, val[0]) + nt(member_bf, val[1]) + nt(member_bf, val[2])
    out_buf[:, 0, :] = packed

    def send_band(d, carry):
        send(out_buf.at[band(d)], in_buf.at[core, t], A2A, band(d), j)
        return carry

    lax.fori_loop(1, tiles, send_band, 0, unroll=9)
    for part in range(len(PARTS)):
        forward_part(part)
        if part >= early:
            send_part(part, False)
    own = pltpu.make_async_copy(out_buf.at[t], in_buf.at[core, t], lsem.at[0])
    own.start()
    arrived(kap_rows.at[0], KAP_U)
    arrived(kap_rows.at[2], KAP_D)
    for r in range(16):
        block, row = divmod(r + 4, 8)
        line = kap_rows[block, row : row + 1, :]
        if r < 4:
            line = jnp.where(t == 0, 0.0, line)
        if r >= 12:
            line = jnp.where(t == tiles - 1, 0.0, line)
        for h in range(2):
            wide = jnp.broadcast_to(line[:, h * LANES : (h + 1) * LANES], (8, LANES))
            kap[r, h] = wide
            if 4 <= r < 12:
                ikap[r - 4, h] = 1.0 / wide

    own.wait()
    arrived(in_buf.at[core, pl.ds(0, tiles - 1)], A2A)
    send(in_buf.at[core], in_buf.at[core], OBS, t, sibling)

    blocks = MOST * tiles // LANES
    per_core = blocks // cores

    def unpack(source):
        for g in range(0, slots * FEATURES // LANES, 2):
            both = jnp.concatenate(
                [in_buf[source, :, 0, n * LANES : (n + 1) * LANES] for n in (g, g + 1)], axis=0
            ).T
            for b in range(LANES // FEATURES):
                at = source * per_core + g * 2 + b
                feat[at] = both[b * FEATURES : (b + 1) * FEATURES, :]

    along = 12

    def in_turn(step, start=0, count=blocks):
        def several(i, carry):
            step([start + i * along + n for n in range(along)])
            return carry

        lax.fori_loop(0, count // along, several, 0)

    my_levels = pl.ds(pl.multiple_of(chip * 8, 8), 8)

    def hits(b, c):
        cell = feat[b, 16 + c : 17 + c, :].astype(jnp.int32)
        row = jnp.where((cell & 1) == core, cell >> 8, -1)
        rows = lax.broadcasted_iota(jnp.int32, (8, 8, LANES), 0)
        return rows == row.reshape(1, 1, LANES)

    def build(which):
        spots = lax.broadcasted_iota(jnp.int32, (LANES, LANES), 0).astype(F32).astype(BF)
        one, none = jnp.ones((), BF), jnp.zeros((), BF)
        for b in which:
            low = (feat[b, 16:24, :].astype(jnp.int32) & 255) >> 1
            low = low.astype(F32).astype(BF)
            for c in range(4):
                spot = spots == low[c : c + 1, :]
                onehot[b, :, c * LANES : (c + 1) * LANES] = jnp.where(spot, one, none)

    def adjoint_obs(which, residual):
        for n, b in enumerate(which):
            z = residual(b)
            jac = feat[b, my_levels, :]
            for c in range(4):
                value = jac * (feat[b, 20 + c : 21 + c, :] * z)
                mask = hits(b, c)
                for k, piece in enumerate(split2(value)):
                    wide = jnp.where(mask, piece.reshape(1, 8, LANES), 0.0).reshape(64, LANES)
                    acols[n, k * 64 : (k + 1) * 64, c * LANES : (c + 1) * LANES] = wide.astype(BF)
        total = acc[...]
        for n, b in enumerate(which):
            total = total + nt(acols[n], onehot[b])
        acc[...] = total

    def summed():
        both = acc[...]
        return (both[:64] + both[64:]).reshape(8, 8, LANES)

    def first(which):
        build(which)
        adjoint_obs(which, lambda b: -(feat[b, 25:26, :] * feat[b, 24:25, :]))

    acc[...] = jnp.zeros(acc.shape, F32)
    unpack(core)
    in_turn(first, core * per_core, per_core)
    arrived(in_buf.at[1 - core], OBS)
    unpack(1 - core)
    in_turn(first, (1 - core) * per_core, per_core)
    x0[j, pl.ds(HALO, 8)] = summed()

    def spread(x, s_core, s_across, s_up, s_down, f_across, f_up, f_down):
        here = x.at[j, pl.ds(HALO, 8)]
        for to in (j, across):
            send(x.at[j, pl.ds(8, 4)], x.at[j, pl.ds(0, 4)], s_up, south, to)
            send(x.at[j, pl.ds(4, 4)], x.at[j, pl.ds(12, 4)], s_down, north, to)
        send(here, here, s_across, t, across)
        send(here, here, s_core, t, sibling)
        got = x.at[across, pl.ds(HALO, 8)]
        arrived(got, s_across)
        send(got, got, f_across, t, sibling)
        for key, forward, first_row in ((s_up, f_up, 0), (s_down, f_down, 12)):
            rows = pl.ds(first_row, 4)
            arrived(x.at[pl.ds(0, 2), rows], key)
            for half in range(2):
                edge = x.at[half * cores + core, rows]
                send(edge, edge, forward, t, sibling)
        arrived(here, s_core)
        arrived(got, f_across)
        arrived(x.at[pl.ds(0, 2), pl.ds(0, 4)], f_up)
        arrived(x.at[pl.ds(0, 2), pl.ds(12, 4)], f_down)

    spread(x0, AC0, AZ0, AU0, AD0, FZ0, FU0, FD0)
    for part in range(len(PARTS) - 1):
        part_arrived(part)

    def sweep(f, lo, hi):
        out = {}
        for r in range(lo, hi):
            here = f.get(r)
            beside = [f[n] for n in (r - 1, r + 1) if n in f]
            pair = []
            for h in range(2):
                terms = [row[h] for row in beside]
                if here is not None:
                    other = here[1 - h]
                    terms.append(other + pltpu.roll(other, (1, LANES - 1)[h], 1))
                beside_all = functools.reduce(jnp.add, terms)
                if here is None:
                    pair.append(kap[r, h] * beside_all)
                else:
                    pair.append(here[h] + kap[r, h] * (beside_all - 4.0 * here[h]))
            out[r] = pair
        return out

    def local_pass(x, control_out):
        up[...] = jnp.zeros(up.shape, F32)
        together = 4
        turns = 2 * members // together

        def group(i, carry):
            ids = []
            for g in range(together):
                lh, m = g % 2, i * (together // 2) + g // 2
                ids.append((lh, m, pl.ds(pl.multiple_of(m * levels + lh * 8, 8), 8)))
            fields = [
                {
                    r: [kap[r, h] * pert[r, h, at, :] * x[lh * 2 + h, r] for h in range(2)]
                    for r in range(16)
                }
                for lh, m, at in ids
            ]
            for k in range(4):
                fields = [sweep(f, k + 1, 15 - k) for f in fields]
            fields = [
                {r: [f[r][h] * ikap[r - HALO, h] for h in range(2)] for r in f} for f in fields
            ]
            if control_out:
                for f, (lh, m, at) in zip(fields, ids):
                    for r in range(8):
                        place_at = pl.ds(m * 128 + lh * 64 + r, 8, stride=8)
                        for h in range(2):
                            flat[h, place_at, :] = f[HALO + r][h]
            for k in range(4):
                fields = [sweep(f, 3 - k, 13 + k) for f in fields]
            for r in range(16):
                for h in range(2):
                    for half in range(2):
                        terms = [
                            pert[r, h, at, :] * f[r][h]
                            for f, (lh, m, at) in zip(fields, ids)
                            if lh == half
                        ]
                        up[half * 2 + h, r] += functools.reduce(jnp.add, terms)
            return carry

        lax.fori_loop(0, turns // 2, group, 0)
        if not control_out:
            part_arrived(len(PARTS) - 1)
        lax.fori_loop(turns // 2, turns, group, 0)

    def reduce_in_chip(source, from_core, key):
        for half in range(2):
            send(source.at[half * cores + 1 - core], from_core.at[half], key, t, sibling)

    def reduce_out(source, from_core, chip_sum, from_chip, from_north, from_south, keys):
        key, k_across, k_up, k_down = keys
        arrived(from_core, key)
        for half in range(2):
            chip_sum[half] = source[half * cores + core] + from_core[half]
        for half in range(2):
            to = half * cores + core
            send(chip_sum.at[half, pl.ds(12, 4)], from_north.at[chip], k_up, south, to)
            send(chip_sum.at[half, pl.ds(0, 4)], from_south.at[chip], k_down, north, to)
        send(chip_sum.at[1 - chip, pl.ds(HALO, 8)], from_chip, k_across, t, across)

    def reduced(chip_sum, from_chip, from_north, from_south, keys):
        key, k_across, k_up, k_down = keys
        arrived(from_chip, k_across)
        arrived(from_north, k_up)
        arrived(from_south, k_down)
        total = chip_sum[chip, pl.ds(HALO, 8)] + from_chip[...]
        edges = [from_north[0] + from_north[1], from_south[0] + from_south[1]]
        return total + jnp.concatenate(edges, axis=0)

    local_pass(x0, False)
    keys = (CR0, RZ0, RU0, RD0)
    reduce_in_chip(up, cr0, CR0)
    reduce_out(up, cr0, cs0, rz0, ru0, rd0, keys)
    state = (-STEP * scale * scale) * reduced(cs0, rz0, ru0, rd0, keys)
    state = jnp.concatenate(split2(state.reshape(64, LANES)), axis=0).astype(BF)

    def observe(which):
        for b in which:
            mixed = nn(state, onehot[b])
            mixed = mixed[:64] + mixed[64:]
            total = jnp.zeros((8, LANES), F32)
            for c in range(4):
                part = mixed[:, c * LANES : (c + 1) * LANES].reshape(8, 8, LANES)
                picked = jnp.sum(jnp.where(hits(b, c), part, 0.0), axis=0)
                total = total + feat[b, 20 + c : 21 + c, :] * picked
            y_own[b] = jnp.sum(feat[b, my_levels, :] * total, axis=0, keepdims=True)

    in_turn(observe)
    for d in range(1, groups):
        send(y_own, y_far.at[d - 1], YS, t, peer(d))
    arrived(y_far, YS)

    def misfit(b):
        y = y_own[b] + y_far[0, b] + y_far[1, b] + y_far[2, b]
        return feat[b, 25:26, :] * (y - feat[b, 24:25, :])

    acc[...] = jnp.zeros(acc.shape, F32)
    in_turn(lambda which: adjoint_obs(which, misfit))
    x1[j, pl.ds(HALO, 8)] = (-scale * STEP) * (STEP * x0[j, pl.ds(HALO, 8)] + summed())
    spread(x1, AC1, AZ1, AU1, AD1, FZ1, FU1, FD1)
    sent(cr0, CR0)
    local_pass(x1, True)

    sub = lax.broadcasted_iota(jnp.int32, (16, 8, LANES), 1)
    for lh in range(2):
        even, odd = up[lh * 2], up[lh * 2 + 1]
        vp[lh * 2] = jnp.where(sub < 4, even, pltpu.roll(odd, 4, 1))
        vp[lh * 2 + 1] = jnp.where(sub < 4, pltpu.roll(even, 4, 1), odd)

    def in_order(wide):
        hi, lo = split2(wide)
        return nn(hi.astype(BF), perm[1]) + nn(lo.astype(BF), perm[1])

    def written(m):
        return pltpu.make_async_copy(ready.at[m], control_ref.at[m], lsem.at[9 + m])

    def unmix(m):
        rows = pl.ds(m * 128, 128)
        wide = jnp.concatenate([flat[0, rows, :], flat[1, rows, :]], axis=1)
        ready[m] = in_order(wide).reshape(levels, 8, 256)
        written(m).start()

    keys = (CR1, RZ1, RU1, RD1)
    reduce_in_chip(vp, cr1, CR1)
    for m in range(members // 4):
        unmix(m)
    reduce_out(vp, cr1, cs1, rz1, ru1, rd1, keys)
    for m in range(members // 4, members):
        unmix(m)
    final = scale * reduced(cs1, rz1, ru1, rd1, keys)
    back = in_order(
        jnp.concatenate(
            [final.reshape(64, LANES), pltpu.roll(final, 4, 1).reshape(64, LANES)], axis=1
        )
    )
    for h in range(2):
        stage[h, 0:64, :] = back[:, h * LANES : (h + 1) * LANES]
        for level in range(4):
            incr_ref[level, :, h * LANES : (h + 1) * LANES] = stage[h, pl.ds(level, 8, stride=8), :]
    for m in range(members):
        written(m).wait()

    sent(in_buf.at[core, pl.ds(0, tiles - 1)], A2A)
    sent(kap_rows.at[0], KAP_U)
    sent(kap_rows.at[2], KAP_D)
    for part in range(len(PARTS)):
        part_sent(part)
    sent(in_buf.at[core], OBS)
    sent(y_far, YS)
    sent(cr1, CR1)
    for k in (AC0, AZ0, FZ0, RZ0, AC1, AZ1, FZ1, RZ1):
        sent(rz0, k)
    for k in (AU0, AD0, FU0, FD0, RU0, RD0, AU1, AD1, FU1, FD1, RU1, RD1):
        sent(ru0, k)


def write_out(control_ref, incr_ref, control_out, incr_out, control_held, incr_held, sems):
    count = control_ref.shape[0]
    ways = [(control_ref.at[m], control_held.at[m], control_out.at[m]) for m in range(count)]
    ways.append((incr_ref, incr_held, incr_out))
    reads = [pltpu.make_async_copy(a, b, sems.at[0, n]) for n, (a, b, c) in enumerate(ways)]
    writes = [pltpu.make_async_copy(b, c, sems.at[1, n]) for n, (a, b, c) in enumerate(ways)]
    for read in reads:
        read.start()
    for read, write in zip(reads, writes):
        read.wait()
        write.start()
    for write in writes:
        write.wait()


def on_device(tiles, groups, perturbations, classes, target, cells, interp, jac, innov, inverse):
    members, levels, rows, cols = perturbations.shape
    obs = target.shape[0]
    vm = pl.BlockSpec(memory_space=pltpu.VMEM)
    hbm = pl.BlockSpec(memory_space=pltpu.HBM)
    window = (groups, 16, 8, LANES)
    message = FEATURES * MOST // 2
    blocks = MOST * tiles // LANES
    reduction = [
        ((2, 16, 8, LANES), F32), ((2, 16, 8, LANES), F32), ((8, 8, LANES), F32),
        ((2, 4, 8, LANES), F32), ((2, 4, 8, LANES), F32),
    ]
    scratch = [
        (perturbations.shape, perturbations.dtype),
        (classes.shape, classes.dtype),
        ((1, obs), target.dtype),
        (cells.shape, cells.dtype),
        (interp.shape, interp.dtype),
        (jac.shape, jac.dtype),
        ((1, obs), innov.dtype),
        ((1, obs), inverse.dtype),
        ((2, 256, 256), BF),
        ((FEATURES, obs), F32),
        ((3, message, obs), BF),
        ((tiles, 1, message), F32),
        ((2, tiles, 1, message), F32),
        ((blocks, FEATURES, LANES), F32),
        ((blocks, LANES, 4 * LANES), BF),
        ((12, 128, 4 * LANES), BF),
        ((128, LANES), F32),
        ((16, 2, members * levels, LANES), F32),
        ((2, LANES, LANES), F32),
        ((3, 8, 256), F32),
        ((16, 2, 8, LANES), F32),
        ((8, 2, 8, LANES), F32),
        (window, F32), (window, F32), (window, F32), (window, F32),
        *reduction,
        *reduction,
        ((blocks, 1, LANES), F32),
        ((groups - 1, blocks, 1, LANES), F32),
        ((2, members * levels * rows, LANES), F32),
        ((members, levels, rows, cols), F32),
        ((2, 4, 2, members * levels // 2, LANES), F32),
    ]
    control, increment = pl.pallas_call(
        functools.partial(kernel, tiles, groups, members),
        out_shape=(
            jax.ShapeDtypeStruct((members, levels, rows, cols), F32),
            jax.ShapeDtypeStruct((levels // groups, rows, cols), F32),
        ),
        in_specs=[hbm] * 8,
        out_specs=(hbm, vm),
        scratch_shapes=[pltpu.VMEM(shape, dtype) for shape, dtype in scratch]
        + [
            pltpu.SemaphoreType.DMA((N_SEM,)),
            pltpu.SemaphoreType.DMA((N_SEM,)),
            pltpu.SemaphoreType.DMA((9 + members,)),
        ],
        compiler_params=pltpu.CompilerParams(
            collective_id=0, has_side_effects=True, vmem_limit_bytes=60 * 1024 * 1024
        ),
        name="assimilate",
    )(
        perturbations, classes, target.reshape(1, obs), cells, interp, jac,
        innov.reshape(1, obs), inverse.reshape(1, obs),
    )
    return pl.pallas_call(
        write_out,
        out_shape=(
            jax.ShapeDtypeStruct(control.shape, F32), jax.ShapeDtypeStruct(increment.shape, F32)
        ),
        in_specs=[hbm, hbm],
        out_specs=(hbm, hbm),
        scratch_shapes=[
            pltpu.VMEM(control.shape, F32),
            pltpu.VMEM(increment.shape, F32),
            pltpu.SemaphoreType.DMA((2, members + 1)),
        ],
        compiler_params=pltpu.CompilerParams(vmem_limit_bytes=60 * 1024 * 1024),
        name="write_out",
    )(control, increment)


def solution(mesh):
    in_specs = (
        P("mem", None, "tile", None),
        P("tile", None),
        P("tile", None),
        P(None, "tile"),
        P(None, "tile"),
        P(None, "tile"),
        P("tile"),
        P("tile"),
    )
    out_specs = (P("mem", None, "tile", None), P("mem", "tile", None))
    return jax.shard_map(
        functools.partial(on_device, mesh.shape["tile"], mesh.shape["mem"]),
        mesh=mesh, in_specs=in_specs, out_specs=out_specs, check_vma=False,
    )
```

```python
import functools
import math

import jax
import jax.numpy as jnp
from jax import lax
from jax.experimental import pallas as pl
from jax.experimental.pallas import tpu as pltpu
from jax.sharding import PartitionSpec as P

MESH = pl.DeviceIdType.MESH
BF = jnp.bfloat16
F32 = jnp.float32
DIFFUSIVITIES = (0.06, 0.1, 0.15, 0.22)
STEP = 0.5
MOST = 48
FEATURES = 32
HALO = 4
LANES = 128

(A2A, KAP_U, KAP_D, OBS, AC0, AZ0, AU0, AD0, FZ0, FU0, FD0, CR0, RZ0, RU0, RD0, YS,
 AC1, AZ1, AU1, AD1, FZ1, FU1, FD1, CR1, RZ1, RU1, RD1, PERT) = range(28)
PARTS = ((0, 32), (32, 64), (64, 128))
EARLY = 1
N_SEM = PERT + 8 * len(PARTS)


def nt(a, b):
    return lax.dot_general(a, b, (((1,), (1,)), ((), ())), preferred_element_type=F32)


def nn(a, b):
    return jnp.dot(a, b, preferred_element_type=F32)


def split2(x):
    hi = x.astype(BF).astype(F32)
    return hi, x - hi


def kernel(
    tiles, groups, members,
    pert_hbm, classes_hbm, target_hbm, cells_hbm, interp_hbm, jac_hbm, innov_hbm, inv_hbm,
    control_ref, incr_ref,
    pert_ref, classes_ref, target_ref, cells_ref, interp_ref, jac_ref, innov_ref, inv_ref,
    perm, pay, val, out_buf, in_buf, feat, onehot, acols, acc,
    pert, stage, kap_rows, kap, ikap,
    x0, x1, up, vp, cr0, cs0, rz0, ru0, rd0, cr1, cs1, rz1, ru1, rd1, y_own, y_far, flat, ready, relay,
    ssem, rsem, lsem,
):
    t = lax.axis_index("tile")
    j = lax.axis_index("mem")
    north, south = lax.rem(t + tiles - 1, tiles), lax.rem(t + 1, tiles)
    cores = 2
    chip, core = j // cores, lax.rem(j, cores)
    slots = MOST // cores
    levels = 16
    scale = 1.0 / math.sqrt(members * groups - 1)
    obs = pay.shape[1]
    early = EARLY

    sibling = j + 1 - 2 * core
    across = lax.rem(j + cores, groups)

    def peer(d):
        return lax.rem(j + d, groups)

    def band(d):
        return lax.rem(t + d, tiles)

    def send(src, dst, k, tile, mem, k_out=None):
        pltpu.make_async_remote_copy(
            src_ref=src, dst_ref=dst, send_sem=ssem.at[k if k_out is None else k_out], recv_sem=rsem.at[k],
            device_id={"tile": tile, "mem": mem}, device_id_type=MESH,
        ).start()

    def arrived(like, k):
        pltpu.make_async_copy(like, like, rsem.at[k]).wait()

    def sent(like, k):
        pltpu.make_async_copy(like, like, ssem.at[k]).wait()

    fetches = [
        pltpu.make_async_copy(source, into, lsem.at[1 + k])
        for k, (source, into) in enumerate((
            (pert_hbm, pert_ref), (classes_hbm, classes_ref),
            (target_hbm, target_ref), (cells_hbm, cells_ref), (interp_hbm, interp_ref),
            (jac_hbm, jac_ref), (innov_hbm, innov_ref), (inv_hbm, inv_ref),
        ))
    ]
    for fetch in fetches:
        fetch.start()

    barrier = pltpu.get_barrier_semaphore()

    def greet(tile, mem):
        pl.semaphore_signal(
            barrier, inc=1, device_id={"tile": tile, "mem": mem}, device_id_type=MESH
        )

    def greet_band(d, carry):
        greet(band(d), j)
        return carry

    lax.fori_loop(1, tiles, greet_band, 0, unroll=9)
    for d in range(1, groups):
        greet(t, peer(d))
    greet(north, across)
    greet(south, across)

    row_id = lax.broadcasted_iota(jnp.int32, (256, 256), 0)
    col_id = lax.broadcasted_iota(jnp.int32, (256, 256), 1)
    perm[0] = jnp.where(col_id == (row_id & 1) * 128 + (row_id >> 1), 1.0, 0.0).astype(BF)
    perm[1] = jnp.where(row_id == (col_id & 1) * 128 + (col_id >> 1), 1.0, 0.0).astype(BF)

    for fetch in fetches[:2]:
        fetch.wait()

    def arrange(i, carry):
        some = [i * 4 + n for n in range(4)]
        for m in some:
            block = pert_ref[m].astype(F32).reshape(levels * 8, 256).astype(BF)
            moved = nn(block, perm[0])
            rows = pl.ds(pl.multiple_of(m * 128, 128), 128)
            for h in range(2):
                flat[h, rows, :] = moved[:, h * LANES : (h + 1) * LANES]
        for m in some:
            for r in range(8):
                for lh in range(2):
                    at = pl.ds(pl.multiple_of(m * levels + lh * 8, 8), 8)
                    for h in range(2):
                        rows = pl.ds(m * 128 + lh * 64 + r, 8, stride=8)
                        pert[HALO + r, h, at, :] = flat[h, rows, :]
        return carry

    lax.fori_loop(0, members // 4, arrange, 0)

    classes = nn(classes_ref[...].astype(F32).astype(BF), perm[0])
    kappa = jnp.zeros(classes.shape, F32)
    for position, coefficient in enumerate(DIFFUSIVITIES):
        kappa = kappa + jnp.where(classes == float(position), coefficient, 0.0)
    kap_rows[1] = kappa

    pl.semaphore_wait(barrier, tiles - 1 + groups - 1 + 2)

    along_x = lax.rem(t, 4)
    ways = (
        (8, 0, south, 3, -3, 4),
        (4, 12, north, 0, 3, -4),
    )

    def edge(first_row, lo, hi):
        return pert.at[pl.ds(first_row, 4), :, pl.ds(lo, hi - lo)]

    def shares(part):
        lo, hi = PARTS[part]
        middle = (lo + hi) // 2
        return (lo, middle), (middle, hi)

    def key_of(way, part):
        return PERT + (way * len(PARTS) + part) * 4

    def waiting(way, part):
        lo, hi = shares(part)[1]
        return relay.at[way, :, :, pl.ds(PARTS[part][0] // 2, hi - lo)]

    def send_part(part, to_relay):
        one, two = shares(part)
        for way, (here, there, to, wraps, hop, onward) in enumerate(ways):
            key = key_of(way, part)
            if to_relay:

                @pl.when(along_x == wraps)
                def _():
                    send(edge(here, *two), waiting(way, part), key + 2, band(hop + tiles), j)

            else:
                send(edge(here, *one), edge(there, *one), key, to, j)

                @pl.when(along_x != wraps)
                def _():
                    send(edge(here, *two), edge(there, *two), key + 1, to, j)

    def forward_part(part):
        two = shares(part)[1]
        for way, (here, there, to, wraps, hop, onward) in enumerate(ways):
            key = key_of(way, part)

            @pl.when(along_x == 3 - wraps)
            def _():
                arrived(waiting(way, part), key + 2)
                send(
                    waiting(way, part), edge(there, *two), key + 1, band(onward + tiles), j, key + 3
                )

    def part_arrived(part):
        one, two = shares(part)
        for way, (here, there, to, wraps, hop, onward) in enumerate(ways):
            arrived(edge(there, *one), key_of(way, part))
            arrived(edge(there, *two), key_of(way, part) + 1)

    def part_sent(part):
        one, two = shares(part)
        for way, (here, there, to, wraps, hop, onward) in enumerate(ways):
            key = key_of(way, part)
            sent(edge(here, *one), key)

            @pl.when(along_x == wraps)
            def _():
                sent(edge(here, *two), key + 2)

            @pl.when(along_x != wraps)
            def _():
                sent(edge(here, *two), key + 1)

            @pl.when(along_x == 3 - wraps)
            def _():
                sent(waiting(way, part), key + 3)

    send(kap_rows.at[1], kap_rows.at[0], KAP_U, south, j)
    send(kap_rows.at[1], kap_rows.at[2], KAP_D, north, j)
    for part in range(len(PARTS)):
        send_part(part, True)
    for part in range(early):
        send_part(part, False)

    for fetch in fetches[2:]:
        fetch.wait()

    target = target_ref[...]
    bands = lax.broadcasted_iota(jnp.int32, (tiles, obs), 0)
    member_of = jnp.where(target == bands, 1.0, 0.0)
    member_bf = member_of.astype(BF)
    before = jnp.where(row_id < col_id, 1.0, 0.0).astype(BF)
    base = jnp.zeros((tiles, 1), F32)
    ranks = []
    for b in range(obs // 256):
        part = slice(b * 256, (b + 1) * 256)
        count = nn(member_bf[:, part], before) + base
        ranks.append(jnp.sum(member_of[:, part] * count, axis=0, keepdims=True))
        base = base + jnp.sum(member_of[:, part], axis=1, keepdims=True)
    rank = jnp.concatenate(ranks, axis=1).astype(jnp.int32) - core * slots

    pay[0:16, :] = jac_ref[...]
    pay[16:24, :] = jnp.concatenate([cells_ref[...].astype(F32), interp_ref[...]], axis=0)
    pay[24:32, :] = jnp.concatenate(
        [innov_ref[...], inv_ref[...], jnp.zeros((6, obs), F32)], axis=0
    )
    whole = pay[...]
    pieces = [piece.astype(BF) for piece in split2(whole)]
    rank = rank.astype(F32).astype(BF)
    nothing = jnp.zeros((), BF)
    for q in range(slots):
        mine = rank == jnp.full((), q, BF)
        for k, piece in enumerate(pieces):
            val[k, q * FEATURES : (q + 1) * FEATURES, :] = jnp.where(mine, piece, nothing)
    packed = nt(member_bf, val[0]) + nt(member_bf, val[1])
    out_buf[:, 0, :] = packed

    def send_band(d, carry):
        send(out_buf.at[band(d)], in_buf.at[core, t], A2A, band(d), j)
        return carry

    lax.fori_loop(1, tiles, send_band, 0, unroll=9)
    for part in range(len(PARTS)):
        forward_part(part)
        if part >= early:
            send_part(part, False)
    own = pltpu.make_async_copy(out_buf.at[t], in_buf.at[core, t], lsem.at[0])
    own.start()
    arrived(kap_rows.at[0], KAP_U)
    arrived(kap_rows.at[2], KAP_D)
    for r in range(16):
        block, row = divmod(r + 4, 8)
        line = kap_rows[block, row : row + 1, :]
        if r < 4:
            line = jnp.where(t == 0, 0.0, line)
        if r >= 12:
            line = jnp.where(t == tiles - 1, 0.0, line)
        for h in range(2):
            wide = jnp.broadcast_to(line[:, h * LANES : (h + 1) * LANES], (8, LANES))
            kap[r, h] = wide
            if 4 <= r < 12:
                ikap[r - 4, h] = 1.0 / wide

    own.wait()
    arrived(in_buf.at[core, pl.ds(0, tiles - 1)], A2A)
    send(in_buf.at[core], in_buf.at[core], OBS, t, sibling)

    blocks = MOST * tiles // LANES
    per_core = blocks // cores

    def unpack(source):
        for g in range(0, slots * FEATURES // LANES, 2):
            both = jnp.concatenate(
                [in_buf[source, :, 0, n * LANES : (n + 1) * LANES] for n in (g, g + 1)], axis=0
            ).T
            for b in range(LANES // FEATURES):
                at = source * per_core + g * 2 + b
                feat[at] = both[b * FEATURES : (b + 1) * FEATURES, :]

    along = 12

    def in_turn(step, start=0, count=blocks):
        def several(i, carry):
            step([start + i * along + n for n in range(along)])
            return carry

        lax.fori_loop(0, count // along, several, 0)

    my_levels = pl.ds(pl.multiple_of(chip * 8, 8), 8)

    def hits(b, c):
        cell = feat[b, 16 + c : 17 + c, :].astype(jnp.int32)
        row = jnp.where((cell & 1) == core, cell >> 8, -1)
        rows = lax.broadcasted_iota(jnp.int32, (8, 8, LANES), 0)
        return rows == row.reshape(1, 1, LANES)

    def build(which):
        spots = lax.broadcasted_iota(jnp.int32, (LANES, LANES), 0).astype(F32).astype(BF)
        one, none = jnp.ones((), BF), jnp.zeros((), BF)
        for b in which:
            low = (feat[b, 16:24, :].astype(jnp.int32) & 255) >> 1
            low = low.astype(F32).astype(BF)
            for c in range(4):
                spot = spots == low[c : c + 1, :]
                onehot[b, :, c * LANES : (c + 1) * LANES] = jnp.where(spot, one, none)

    def adjoint_obs(which, residual):
        for n, b in enumerate(which):
            z = residual(b)
            jac = feat[b, my_levels, :]
            for c in range(4):
                value = jac * (feat[b, 20 + c : 21 + c, :] * z)
                mask = hits(b, c)
                for k, piece in enumerate(split2(value)):
                    wide = jnp.where(mask, piece.reshape(1, 8, LANES), 0.0).reshape(64, LANES)
                    acols[n, k * 64 : (k + 1) * 64, c * LANES : (c + 1) * LANES] = wide.astype(BF)
        total = acc[...]
        for n, b in enumerate(which):
            total = total + nt(acols[n], onehot[b])
        acc[...] = total

    def summed():
        both = acc[...]
        return (both[:64] + both[64:]).reshape(8, 8, LANES)

    def first(which):
        build(which)
        adjoint_obs(which, lambda b: -(feat[b, 25:26, :] * feat[b, 24:25, :]))

    acc[...] = jnp.zeros(acc.shape, F32)
    unpack(core)
    in_turn(first, core * per_core, per_core)
    arrived(in_buf.at[1 - core], OBS)
    unpack(1 - core)
    in_turn(first, (1 - core) * per_core, per_core)
    x0[j, pl.ds(HALO, 8)] = summed()

    def spread(x, s_core, s_across, s_up, s_down, f_across, f_up, f_down):
        here = x.at[j, pl.ds(HALO, 8)]
        for to in (j, across):
            send(x.at[j, pl.ds(8, 4)], x.at[j, pl.ds(0, 4)], s_up, south, to)
            send(x.at[j, pl.ds(4, 4)], x.at[j, pl.ds(12, 4)], s_down, north, to)
        send(here, here, s_across, t, across)
        send(here, here, s_core, t, sibling)
        got = x.at[across, pl.ds(HALO, 8)]
        arrived(got, s_across)
        send(got, got, f_across, t, sibling)
        for key, forward, first_row in ((s_up, f_up, 0), (s_down, f_down, 12)):
            rows = pl.ds(first_row, 4)
            arrived(x.at[pl.ds(0, 2), rows], key)
            for half in range(2):
                edge = x.at[half * cores + core, rows]
                send(edge, edge, forward, t, sibling)
        arrived(here, s_core)
        arrived(got, f_across)
        arrived(x.at[pl.ds(0, 2), pl.ds(0, 4)], f_up)
        arrived(x.at[pl.ds(0, 2), pl.ds(12, 4)], f_down)

    spread(x0, AC0, AZ0, AU0, AD0, FZ0, FU0, FD0)
    for part in range(len(PARTS) - 1):
        part_arrived(part)

    def sweep(f, lo, hi):
        out = {}
        for r in range(lo, hi):
            here = f.get(r)
            beside = [f[n] for n in (r - 1, r + 1) if n in f]
            pair = []
            for h in range(2):
                terms = [row[h] for row in beside]
                if here is not None:
                    other = here[1 - h]
                    terms.append(other + pltpu.roll(other, (1, LANES - 1)[h], 1))
                beside_all = functools.reduce(jnp.add, terms)
                if here is None:
                    pair.append(kap[r, h] * beside_all)
                else:
                    pair.append(here[h] + kap[r, h] * (beside_all - 4.0 * here[h]))
            out[r] = pair
        return out

    def local_pass(x, control_out):
        up[...] = jnp.zeros(up.shape, F32)
        together = 4
        turns = 2 * members // together

        def group(i, carry):
            ids = []
            for g in range(together):
                lh, m = g % 2, i * (together // 2) + g // 2
                ids.append((lh, m, pl.ds(pl.multiple_of(m * levels + lh * 8, 8), 8)))
            fields = [
                {
                    r: [kap[r, h] * pert[r, h, at, :] * x[lh * 2 + h, r] for h in range(2)]
                    for r in range(16)
                }
                for lh, m, at in ids
            ]
            for k in range(4):
                fields = [sweep(f, k + 1, 15 - k) for f in fields]
            fields = [
                {r: [f[r][h] * ikap[r - HALO, h] for h in range(2)] for r in f} for f in fields
            ]
            if control_out:
                for f, (lh, m, at) in zip(fields, ids):
                    for r in range(8):
                        place_at = pl.ds(m * 128 + lh * 64 + r, 8, stride=8)
                        for h in range(2):
                            flat[h, place_at, :] = f[HALO + r][h]
            for k in range(4):
                fields = [sweep(f, 3 - k, 13 + k) for f in fields]
            for r in range(16):
                for h in range(2):
                    for half in range(2):
                        terms = [
                            pert[r, h, at, :] * f[r][h]
                            for f, (lh, m, at) in zip(fields, ids)
                            if lh == half
                        ]
                        up[half * 2 + h, r] += functools.reduce(jnp.add, terms)
            return carry

        lax.fori_loop(0, turns // 2, group, 0)
        if not control_out:
            part_arrived(len(PARTS) - 1)
        lax.fori_loop(turns // 2, turns, group, 0)

    def reduce_in_chip(source, from_core, key):
        for half in range(2):
            send(source.at[half * cores + 1 - core], from_core.at[half], key, t, sibling)

    def reduce_out(source, from_core, chip_sum, from_chip, from_north, from_south, keys):
        key, k_across, k_up, k_down = keys
        arrived(from_core, key)
        for half in range(2):
            chip_sum[half] = source[half * cores + core] + from_core[half]
        for half in range(2):
            to = half * cores + core
            send(chip_sum.at[half, pl.ds(12, 4)], from_north.at[chip], k_up, south, to)
            send(chip_sum.at[half, pl.ds(0, 4)], from_south.at[chip], k_down, north, to)
        send(chip_sum.at[1 - chip, pl.ds(HALO, 8)], from_chip, k_across, t, across)

    def reduced(chip_sum, from_chip, from_north, from_south, keys):
        key, k_across, k_up, k_down = keys
        arrived(from_chip, k_across)
        arrived(from_north, k_up)
        arrived(from_south, k_down)
        total = chip_sum[chip, pl.ds(HALO, 8)] + from_chip[...]
        edges = [from_north[0] + from_north[1], from_south[0] + from_south[1]]
        return total + jnp.concatenate(edges, axis=0)

    local_pass(x0, False)
    keys = (CR0, RZ0, RU0, RD0)
    reduce_in_chip(up, cr0, CR0)
    reduce_out(up, cr0, cs0, rz0, ru0, rd0, keys)
    state = (-STEP * scale * scale) * reduced(cs0, rz0, ru0, rd0, keys)
    state = jnp.concatenate(split2(state.reshape(64, LANES)), axis=0).astype(BF)

    def observe(which):
        for b in which:
            mixed = nn(state, onehot[b])
            mixed = mixed[:64] + mixed[64:]
            total = jnp.zeros((8, LANES), F32)
            for c in range(4):
                part = mixed[:, c * LANES : (c + 1) * LANES].reshape(8, 8, LANES)
                picked = jnp.sum(jnp.where(hits(b, c), part, 0.0), axis=0)
                total = total + feat[b, 20 + c : 21 + c, :] * picked
            y_own[b] = jnp.sum(feat[b, my_levels, :] * total, axis=0, keepdims=True)

    in_turn(observe)
    for d in range(1, groups):
        send(y_own, y_far.at[d - 1], YS, t, peer(d))
    arrived(y_far, YS)

    def misfit(b):
        y = y_own[b] + y_far[0, b] + y_far[1, b] + y_far[2, b]
        return feat[b, 25:26, :] * (y - feat[b, 24:25, :])

    acc[...] = jnp.zeros(acc.shape, F32)
    in_turn(lambda which: adjoint_obs(which, misfit))
    x1[j, pl.ds(HALO, 8)] = (-scale * STEP) * (STEP * x0[j, pl.ds(HALO, 8)] + summed())
    spread(x1, AC1, AZ1, AU1, AD1, FZ1, FU1, FD1)
    sent(cr0, CR0)
    local_pass(x1, True)

    sub = lax.broadcasted_iota(jnp.int32, (16, 8, LANES), 1)
    for lh in range(2):
        even, odd = up[lh * 2], up[lh * 2 + 1]
        vp[lh * 2] = jnp.where(sub < 4, even, pltpu.roll(odd, 4, 1))
        vp[lh * 2 + 1] = jnp.where(sub < 4, pltpu.roll(even, 4, 1), odd)

    def in_order(wide):
        hi, lo = split2(wide)
        return nn(hi.astype(BF), perm[1]) + nn(lo.astype(BF), perm[1])

    def written(m):
        return pltpu.make_async_copy(ready.at[m], control_ref.at[m], lsem.at[9 + m])

    def unmix(m):
        rows = pl.ds(m * 128, 128)
        wide = jnp.concatenate([flat[0, rows, :], flat[1, rows, :]], axis=1)
        ready[m] = in_order(wide).reshape(levels, 8, 256)
        written(m).start()

    keys = (CR1, RZ1, RU1, RD1)
    reduce_in_chip(vp, cr1, CR1)
    for m in range(members // 4):
        unmix(m)
    reduce_out(vp, cr1, cs1, rz1, ru1, rd1, keys)
    for m in range(members // 4, members):
        unmix(m)
    final = scale * reduced(cs1, rz1, ru1, rd1, keys)
    back = in_order(
        jnp.concatenate(
            [final.reshape(64, LANES), pltpu.roll(final, 4, 1).reshape(64, LANES)], axis=1
        )
    )
    for h in range(2):
        stage[h, 0:64, :] = back[:, h * LANES : (h + 1) * LANES]
        for level in range(4):
            incr_ref[level, :, h * LANES : (h + 1) * LANES] = stage[h, pl.ds(level, 8, stride=8), :]
    for m in range(members):
        written(m).wait()

    sent(in_buf.at[core, pl.ds(0, tiles - 1)], A2A)
    sent(kap_rows.at[0], KAP_U)
    sent(kap_rows.at[2], KAP_D)
    for part in range(len(PARTS)):
        part_sent(part)
    sent(in_buf.at[core], OBS)
    sent(y_far, YS)
    sent(cr1, CR1)
    for k in (AC0, AZ0, FZ0, RZ0, AC1, AZ1, FZ1, RZ1):
        sent(rz0, k)
    for k in (AU0, AD0, FU0, FD0, RU0, RD0, AU1, AD1, FU1, FD1, RU1, RD1):
        sent(ru0, k)


def write_out(control_ref, incr_ref, control_out, incr_out, control_held, incr_held, sems):
    count = control_ref.shape[0]
    ways = [(control_ref.at[m], control_held.at[m], control_out.at[m]) for m in range(count)]
    ways.append((incr_ref, incr_held, incr_out))
    reads = [pltpu.make_async_copy(a, b, sems.at[0, n]) for n, (a, b, c) in enumerate(ways)]
    writes = [pltpu.make_async_copy(b, c, sems.at[1, n]) for n, (a, b, c) in enumerate(ways)]
    for read in reads:
        read.start()
    for read, write in zip(reads, writes):
        read.wait()
        write.start()
    for write in writes:
        write.wait()


def on_device(tiles, groups, perturbations, classes, target, cells, interp, jac, innov, inverse):
    members, levels, rows, cols = perturbations.shape
    obs = target.shape[0]
    vm = pl.BlockSpec(memory_space=pltpu.VMEM)
    hbm = pl.BlockSpec(memory_space=pltpu.HBM)
    window = (groups, 16, 8, LANES)
    message = FEATURES * MOST // 2
    blocks = MOST * tiles // LANES
    reduction = [
        ((2, 16, 8, LANES), F32), ((2, 16, 8, LANES), F32), ((8, 8, LANES), F32),
        ((2, 4, 8, LANES), F32), ((2, 4, 8, LANES), F32),
    ]
    scratch = [
        (perturbations.shape, perturbations.dtype),
        (classes.shape, classes.dtype),
        ((1, obs), target.dtype),
        (cells.shape, cells.dtype),
        (interp.shape, interp.dtype),
        (jac.shape, jac.dtype),
        ((1, obs), innov.dtype),
        ((1, obs), inverse.dtype),
        ((2, 256, 256), BF),
        ((FEATURES, obs), F32),
        ((2, message, obs), BF),
        ((tiles, 1, message), F32),
        ((2, tiles, 1, message), F32),
        ((blocks, FEATURES, LANES), F32),
        ((blocks, LANES, 4 * LANES), BF),
        ((12, 128, 4 * LANES), BF),
        ((128, LANES), F32),
        ((16, 2, members * levels, LANES), F32),
        ((2, LANES, LANES), F32),
        ((3, 8, 256), F32),
        ((16, 2, 8, LANES), F32),
        ((8, 2, 8, LANES), F32),
        (window, F32), (window, F32), (window, F32), (window, F32),
        *reduction,
        *reduction,
        ((blocks, 1, LANES), F32),
        ((groups - 1, blocks, 1, LANES), F32),
        ((2, members * levels * rows, LANES), F32),
        ((members, levels, rows, cols), F32),
        ((2, 4, 2, members * levels // 2, LANES), F32),
    ]
    control, increment = pl.pallas_call(
        functools.partial(kernel, tiles, groups, members),
        out_shape=(
            jax.ShapeDtypeStruct((members, levels, rows, cols), F32),
            jax.ShapeDtypeStruct((levels // groups, rows, cols), F32),
        ),
        in_specs=[hbm] * 8,
        out_specs=(hbm, vm),
        scratch_shapes=[pltpu.VMEM(shape, dtype) for shape, dtype in scratch]
        + [
            pltpu.SemaphoreType.DMA((N_SEM,)),
            pltpu.SemaphoreType.DMA((N_SEM,)),
            pltpu.SemaphoreType.DMA((9 + members,)),
        ],
        compiler_params=pltpu.CompilerParams(
            collective_id=0, has_side_effects=True, vmem_limit_bytes=60 * 1024 * 1024
        ),
        name="assimilate",
    )(
        perturbations, classes, target.reshape(1, obs), cells, interp, jac,
        innov.reshape(1, obs), inverse.reshape(1, obs),
    )
    return pl.pallas_call(
        write_out,
        out_shape=(
            jax.ShapeDtypeStruct(control.shape, F32), jax.ShapeDtypeStruct(increment.shape, F32)
        ),
        in_specs=[hbm, hbm],
        out_specs=(hbm, hbm),
        scratch_shapes=[
            pltpu.VMEM(control.shape, F32),
            pltpu.VMEM(increment.shape, F32),
            pltpu.SemaphoreType.DMA((2, members + 1)),
        ],
        compiler_params=pltpu.CompilerParams(vmem_limit_bytes=60 * 1024 * 1024),
        name="write_out",
    )(control, increment)


def solution(mesh):
    in_specs = (
        P("mem", None, "tile", None),
        P("tile", None),
        P("tile", None),
        P(None, "tile"),
        P(None, "tile"),
        P(None, "tile"),
        P("tile"),
        P("tile"),
    )
    out_specs = (P("mem", None, "tile", None), P("mem", "tile", None))
    return jax.shard_map(
        functools.partial(on_device, mesh.shape["tile"], mesh.shape["mem"]),
        mesh=mesh, in_specs=in_specs, out_specs=out_specs, check_vma=False,
    )
```

```python
import functools
import math

import jax
import jax.numpy as jnp
from jax import lax
from jax.experimental import pallas as pl
from jax.experimental.pallas import tpu as pltpu
from jax.sharding import PartitionSpec as P

MESH = pl.DeviceIdType.MESH
BF = jnp.bfloat16
F32 = jnp.float32
DIFFUSIVITIES = (0.06, 0.1, 0.15, 0.22)
STEP = 0.5
MOST = 48
FEATURES = 32
HALO = 4
LANES = 128

(A2A, KAP_U, KAP_D, OBS, AC0, AZ0, AU0, AD0, FZ0, FU0, FD0, CR0, RZ0, RU0, RD0, YS,
 AC1, AZ1, AU1, AD1, FZ1, FU1, FD1, CR1, RZ1, RU1, RD1, PERT) = range(28)
PARTS = ((0, 32), (32, 64), (64, 128))
EARLY = 2
N_SEM = PERT + 8 * len(PARTS)


def nt(a, b):
    return lax.dot_general(a, b, (((1,), (1,)), ((), ())), preferred_element_type=F32)


def nn(a, b):
    return jnp.dot(a, b, preferred_element_type=F32)


def split2(x):
    hi = x.astype(BF).astype(F32)
    return hi, x - hi


def kernel(
    tiles, groups, members,
    pert_hbm, classes_hbm, target_hbm, cells_hbm, interp_hbm, jac_hbm, innov_hbm, inv_hbm,
    control_ref, incr_ref,
    pert_ref, classes_ref, target_ref, cells_ref, interp_ref, jac_ref, innov_ref, inv_ref,
    perm, pay, val, out_buf, in_buf, feat, onehot, acols, acc,
    pert, stage, kap_rows, kap, ikap,
    x0, x1, up, vp, cr0, cs0, rz0, ru0, rd0, cr1, cs1, rz1, ru1, rd1, y_own, y_far, flat, ready, relay,
    ssem, rsem, lsem,
):
    t = lax.axis_index("tile")
    j = lax.axis_index("mem")
    north, south = lax.rem(t + tiles - 1, tiles), lax.rem(t + 1, tiles)
    cores = 2
    chip, core = j // cores, lax.rem(j, cores)
    slots = MOST // cores
    levels = 16
    scale = 1.0 / math.sqrt(members * groups - 1)
    obs = pay.shape[1]
    early = EARLY

    sibling = j + 1 - 2 * core
    across = lax.rem(j + cores, groups)

    def peer(d):
        return lax.rem(j + d, groups)

    def band(d):
        return lax.rem(t + d, tiles)

    def send(src, dst, k, tile, mem, k_out=None):
        pltpu.make_async_remote_copy(
            src_ref=src, dst_ref=dst, send_sem=ssem.at[k if k_out is None else k_out], recv_sem=rsem.at[k],
            device_id={"tile": tile, "mem": mem}, device_id_type=MESH,
        ).start()

    def arrived(like, k):
        pltpu.make_async_copy(like, like, rsem.at[k]).wait()

    def sent(like, k):
        pltpu.make_async_copy(like, like, ssem.at[k]).wait()

    fetches = [
        pltpu.make_async_copy(source, into, lsem.at[1 + k])
        for k, (source, into) in enumerate((
            (pert_hbm, pert_ref), (classes_hbm, classes_ref),
            (target_hbm, target_ref), (cells_hbm, cells_ref), (interp_hbm, interp_ref),
            (jac_hbm, jac_ref), (innov_hbm, innov_ref), (inv_hbm, inv_ref),
        ))
    ]
    for fetch in fetches:
        fetch.start()

    barrier = pltpu.get_barrier_semaphore()

    def greet(tile, mem):
        pl.semaphore_signal(
            barrier, inc=1, device_id={"tile": tile, "mem": mem}, device_id_type=MESH
        )

    def greet_band(d, carry):
        greet(band(d), j)
        return carry

    lax.fori_loop(1, tiles, greet_band, 0, unroll=9)
    for d in range(1, groups):
        greet(t, peer(d))
    greet(north, across)
    greet(south, across)

    row_id = lax.broadcasted_iota(jnp.int32, (256, 256), 0)
    col_id = lax.broadcasted_iota(jnp.int32, (256, 256), 1)
    perm[0] = jnp.where(col_id == (row_id & 1) * 128 + (row_id >> 1), 1.0, 0.0).astype(BF)
    perm[1] = jnp.where(row_id == (col_id & 1) * 128 + (col_id >> 1), 1.0, 0.0).astype(BF)

    for fetch in fetches[:2]:
        fetch.wait()

    def arrange(m, carry):
        block = pert_ref[m].astype(F32).reshape(levels * 8, 256).astype(BF)
        moved = nn(block, perm[0])
        stage[0] = moved[:, :LANES]
        stage[1] = moved[:, LANES:]
        for r in range(8):
            for lh in range(2):
                at = pl.ds(pl.multiple_of(m * levels + lh * 8, 8), 8)
                for h in range(2):
                    pert[HALO + r, h, at, :] = stage[h, pl.ds(lh * 64 + r, 8, stride=8), :]
        return carry

    lax.fori_loop(0, members, arrange, 0)

    classes = nn(classes_ref[...].astype(F32).astype(BF), perm[0])
    kappa = jnp.zeros(classes.shape, F32)
    for position, coefficient in enumerate(DIFFUSIVITIES):
        kappa = kappa + jnp.where(classes == float(position), coefficient, 0.0)
    kap_rows[1] = kappa

    pl.semaphore_wait(barrier, tiles - 1 + groups - 1 + 2)

    along_x = lax.rem(t, 4)
    ways = (
        (8, 0, south, 3, -3, 4),
        (4, 12, north, 0, 3, -4),
    )

    def edge(first_row, lo, hi):
        return pert.at[pl.ds(first_row, 4), :, pl.ds(lo, hi - lo)]

    def shares(part):
        lo, hi = PARTS[part]
        middle = (lo + hi) // 2
        return (lo, middle), (middle, hi)

    def key_of(way, part):
        return PERT + (way * len(PARTS) + part) * 4

    def waiting(way, part):
        lo, hi = shares(part)[1]
        return relay.at[way, :, :, pl.ds(PARTS[part][0] // 2, hi - lo)]

    def send_part(part, to_relay):
        one, two = shares(part)
        for way, (here, there, to, wraps, hop, onward) in enumerate(ways):
            key = key_of(way, part)
            if to_relay:

                @pl.when(along_x == wraps)
                def _():
                    send(edge(here, *two), waiting(way, part), key + 2, band(hop + tiles), j)

            else:
                send(edge(here, *one), edge(there, *one), key, to, j)

                @pl.when(along_x != wraps)
                def _():
                    send(edge(here, *two), edge(there, *two), key + 1, to, j)

    def forward_part(part):
        two = shares(part)[1]
        for way, (here, there, to, wraps, hop, onward) in enumerate(ways):
            key = key_of(way, part)

            @pl.when(along_x == 3 - wraps)
            def _():
                arrived(waiting(way, part), key + 2)
                send(
                    waiting(way, part), edge(there, *two), key + 1, band(onward + tiles), j, key + 3
                )

    def part_arrived(part):
        one, two = shares(part)
        for way, (here, there, to, wraps, hop, onward) in enumerate(ways):
            arrived(edge(there, *one), key_of(way, part))
            arrived(edge(there, *two), key_of(way, part) + 1)

    def part_sent(part):
        one, two = shares(part)
        for way, (here, there, to, wraps, hop, onward) in enumerate(ways):
            key = key_of(way, part)
            sent(edge(here, *one), key)

            @pl.when(along_x == wraps)
            def _():
                sent(edge(here, *two), key + 2)

            @pl.when(along_x != wraps)
            def _():
                sent(edge(here, *two), key + 1)

            @pl.when(along_x == 3 - wraps)
            def _():
                sent(waiting(way, part), key + 3)

    send(kap_rows.at[1], kap_rows.at[0], KAP_U, south, j)
    send(kap_rows.at[1], kap_rows.at[2], KAP_D, north, j)
    for part in range(len(PARTS)):
        send_part(part, True)
    for part in range(early):
        send_part(part, False)

    for fetch in fetches[2:]:
        fetch.wait()

    target = target_ref[...]
    bands = lax.broadcasted_iota(jnp.int32, (tiles, obs), 0)
    member_of = jnp.where(target == bands, 1.0, 0.0)
    member_bf = member_of.astype(BF)
    before = jnp.where(row_id < col_id, 1.0, 0.0).astype(BF)
    base = jnp.zeros((tiles, 1), F32)
    ranks = []
    for b in range(obs // 256):
        part = slice(b * 256, (b + 1) * 256)
        count = nn(member_bf[:, part], before) + base
        ranks.append(jnp.sum(member_of[:, part] * count, axis=0, keepdims=True))
        base = base + jnp.sum(member_of[:, part], axis=1, keepdims=True)
    rank = jnp.concatenate(ranks, axis=1).astype(jnp.int32) - core * slots

    pay[0:16, :] = jac_ref[...]
    pay[16:24, :] = jnp.concatenate([cells_ref[...].astype(F32), interp_ref[...]], axis=0)
    pay[24:32, :] = jnp.concatenate(
        [innov_ref[...], inv_ref[...], jnp.zeros((6, obs), F32)], axis=0
    )
    whole = pay[...]
    high = whole.astype(BF).astype(F32)
    rest = whole - high
    middle = rest.astype(BF).astype(F32)
    low = rest - middle
    for q in range(slots):
        mine = rank == q
        for k, piece in enumerate((high, middle, low)):
            val[k, q * FEATURES : (q + 1) * FEATURES, :] = jnp.where(mine, piece, 0.0).astype(BF)
    packed = nt(member_bf, val[0]) + nt(member_bf, val[1]) + nt(member_bf, val[2])
    out_buf[:, 0, :] = packed

    def send_band(d, carry):
        send(out_buf.at[band(d)], in_buf.at[core, t], A2A, band(d), j)
        return carry

    lax.fori_loop(1, tiles, send_band, 0, unroll=9)
    for part in range(len(PARTS)):
        forward_part(part)
        if part >= early:
            send_part(part, False)
    own = pltpu.make_async_copy(out_buf.at[t], in_buf.at[core, t], lsem.at[0])
    own.start()
    arrived(kap_rows.at[0], KAP_U)
    arrived(kap_rows.at[2], KAP_D)
    for r in range(16):
        block, row = divmod(r + 4, 8)
        line = kap_rows[block, row : row + 1, :]
        if r < 4:
            line = jnp.where(t == 0, 0.0, line)
        if r >= 12:
            line = jnp.where(t == tiles - 1, 0.0, line)
        for h in range(2):
            wide = jnp.broadcast_to(line[:, h * LANES : (h + 1) * LANES], (8, LANES))
            kap[r, h] = wide
            if 4 <= r < 12:
                ikap[r - 4, h] = 1.0 / wide

    own.wait()
    arrived(in_buf.at[core, pl.ds(0, tiles - 1)], A2A)
    send(in_buf.at[core], in_buf.at[core], OBS, t, sibling)

    blocks = MOST * tiles // LANES
    per_core = blocks // cores

    def unpack(source):
        for g in range(0, slots * FEATURES // LANES, 2):
            both = jnp.concatenate(
                [in_buf[source, :, 0, n * LANES : (n + 1) * LANES] for n in (g, g + 1)], axis=0
            ).T
            for b in range(LANES // FEATURES):
                at = source * per_core + g * 2 + b
                feat[at] = both[b * FEATURES : (b + 1) * FEATURES, :]

    along = 12

    def in_turn(step, start=0, count=blocks):
        def several(i, carry):
            step([start + i * along + n for n in range(along)])
            return carry

        lax.fori_loop(0, count // along, several, 0)

    my_levels = pl.ds(pl.multiple_of(chip * 8, 8), 8)

    def hits(b, c):
        cell = feat[b, 16 + c : 17 + c, :].astype(jnp.int32)
        row = jnp.where((cell & 1) == core, cell >> 8, -1)
        rows = lax.broadcasted_iota(jnp.int32, (8, 8, LANES), 0)
        return rows == row.reshape(1, 1, LANES)

    def build(which):
        spots = lax.broadcasted_iota(jnp.int32, (LANES, LANES), 0).astype(F32).astype(BF)
        one, none = jnp.ones((), BF), jnp.zeros((), BF)
        for b in which:
            low = (feat[b, 16:24, :].astype(jnp.int32) & 255) >> 1
            low = low.astype(F32).astype(BF)
            for c in range(4):
                spot = spots == low[c : c + 1, :]
                onehot[b, :, c * LANES : (c + 1) * LANES] = jnp.where(spot, one, none)

    def adjoint_obs(which, residual):
        for n, b in enumerate(which):
            z = residual(b)
            jac = feat[b, my_levels, :]
            for c in range(4):
                value = jac * (feat[b, 20 + c : 21 + c, :] * z)
                mask = hits(b, c)
                for k, piece in enumerate(split2(value)):
                    wide = jnp.where(mask, piece.reshape(1, 8, LANES), 0.0).reshape(64, LANES)
                    acols[n, k * 64 : (k + 1) * 64, c * LANES : (c + 1) * LANES] = wide.astype(BF)
        total = acc[...]
        for n, b in enumerate(which):
            total = total + nt(acols[n], onehot[b])
        acc[...] = total

    def summed():
        both = acc[...]
        return (both[:64] + both[64:]).reshape(8, 8, LANES)

    def first(which):
        build(which)
        adjoint_obs(which, lambda b: -(feat[b, 25:26, :] * feat[b, 24:25, :]))

    acc[...] = jnp.zeros(acc.shape, F32)
    unpack(core)
    in_turn(first, core * per_core, per_core)
    arrived(in_buf.at[1 - core], OBS)
    unpack(1 - core)
    in_turn(first, (1 - core) * per_core, per_core)
    x0[j, pl.ds(HALO, 8)] = summed()

    def spread(x, s_core, s_across, s_up, s_down, f_across, f_up, f_down):
        here = x.at[j, pl.ds(HALO, 8)]
        for to in (j, across):
            send(x.at[j, pl.ds(8, 4)], x.at[j, pl.ds(0, 4)], s_up, south, to)
            send(x.at[j, pl.ds(4, 4)], x.at[j, pl.ds(12, 4)], s_down, north, to)
        send(here, here, s_across, t, across)
        send(here, here, s_core, t, sibling)
        got = x.at[across, pl.ds(HALO, 8)]
        arrived(got, s_across)
        send(got, got, f_across, t, sibling)
        for key, forward, first_row in ((s_up, f_up, 0), (s_down, f_down, 12)):
            rows = pl.ds(first_row, 4)
            arrived(x.at[pl.ds(0, 2), rows], key)
            for half in range(2):
                edge = x.at[half * cores + core, rows]
                send(edge, edge, forward, t, sibling)
        arrived(here, s_core)
        arrived(got, f_across)
        arrived(x.at[pl.ds(0, 2), pl.ds(0, 4)], f_up)
        arrived(x.at[pl.ds(0, 2), pl.ds(12, 4)], f_down)

    spread(x0, AC0, AZ0, AU0, AD0, FZ0, FU0, FD0)
    for part in range(len(PARTS) - 1):
        part_arrived(part)

    def sweep(f, lo, hi):
        out = {}
        for r in range(lo, hi):
            here = f.get(r)
            beside = [f[n] for n in (r - 1, r + 1) if n in f]
            pair = []
            for h in range(2):
                terms = [row[h] for row in beside]
                if here is not None:
                    other = here[1 - h]
                    terms.append(other + pltpu.roll(other, (1, LANES - 1)[h], 1))
                beside_all = functools.reduce(jnp.add, terms)
                if here is None:
                    pair.append(kap[r, h] * beside_all)
                else:
                    pair.append(here[h] + kap[r, h] * (beside_all - 4.0 * here[h]))
            out[r] = pair
        return out

    def local_pass(x, control_out):
        up[...] = jnp.zeros(up.shape, F32)
        together = 4
        turns = 2 * members // together

        def group(i, carry):
            ids = []
            for g in range(together):
                lh, m = g % 2, i * (together // 2) + g // 2
                ids.append((lh, m, pl.ds(pl.multiple_of(m * levels + lh * 8, 8), 8)))
            fields = [
                {
                    r: [kap[r, h] * pert[r, h, at, :] * x[lh * 2 + h, r] for h in range(2)]
                    for r in range(16)
                }
                for lh, m, at in ids
            ]
            for k in range(4):
                fields = [sweep(f, k + 1, 15 - k) for f in fields]
            fields = [
                {r: [f[r][h] * ikap[r - HALO, h] for h in range(2)] for r in f} for f in fields
            ]
            if control_out:
                for f, (lh, m, at) in zip(fields, ids):
                    for r in range(8):
                        place_at = pl.ds(m * 128 + lh * 64 + r, 8, stride=8)
                        for h in range(2):
                            flat[h, place_at, :] = f[HALO + r][h]
            for k in range(4):
                fields = [sweep(f, 3 - k, 13 + k) for f in fields]
            for r in range(16):
                for h in range(2):
                    for half in range(2):
                        terms = [
                            pert[r, h, at, :] * f[r][h]
                            for f, (lh, m, at) in zip(fields, ids)
                            if lh == half
                        ]
                        up[half * 2 + h, r] += functools.reduce(jnp.add, terms)
            return carry

        lax.fori_loop(0, turns // 2, group, 0)
        if not control_out:
            part_arrived(len(PARTS) - 1)
        lax.fori_loop(turns // 2, turns, group, 0)

    def reduce_in_chip(source, from_core, key):
        for half in range(2):
            send(source.at[half * cores + 1 - core], from_core.at[half], key, t, sibling)

    def reduce_out(source, from_core, chip_sum, from_chip, from_north, from_south, keys):
        key, k_across, k_up, k_down = keys
        arrived(from_core, key)
        for half in range(2):
            chip_sum[half] = source[half * cores + core] + from_core[half]
        for half in range(2):
            to = half * cores + core
            send(chip_sum.at[half, pl.ds(12, 4)], from_north.at[chip], k_up, south, to)
            send(chip_sum.at[half, pl.ds(0, 4)], from_south.at[chip], k_down, north, to)
        send(chip_sum.at[1 - chip, pl.ds(HALO, 8)], from_chip, k_across, t, across)

    def reduced(chip_sum, from_chip, from_north, from_south, keys):
        key, k_across, k_up, k_down = keys
        arrived(from_chip, k_across)
        arrived(from_north, k_up)
        arrived(from_south, k_down)
        total = chip_sum[chip, pl.ds(HALO, 8)] + from_chip[...]
        edges = [from_north[0] + from_north[1], from_south[0] + from_south[1]]
        return total + jnp.concatenate(edges, axis=0)

    local_pass(x0, False)
    keys = (CR0, RZ0, RU0, RD0)
    reduce_in_chip(up, cr0, CR0)
    reduce_out(up, cr0, cs0, rz0, ru0, rd0, keys)
    state = (-STEP * scale * scale) * reduced(cs0, rz0, ru0, rd0, keys)
    state = jnp.concatenate(split2(state.reshape(64, LANES)), axis=0).astype(BF)

    def observe(which):
        for b in which:
            mixed = nn(state, onehot[b])
            mixed = mixed[:64] + mixed[64:]
            total = jnp.zeros((8, LANES), F32)
            for c in range(4):
                part = mixed[:, c * LANES : (c + 1) * LANES].reshape(8, 8, LANES)
                picked = jnp.sum(jnp.where(hits(b, c), part, 0.0), axis=0)
                total = total + feat[b, 20 + c : 21 + c, :] * picked
            y_own[b] = jnp.sum(feat[b, my_levels, :] * total, axis=0, keepdims=True)

    in_turn(observe)
    for d in range(1, groups):
        send(y_own, y_far.at[d - 1], YS, t, peer(d))
    arrived(y_far, YS)

    def misfit(b):
        y = y_own[b] + y_far[0, b] + y_far[1, b] + y_far[2, b]
        return feat[b, 25:26, :] * (y - feat[b, 24:25, :])

    acc[...] = jnp.zeros(acc.shape, F32)
    in_turn(lambda which: adjoint_obs(which, misfit))
    x1[j, pl.ds(HALO, 8)] = (-scale * STEP) * (STEP * x0[j, pl.ds(HALO, 8)] + summed())
    spread(x1, AC1, AZ1, AU1, AD1, FZ1, FU1, FD1)
    sent(cr0, CR0)
    local_pass(x1, True)

    sub = lax.broadcasted_iota(jnp.int32, (16, 8, LANES), 1)
    for lh in range(2):
        even, odd = up[lh * 2], up[lh * 2 + 1]
        vp[lh * 2] = jnp.where(sub < 4, even, pltpu.roll(odd, 4, 1))
        vp[lh * 2 + 1] = jnp.where(sub < 4, pltpu.roll(even, 4, 1), odd)

    def in_order(wide):
        hi, lo = split2(wide)
        return nn(hi.astype(BF), perm[1]) + nn(lo.astype(BF), perm[1])

    def written(m):
        return pltpu.make_async_copy(ready.at[m], control_ref.at[m], lsem.at[9 + m])

    def unmix(m):
        rows = pl.ds(m * 128, 128)
        wide = jnp.concatenate([flat[0, rows, :], flat[1, rows, :]], axis=1)
        ready[m] = in_order(wide).reshape(levels, 8, 256)
        written(m).start()

    keys = (CR1, RZ1, RU1, RD1)
    reduce_in_chip(vp, cr1, CR1)
    for m in range(members // 4):
        unmix(m)
    reduce_out(vp, cr1, cs1, rz1, ru1, rd1, keys)
    for m in range(members // 4, members):
        unmix(m)
    final = scale * reduced(cs1, rz1, ru1, rd1, keys)
    back = in_order(
        jnp.concatenate(
            [final.reshape(64, LANES), pltpu.roll(final, 4, 1).reshape(64, LANES)], axis=1
        )
    )
    for h in range(2):
        stage[h, 0:64, :] = back[:, h * LANES : (h + 1) * LANES]
        for level in range(4):
            incr_ref[level, :, h * LANES : (h + 1) * LANES] = stage[h, pl.ds(level, 8, stride=8), :]
    for m in range(members):
        written(m).wait()

    sent(in_buf.at[core, pl.ds(0, tiles - 1)], A2A)
    sent(kap_rows.at[0], KAP_U)
    sent(kap_rows.at[2], KAP_D)
    for part in range(len(PARTS)):
        part_sent(part)
    sent(in_buf.at[core], OBS)
    sent(y_far, YS)
    sent(cr1, CR1)
    for k in (AC0, AZ0, FZ0, RZ0, AC1, AZ1, FZ1, RZ1):
        sent(rz0, k)
    for k in (AU0, AD0, FU0, FD0, RU0, RD0, AU1, AD1, FU1, FD1, RU1, RD1):
        sent(ru0, k)


def write_out(control_ref, incr_ref, control_out, incr_out, control_held, incr_held, sems):
    count = control_ref.shape[0]
    ways = [(control_ref.at[m], control_held.at[m], control_out.at[m]) for m in range(count)]
    ways.append((incr_ref, incr_held, incr_out))
    reads = [pltpu.make_async_copy(a, b, sems.at[0, n]) for n, (a, b, c) in enumerate(ways)]
    writes = [pltpu.make_async_copy(b, c, sems.at[1, n]) for n, (a, b, c) in enumerate(ways)]
    for read in reads:
        read.start()
    for read, write in zip(reads, writes):
        read.wait()
        write.start()
    for write in writes:
        write.wait()


def on_device(tiles, groups, perturbations, classes, target, cells, interp, jac, innov, inverse):
    members, levels, rows, cols = perturbations.shape
    obs = target.shape[0]
    vm = pl.BlockSpec(memory_space=pltpu.VMEM)
    hbm = pl.BlockSpec(memory_space=pltpu.HBM)
    window = (groups, 16, 8, LANES)
    message = FEATURES * MOST // 2
    blocks = MOST * tiles // LANES
    reduction = [
        ((2, 16, 8, LANES), F32), ((2, 16, 8, LANES), F32), ((8, 8, LANES), F32),
        ((2, 4, 8, LANES), F32), ((2, 4, 8, LANES), F32),
    ]
    scratch = [
        (perturbations.shape, perturbations.dtype),
        (classes.shape, classes.dtype),
        ((1, obs), target.dtype),
        (cells.shape, cells.dtype),
        (interp.shape, interp.dtype),
        (jac.shape, jac.dtype),
        ((1, obs), innov.dtype),
        ((1, obs), inverse.dtype),
        ((2, 256, 256), BF),
        ((FEATURES, obs), F32),
        ((3, message, obs), BF),
        ((tiles, 1, message), F32),
        ((2, tiles, 1, message), F32),
        ((blocks, FEATURES, LANES), F32),
        ((blocks, LANES, 4 * LANES), BF),
        ((12, 128, 4 * LANES), BF),
        ((128, LANES), F32),
        ((16, 2, members * levels, LANES), F32),
        ((2, LANES, LANES), F32),
        ((3, 8, 256), F32),
        ((16, 2, 8, LANES), F32),
        ((8, 2, 8, LANES), F32),
        (window, F32), (window, F32), (window, F32), (window, F32),
        *reduction,
        *reduction,
        ((blocks, 1, LANES), F32),
        ((groups - 1, blocks, 1, LANES), F32),
        ((2, members * levels * rows, LANES), F32),
        ((members, levels, rows, cols), F32),
        ((2, 4, 2, members * levels // 2, LANES), F32),
    ]
    control, increment = pl.pallas_call(
        functools.partial(kernel, tiles, groups, members),
        out_shape=(
            jax.ShapeDtypeStruct((members, levels, rows, cols), F32),
            jax.ShapeDtypeStruct((levels // groups, rows, cols), F32),
        ),
        in_specs=[hbm] * 8,
        out_specs=(hbm, vm),
        scratch_shapes=[pltpu.VMEM(shape, dtype) for shape, dtype in scratch]
        + [
            pltpu.SemaphoreType.DMA((N_SEM,)),
            pltpu.SemaphoreType.DMA((N_SEM,)),
            pltpu.SemaphoreType.DMA((9 + members,)),
        ],
        compiler_params=pltpu.CompilerParams(
            collective_id=0, has_side_effects=True, vmem_limit_bytes=60 * 1024 * 1024
        ),
        name="assimilate",
    )(
        perturbations, classes, target.reshape(1, obs), cells, interp, jac,
        innov.reshape(1, obs), inverse.reshape(1, obs),
    )
    return pl.pallas_call(
        write_out,
        out_shape=(
            jax.ShapeDtypeStruct(control.shape, F32), jax.ShapeDtypeStruct(increment.shape, F32)
        ),
        in_specs=[hbm, hbm],
        out_specs=(hbm, hbm),
        scratch_shapes=[
            pltpu.VMEM(control.shape, F32),
            pltpu.VMEM(increment.shape, F32),
            pltpu.SemaphoreType.DMA((2, members + 1)),
        ],
        compiler_params=pltpu.CompilerParams(vmem_limit_bytes=60 * 1024 * 1024),
        name="write_out",
    )(control, increment)


def solution(mesh):
    in_specs = (
        P("mem", None, "tile", None),
        P("tile", None),
        P("tile", None),
        P(None, "tile"),
        P(None, "tile"),
        P(None, "tile"),
        P("tile"),
        P("tile"),
    )
    out_specs = (P("mem", None, "tile", None), P("mem", "tile", None))
    return jax.shard_map(
        functools.partial(on_device, mesh.shape["tile"], mesh.shape["mem"]),
        mesh=mesh, in_specs=in_specs, out_specs=out_specs, check_vma=False,
    )
```
